32 devices in a mesh: seq: 8 (over y, x, core), batch: 4 (over z).
Axes of the slice: x: 2, y: 2, z: 4, core: 2. Of those that a mesh axis runs over, the one named last changes fastest.
Arguments:
- tokens: bfloat16 [16, 4096, 768], P('batch', 'seq'), may hold values from -6 to 6
- w_in: bfloat16 [768, 3072], P(None, ('seq', 'batch')), may hold values from -0.21875 to 0.21875
- b_in: bfloat16 [3072], P(('seq', 'batch')), may hold values from -3 to 3
- w_out: bfloat16 [3072, 768], P(('seq', 'batch')), may hold values from -0.109375 to 0.109375
- b_out: bfloat16 [768], P(('seq', 'batch')), may hold values from -3 to 3
- gain_one: bfloat16 [768], P(('seq', 'batch')), may hold values from 0.099609375 to 1.8984375
- shift_one: bfloat16 [768], P(('seq', 'batch')), may hold values from -3 to 3
- gain_two: bfloat16 [768], P(('seq', 'batch')), may hold values from 0.099609375 to 1.8984375
- shift_two: bfloat16 [768], P(('seq', 'batch')), may hold values from -3 to 3
- cotangent: bfloat16 [16, 4096, 768], P('batch', 'seq'), may hold values from -6 to 6
Outputs:
- output: bfloat16 [16, 4096, 768], P('batch', 'seq')
- grad_tokens: bfloat16 [16, 4096, 768], P('batch', 'seq')
- grad_w_in: float32 [768, 3072], P(None, ('seq', 'batch'))
- grad_b_in: float32 [3072], P(('seq', 'batch'))
- grad_w_out: float32 [3072, 768], P(('seq', 'batch'))
- grad_b_out: float32 [768], P(('seq', 'batch'))
- grad_gain_one: float32 [768], P(('seq', 'batch'))
- grad_shift_one: float32 [768], P(('seq', 'batch'))
- grad_gain_two: float32 [768], P(('seq', 'batch'))
- grad_shift_two: float32 [768], P(('seq', 'batch'))
The draws below stay inside these ranges and needn't reach their ends.
All inputs are finite; a program needn't handle non-finite values.
Results may differ from the reference program's by a relative error of at most 0.0076.
Values may be sent and summed in bfloat16 or wider, within the bound.
A program may use at most 384 MiB of HBM per device.

```python
import math
import jax
import jax.numpy as jnp
from jax import lax

D = 768
FF = 3072
L = 4096
SEQS = 16


def spiked(drawn, rng, source, target, shards_of, factor):
    owner, partner = [(jnp.arange(drawn.shape[dim]) // (drawn.shape[dim] // shards_of)).reshape([-1 if axis == dim else 1 for axis in range(drawn.ndim)]) for dim in (source, target)]
    chosen = jax.random.permutation(rng, shards_of)[partner]
    strong = (owner == chosen) | (owner == (partner + shards_of // 2) % shards_of)
    return jnp.where(strong, factor * drawn, drawn)


def levels(stream_key, shape, pieces, smallest, largest):
    def one(position, blocks):
        heights = jax.random.uniform(jax.random.fold_in(jax.random.fold_in(stream_key, 6), position), (blocks,), jnp.float32, smallest / len(pieces), largest / len(pieces))
        return jnp.repeat(jnp.exp(heights), shape[position] // blocks).reshape((-1,) + (1,) * (len(shape) - position - 1))

    level = one(*pieces[0])
    for cut in pieces[1:]:
        level = level * one(*cut)
    return level


def noise(key, shape, deviation, reach, cuts=(), kind=jnp.bfloat16):
    loudness = levels(key, shape, cuts, -0.22, 0.18) if cuts else 1.0
    entries = jax.random.normal(key, shape, jnp.float32) * deviation * loudness
    return jnp.minimum(jnp.maximum(entries, -reach), reach).astype(kind)


def gaussian_with(own_key, shape, width, limit, cuts, heavy, held_as=jnp.bfloat16):
    array = width * jax.random.normal(own_key, shape, jnp.float32)
    if cuts:
        array = array * levels(own_key, shape, cuts, -0.22, 0.18)
    return jnp.clip(spiked(array, jax.random.fold_in(own_key, 3), *heavy), -limit, limit).astype(held_as)


def setup_inputs(seed: int = 0) -> dict:
    key_of = jax.random.split(jax.random.key(seed), 11)
    return {
        "tokens": noise(key_of[0], (SEQS, L, D), 1.0, 6.0, ((0, 4), (1, 8))),
        "w_in": noise(key_of[1], (D, FF), D ** -0.5, 0.21875, ((1, 32),)),
        "b_in": noise(key_of[2], (FF,), 0.5, 3.0, ((0, 32),)),
        "w_out": noise(key_of[3], (FF, D), FF ** -0.5, 0.109375, ((0, 32),)),
        "b_out": noise(key_of[4], (D,), 0.5, 3.0, ((0, 32),)),
        "gain_one": jnp.clip(1.0 + 0.18 * jax.random.normal(key_of[5], (D,), jnp.float32), 0.099609375, 1.8984375).astype(jnp.bfloat16),
        "shift_one": noise(key_of[6], (D,), 0.5, 3.0, ((0, 32),)),
        "gain_two": jnp.clip(1.0 + 0.18 * jax.random.normal(key_of[7], (D,), jnp.float32), 0.099609375, 1.8984375).astype(jnp.bfloat16),
        "shift_two": noise(key_of[8], (D,), 0.5, 3.0, ((0, 32),)),
        "cotangent": gaussian_with(key_of[9], (SEQS, L, D), 1.0, 6.0, ((0, 4), (1, 8)), (1, 2, 8, 2.0)),
    }


@jax.custom_vjp
def low(v):
    return lax.optimization_barrier(v.astype(jnp.bfloat16)).astype(jnp.float32)

@jax.custom_vjp
def low_back(v):
    return v

def low_keep(v):
    return (low(v), None)

def low_pass(kept, grad):
    return (grad,)

def back_keep(v):
    return (v, None)

def back_low(kept, grad):
    return (low(grad),)
low.defvjp(low_keep, low_pass)
low_back.defvjp(back_keep, back_low)
epsilon = 1e-05

def hidden_table(extent):
    idx_all = jnp.arange(extent, dtype=jnp.int32)
    angles = (idx_all[:, None] * idx_all[None, :] % extent).astype(jnp.float32) * (2.0 * math.pi / extent)
    factor = 1.0 / math.sqrt(extent)
    return jnp.concatenate([jnp.cos(angles) * factor, jnp.sin(angles) * factor], axis=1)

def sequence_table(length):
    idx_all = jnp.arange(length, dtype=jnp.int32)
    angles = (idx_all[:, None] * idx_all[None, :] % length).astype(jnp.float32) * (2.0 * math.pi / length)
    factor = 1.0 / math.sqrt(length)
    return jnp.stack([jnp.cos(angles) * factor, -jnp.sin(angles) * factor])

def layer_norm(values, gain, shift):
    center = values - lax.optimization_barrier(jnp.mean(values, axis=-1, keepdims=True))
    inv_std = lax.rsqrt(lax.optimization_barrier(jnp.mean(center * center, axis=-1, keepdims=True)) + epsilon)
    return center * inv_std * gain + shift

def highest(left, right):
    return jnp.dot(left, right, precision=lax.Precision.HIGHEST)

def reference(tokens, w_in, b_in, w_out, b_out, gain_one, shift_one, gain_two, shift_two, cotangent):
    model_width = tokens.shape[2]
    h_table = low(hidden_table(model_width))
    s_table = low(sequence_table(tokens.shape[1]))
    params = tuple((p.astype(jnp.float32) for p in (w_in, b_in, w_out, b_out, gain_one, shift_one, gain_two, shift_two)))

    def forward(seq_x, prm):
        wi, bi, wo, bo, g_one, s_one, g_two, s_two = prm
        spectra = low_back(low(highest(seq_x, h_table)))
        mixv = highest(s_table[0], spectra[:, :model_width]) + highest(s_table[1], spectra[:, model_width:])
        mixv = low_back(low(mixv))
        act_one = layer_norm(seq_x + mixv, g_one, s_one)
        pre = low_back(highest(low(act_one), wi) + bi)
        hidden = low(jax.nn.gelu(pre, approximate=True))
        branch = low_back(highest(hidden, wo) + bo)
        return layer_norm(act_one + branch, g_two, s_two)

    def one_seq(totals, pair):
        seq_x, seq_c = pair
        result, pull = jax.vjp(forward, seq_x, params)
        grad_x, grad_p = pull(seq_c)
        totals = jax.tree.map(lambda a, b: a + b, totals, grad_p)
        return (totals, (result.astype(jnp.bfloat16), grad_x.astype(jnp.bfloat16)))
    zeros = jax.tree.map(jnp.zeros_like, params)
    totals, (outputs, grads_x) = lax.scan(one_seq, zeros, (tokens.astype(jnp.float32), cotangent.astype(jnp.float32)))
    return (outputs, grads_x, totals[0], totals[1], totals[2], totals[3], totals[4], totals[5], totals[6], totals[7])
```

```python
from functools import partial
import math

import jax
import jax.numpy as jnp
import ml_dtypes
import numpy as np
from jax import lax
from jax.experimental import pallas as pl
from jax.experimental.pallas import tpu as pltpu
from jax.sharding import PartitionSpec as P

epsilon = 1e-05
f32, bf16 = jnp.float32, jnp.bfloat16
MESH = pl.DeviceIdType.MESH


def dot_nn(a, b):
    return lax.dot_general(a, b, (((1,), (0,)), ((), ())), preferred_element_type=f32)


def dot_nt(a, b):
    return lax.dot_general(a, b, (((1,), (1,)), ((), ())), preferred_element_type=f32)


def dot_tn(a, b):
    return lax.dot_general(a, b, (((0,), (0,)), ((), ())), preferred_element_type=f32)


def plan_columns(width, parts):
    pairs = width // 2 // parts
    r = np.arange(width)
    dev, kind, i = r // (2 * pairs), (r // pairs) % 2, r % pairs
    j = dev * pairs + i
    first = (kind == 1) & (j == 0)
    return j, kind, first


def packed_hidden(width, parts):
    j, kind, first = plan_columns(width, parts)
    k = np.arange(width)
    angle = (j[:, None] * k[None, :] % width) * (2.0 * math.pi / width)
    table = np.where(kind[:, None] == 0, np.cos(angle), np.sin(angle))
    nyquist = np.cos(np.pi * (k % 2))
    table = np.where(first[:, None], nyquist[None, :], table) / math.sqrt(width)
    return table.astype(np.float32).astype(ml_dtypes.bfloat16)


def column_order(width, parts):
    j, kind, first = plan_columns(width, parts)
    col = np.where(kind == 0, j, np.where(first, width // 2, (width - j) % width))
    return (col[:, None] == np.arange(width)[None, :]).astype(ml_dtypes.bfloat16)


def inner_table(span, length):
    a = np.arange(span)
    angle = (a[:, None] * a[None, :] % span) * (2.0 * math.pi / span)
    table = np.concatenate([np.cos(angle), np.sin(angle)], axis=0)
    return (table / math.sqrt(length)).astype(np.float32).astype(ml_dtypes.bfloat16)


def twiddles(parts, span):
    b = np.arange(parts)[:, None]
    angle = b * np.arange(span)[None, :] * (2.0 * math.pi / (parts * span))
    return np.concatenate([np.cos(angle), np.sin(angle)], axis=0).astype(np.float32)


def add(a, b):
    return (a[0] + b[0], a[1] + b[1])


def sub(a, b):
    return (a[0] - b[0], a[1] - b[1])


def minus_i(a):
    return (a[1], -a[0])


def dft4(x0, x1, x2, x3):
    t0, t1, t2, t3 = add(x0, x2), sub(x0, x2), add(x1, x3), sub(x1, x3)
    r = minus_i(t3)
    return add(t0, t2), add(t1, r), sub(t0, t2), sub(t1, r)


def dft8(x):
    e = dft4(x[0], x[2], x[4], x[6])
    o = dft4(x[1], x[3], x[5], x[7])
    h = math.sqrt(0.5)
    o1 = (h * (o[1][0] + o[1][1]), h * (o[1][1] - o[1][0]))
    o2 = minus_i(o[2])
    o3 = (h * (o[3][1] - o[3][0]), -h * (o[3][0] + o[3][1]))
    o = (o[0], o1, o2, o3)
    return [add(e[k], o[k]) for k in range(4)] + [sub(e[k], o[k]) for k in range(4)]


def radix_step(rec, tw, t_ref, parts, pairs, span):
    groups = pairs // 16
    count = 2 * parts * pairs

    def tile(u, carry):
        lanes = pl.ds(pl.multiple_of(u * 128, 128), 128)
        lanes_im = pl.ds(pl.multiple_of(span + u * 128, 128), 128)
        extra = [jnp.zeros((16, 128), f32), jnp.zeros((16, 128), f32)]
        row = lax.broadcasted_iota(jnp.int32, (16, 128), 0)
        for g in range(groups):
            x = []
            for s in range(parts):
                re = rec[s, g * 16:g * 16 + 16, lanes].astype(f32)
                im = rec[s, pairs + g * 16:pairs + g * 16 + 16, lanes].astype(f32)
                x.append((re, -im))
            y = dft8(x)
            for b in range(parts):
                c, s = tw[b:b + 1, lanes], tw[parts + b:parts + b + 1, lanes]
                conj = y[(parts - b) % parts]
                for kind, (zr, zi) in enumerate((y[b], (conj[0], -conj[1]))):
                    tr = c * zr + s * zi
                    ti = c * zi - s * zr
                    base = (kind * parts + b) * pairs + g * 16
                    t_ref[base:base + 16, lanes] = tr.astype(bf16)
                    t_ref[base:base + 16, lanes_im] = ti.astype(bf16)
                    if g == 0:
                        hit = row == kind * parts + b
                        extra[0] = jnp.where(hit, jnp.broadcast_to(-ti[0:1], (16, 128)), extra[0])
                        extra[1] = jnp.where(hit, jnp.broadcast_to(tr[0:1], (16, 128)), extra[1])
        t_ref[count:count + 16, lanes] = extra[0].astype(bf16)
        t_ref[count:count + 16, lanes_im] = extra[1].astype(bf16)
        return carry

    lax.fori_loop(0, span // 128, tile, 0)


def spread_step(o_ref, put, me, parts, pairs, span, u):
    count = 2 * parts * pairs
    lanes = pl.ds(pl.multiple_of(u * 128, 128), 128)
    low = lax.broadcasted_iota(jnp.int32, (16, 128), 1) < 64
    row = lax.broadcasted_iota(jnp.int32, (16, 128), 0)
    special = (row == 0) & (jnp.zeros((16, 128), jnp.int32) + me == 0)
    extra = o_ref[count:count + 16, lanes]
    for p in range(parts // 2):
        for g in range(pairs // 16):
            v = [[None, None], [None, None]]
            for kind in range(2):
                for h in range(2):
                    base = (kind * parts + 2 * p + h) * pairs + g * 16
                    v[kind][h] = o_ref[base:base + 16, lanes]
            if g == 0:
                for h in range(2):
                    b = 2 * p + h
                    even = 0.5 * (v[0][h] + v[1][h])
                    odd = jnp.broadcast_to(0.5 * (extra[b:b + 1] - extra[parts + b:parts + b + 1]), (16, 128))
                    v[0][h] = jnp.where(special, even, v[0][h])
                    v[1][h] = jnp.where(special, odd, v[1][h])
            for kind in range(2):
                v0, v1 = v[kind]
                rows = pl.ds(kind * pairs + g * 16, 16)
                cols = pl.ds(p * 128, 128)
                put(2 * u, rows, cols, jnp.where(low, v0, pltpu.roll(v1, 64, 1)).astype(bf16))
                put(2 * u + 1, rows, cols, jnp.where(low, pltpu.roll(v0, 64, 1), v1).astype(bf16))


def fold(v):
    total = v[0:8]
    for k in range(8, v.shape[0], 8):
        total = total + v[k:k + 8]
    return total


def rows_of(ref, at):
    return jnp.concatenate([ref[c, at, :] for c in range(ref.shape[0])], axis=1)


def set_rows(ref, at, value):
    for c in range(ref.shape[0]):
        ref[c, at, :] = value[:, c * 128:(c + 1) * 128]


def mean_of(v):
    return jnp.mean(v, axis=-1, keepdims=True)


def gelu_pair(x):
    k = math.sqrt(2.0 / math.pi)
    c = 0.044715
    x2 = x * x
    half = 0.5 + 0.5 * jnp.tanh(x * (k + (k * c) * x2))
    value = x * half
    slope = half + value * (1.0 - half) * (2.0 * k + (6.0 * k * c) * x2)
    return value, slope


def ffn_forward(x_get, nbuf, sbuf, alow, hid, slope, acc, w, vec, bias_in, chunk, rows_step):
    rows = nbuf.shape[1]

    def first(r, carry):
        at = pl.ds(pl.multiple_of(r * rows_step, rows_step), rows_step)
        v = x_get(at).astype(f32) + rows_of(nbuf, at)
        center = v - mean_of(v)
        inv = lax.rsqrt(mean_of(center * center) + epsilon)
        n = center * inv
        set_rows(nbuf, at, n)
        sbuf[at, :] = jnp.broadcast_to(inv, (rows_step, 128))
        alow[at, :] = (n * vec[0:1] + vec[1:2]).astype(bf16)
        return carry

    lax.fori_loop(0, rows // rows_step, first, 0)

    def step(c, carry):
        at = pl.ds(pl.multiple_of(c * chunk, chunk), chunk)
        pre = dot_nt(alow[...], w[0, at, :]) + bias_in[c]
        value, back = gelu_pair(pre)
        low = value.astype(bf16)
        hid[c] = low
        slope[c] = back.astype(bf16)
        part = dot_nn(low, w[1, at, :])

        @pl.when(c == 0)
        def _():
            acc[...] = part

        @pl.when(c > 0)
        def _():
            acc[...] += part

        return carry

    lax.fori_loop(0, hid.shape[0], step, 0)


def ffn_middle(nbuf, acc, glow, cot, outv, vec, sums, rows_step):
    rows = nbuf.shape[1]

    def second(r, carry):
        at = pl.ds(pl.multiple_of(r * rows_step, rows_step), rows_step)
        v = rows_of(nbuf, at) * vec[0:1] + vec[1:2] + (acc[at, :] + vec[4:5])
        center = v - mean_of(v)
        inv = lax.rsqrt(mean_of(center * center) + epsilon)
        n = center * inv
        outv[at, :] = (n * vec[2:3] + vec[3:4]).astype(bf16)
        g = cot[at, :].astype(f32)
        q = g * vec[2:3]
        gr = inv * (q - mean_of(q) - n * mean_of(q * n))
        acc[at, :] = gr
        low = gr.astype(bf16)
        glow[at, :] = low
        sums[2] += fold(g * n)
        sums[3] += fold(g)
        sums[4] += fold(low.astype(f32))
        return carry

    lax.fori_loop(0, rows // rows_step, second, 0)


def ffn_backward(nbuf, sbuf, alow, hid, slope, acc, glow, w, dw, bsum, vec, sums, chunk, rows_step, put):
    rows = nbuf.shape[1]

    def step(c, carry):
        at = pl.ds(pl.multiple_of(c * chunk, chunk), chunk)
        gh = dot_nt(glow[...], w[1, at, :])
        pre32 = gh * slope[c].astype(f32)
        gpre = pre32.astype(bf16)
        bsum[c] += fold(gpre.astype(f32))
        dw[1, at, :] += dot_tn(hid[c], glow[...])
        dw[0, at, :] += dot_tn(gpre, alow[...])
        acc[...] += dot_nn(gpre, w[0, at, :])
        return carry

    lax.fori_loop(0, hid.shape[0], step, 0)

    def last(r, carry):
        at = pl.ds(pl.multiple_of(r * rows_step, rows_step), rows_step)
        ga = acc[at, :]
        n = rows_of(nbuf, at)
        sums[0] += fold(ga * n)
        sums[1] += fold(ga)
        q = ga * vec[0:1]
        put(at, sbuf[at, 0:1] * (q - mean_of(q) - n * mean_of(q * n)))
        return carry

    lax.fori_loop(0, rows // rows_step, last, 0)


def layer_kernel(geo, tok, cot, w_all, hp_all, wd_all, cp_all, tw, vec, bias_in,
                 out, gtok, grow, dw_all, small, bsum,
                 tokv, cotv, outv, w, hp, wd, cp, dw, send1, recv1, send2, recv2, t_ref, o_ref,
                 nbuf, sbuf, alow, hid, slope, acc, glow, sums,
                 ss1, rs1, ss2, rs2, free1, free2, load, io):
    parts, pairs, span, width, jobs, chunk, rows_step = geo
    me = lax.axis_index("seq")
    plane = lax.axis_index("batch")

    def peer(d):
        return lax.rem(me + d, parts)

    def load_of(k):
        if k < jobs:
            return pltpu.make_async_copy(tok.at[k], tokv.at[k], load.at[k])
        a, b = ((hp_all, hp), (wd_all, wd), (cp_all, cp), (w_all, w))[k - jobs]
        return pltpu.make_async_copy(a, b, load.at[k])

    for k in (jobs, 0, 1, jobs + 1, 2, 3, jobs + 2, jobs + 3):
        load_of(k).start()

    barrier = pltpu.get_barrier_semaphore()

    def greet(d, carry):
        pl.semaphore_signal(barrier, inc=1, device_id=(peer(d), plane), device_id_type=MESH)
        return carry

    lax.fori_loop(1, parts, greet, 0)
    pl.semaphore_wait(barrier, parts - 1)

    def remote(send, recv, ss, rs, k, d):
        p = peer(d)
        return pltpu.make_async_remote_copy(
            src_ref=send.at[lax.rem(k, 2), p], dst_ref=recv.at[lax.rem(k, jobs), me],
            send_sem=ss.at[lax.rem(k, 2), d], recv_sem=rs.at[lax.rem(k, jobs), d],
            device_id=(p, plane), device_id_type=MESH)

    def own(send, recv, rs, k):
        return pltpu.make_async_copy(
            send.at[lax.rem(k, 2), me], recv.at[lax.rem(k, jobs), me], rs.at[lax.rem(k, jobs), 0])

    def wait_sends(send, recv, ss, rs, k):
        def one(d, carry):
            remote(send, recv, ss, rs, k, d).wait_send()
            return carry

        lax.fori_loop(1, parts, one, 0)

    def wait_recvs(send, recv, ss, rs, k):
        own(send, recv, rs, k).wait()

        def one(d, carry):
            source = lax.rem(me + parts - d, parts)
            slot = lax.rem(k, jobs)
            pltpu.make_async_remote_copy(
                src_ref=send.at[0, 0], dst_ref=recv.at[slot, source],
                send_sem=ss.at[0, d], recv_sem=rs.at[slot, d],
                device_id=(source, plane), device_id_type=MESH).wait_recv()
            return carry

        lax.fori_loop(1, parts, one, 0)

    def tell(sem, slot):
        def one(d, carry):
            pl.semaphore_signal(sem.at[slot], inc=1, device_id=(peer(d), plane), device_id_type=MESH)
            return carry

        lax.fori_loop(1, parts, one, 0)

    one_way = (send1, recv1, ss1, rs1)
    way_back = (send2, recv2, ss2, rs2)

    def hidden_job(k):
        table = dot_nt(hp[...], tokv[lax.rem(k, jobs)]).astype(bf16)
        send1[lax.rem(k, 2)] = table.reshape(parts, 2 * pairs, span)
        own(send1, recv1, rs1, k).start()

        def one(d, carry):
            remote(*one_way, k, d).start()
            return carry

        lax.fori_loop(1, parts, one, 0)

    def sequence_job(k, before_send):
        wait_recvs(*one_way, k)
        radix_step(recv1.at[lax.rem(k, jobs)], tw, t_ref, parts, pairs, span)
        o_ref[...] = dot_nn(t_ref[...], wd[...])
        before_send()
        slot = lax.rem(k, 2)

        def one(u, carry):
            def put(p, rows, cols, value):
                send2[slot, p, rows, cols] = value

            spread_step(o_ref, put, me, parts, pairs, span, u)
            for h in range(2):
                d = lax.rem(2 * u + h - me + parts, parts)

                @pl.when(d > 0)
                def _():
                    remote(*way_back, k, d).start()

                @pl.when(d == 0)
                def _():
                    own(send2, recv2, rs2, k).start()
            return carry

        lax.fori_loop(0, parts // 2, one, 0)

    def mixed_job(k):
        wait_recvs(*way_back, k)
        blocks = recv2[lax.rem(k, jobs)].reshape(width, span)
        natural = dot_tn(blocks, cp[...])
        step = span // parts
        for b in range(parts):
            for c in range(width // 128):
                nbuf[c, pl.ds(b, step, stride=parts), :] = natural[b * step:(b + 1) * step, c * 128:(c + 1) * 128]

    load_of(jobs).wait()
    for k in range(2):
        load_of(k).wait()

    def lead(k, carry):
        hidden_job(k)
        return carry

    lax.fori_loop(0, 2, lead, 0)
    dw[...] = jnp.zeros_like(dw)
    sums[...] = jnp.zeros_like(sums)
    bsum[...] = jnp.zeros_like(bsum)
    for k in (2, 3, jobs + 1, jobs + 2):
        load_of(k).wait()

    def fill(k, carry):
        sequence_job(k, lambda: None)
        tell(free1, k)
        wait_sends(*one_way, k)
        hidden_job(k + 2)
        return carry

    lax.fori_loop(0, 2, fill, 0)
    load_of(jobs + 3).wait()

    def out_copy(i):
        return pltpu.make_async_copy(outv, out.at[i], io.at[0])

    def cot_copy(i):
        return pltpu.make_async_copy(cot.at[i], cotv, io.at[1])

    def row_copy(i):
        return pltpu.make_async_copy(acc, grow.at[i], io.at[2])

    def main(i, carry):
        cot_copy(i).start()
        mixed_job(i)
        tell(free2, i)
        ffn_forward(lambda at: tokv[i, at, :], nbuf, sbuf, alow, hid, slope, acc, w, vec, bias_in, chunk, rows_step)

        def before():
            wait_sends(*way_back, i)

            @pl.when(i >= 2)
            def _():
                pl.semaphore_wait(free2.at[lax.rem(i + 2, jobs)], parts - 1)

        sequence_job(i + 2, before)

        @pl.when(i < 2)
        def _():
            tell(free1, lax.rem(i + 2, jobs))

        cot_copy(i).wait()

        @pl.when(i > 0)
        def _():
            out_copy(i - 1).wait()

        ffn_middle(nbuf, acc, glow, cotv, outv, vec, sums, rows_step)
        out_copy(i).start()

        def put(at, value):
            acc[at, :] = value
            tokv[i, at, :] = value.astype(bf16)

        ffn_backward(nbuf, sbuf, alow, hid, slope, acc, glow, w, dw, bsum, vec, sums, chunk, rows_step, put)
        row_copy(i).start()
        wait_sends(*one_way, i + 2)
        pl.semaphore_wait(free1.at[i], parts - 1)
        hidden_job(i + jobs)
        row_copy(i).wait()
        return carry

    lax.fori_loop(0, jobs, main, 0)
    dw_copy = pltpu.make_async_copy(dw, dw_all, io.at[3])
    dw_copy.start()
    small[...] = sums[...]

    def gt_copy(i):
        return pltpu.make_async_copy(tokv.at[i], gtok.at[i], io.at[4 + i])

    def final(i):
        back = pltpu.make_async_copy(grow.at[i], acc, io.at[2])
        back.start()
        mixed_job(i + jobs)
        back.wait()
        for c in range(width // 128):
            tokv[i, :, c * 128:(c + 1) * 128] = (nbuf[c] + acc[:, c * 128:(c + 1) * 128]).astype(bf16)
        gt_copy(i).start()

    def drain(i, carry):
        final(i)

        def before():
            wait_sends(*way_back, i + 4)
            pl.semaphore_wait(free2.at[i + 2], parts - 1)

        sequence_job(i + 6, before)
        return carry

    lax.fori_loop(0, 2, drain, 0)

    def finish(i, carry):
        final(i + 2)
        wait_sends(*way_back, i + 6)
        wait_sends(*one_way, i + 6)
        return carry

    lax.fori_loop(0, 2, finish, 0)
    out_copy(jobs - 1).wait()
    dw_copy.wait()
    for i in range(jobs):
        gt_copy(i).wait()


def layer_call(tok, cot, w_all, vec, bias_in, parts):
    jobs, span, width = tok.shape
    ff = w_all.shape[1]
    pairs = width // 2 // parts
    chunk, rows_step = ff // 3, span // 2
    steps = ff // chunk
    length = span * parts
    geo = (parts, pairs, span, width, jobs, chunk, rows_step)
    tables = (
        jnp.asarray(packed_hidden(width, parts)),
        jnp.asarray(inner_table(span, length)),
        jnp.asarray(column_order(width, parts)),
        jnp.asarray(twiddles(parts, span)),
    )
    hbm, vmem, dma = pl.BlockSpec(memory_space=pl.ANY), pl.BlockSpec(memory_space=pltpu.VMEM), pltpu.SemaphoreType.DMA
    block = (parts, 2 * pairs, span)
    scratch = [
        pltpu.VMEM((jobs, span, width), bf16),
        pltpu.VMEM((span, width), bf16),
        pltpu.VMEM((span, width), bf16),
        pltpu.VMEM((2, ff, width), bf16),
        pltpu.VMEM((width, width), bf16),
        pltpu.VMEM((2 * span, span), bf16),
        pltpu.VMEM((width, width), bf16),
        pltpu.VMEM((2, ff, width), f32),
        pltpu.VMEM((2,) + block, bf16),
        pltpu.VMEM((jobs,) + block, bf16),
        pltpu.VMEM((2,) + block, bf16),
        pltpu.VMEM((jobs,) + block, bf16),
        pltpu.VMEM((2 * parts * pairs + 16, 2 * span), bf16),
        pltpu.VMEM((2 * parts * pairs + 16, span), f32),
        pltpu.VMEM((width // 128, span, 128), f32),
        pltpu.VMEM((span, 128), f32),
        pltpu.VMEM((span, width), bf16),
        pltpu.VMEM((steps, span, chunk), bf16),
        pltpu.VMEM((steps, span, chunk), bf16),
        pltpu.VMEM((span, width), f32),
        pltpu.VMEM((span, width), bf16),
        pltpu.VMEM((5, 8, width), f32),
        dma((2, parts)), dma((jobs, parts)), dma((2, parts)), dma((jobs, parts)),
        pltpu.SemaphoreType.REGULAR((jobs,)), pltpu.SemaphoreType.REGULAR((jobs,)),
        dma((jobs + 4,)), dma((4 + jobs,)),
    ]
    shape = jax.ShapeDtypeStruct
    return pl.pallas_call(
        partial(layer_kernel, geo),
        out_shape=(
            shape(tok.shape, bf16),
            shape(tok.shape, bf16),
            shape(tok.shape, f32),
            shape((2, ff, width), f32),
            shape((5, 8, width), f32),
            shape((steps, 8, chunk), f32),
        ),
        in_specs=[hbm] * 6 + [vmem] * 3,
        out_specs=(hbm,) * 4 + (vmem,) * 2,
        scratch_shapes=scratch,
        compiler_params=pltpu.CompilerParams(
            collective_id=1, has_side_effects=True, vmem_limit_bytes=64 * 1024 * 1024 - 256 * 1024),
        name="encoder_layer",
    )(tok, cot, w_all, tables[0], tables[1], tables[2], tables[3], vec, bias_in.reshape(steps, 1, chunk))


def local_fast(tokens, w_in, b_in, w_out, b_out, gain_one, shift_one, gain_two, shift_two, cotangent):
    both = ("seq", "batch")
    parts = lax.axis_size("seq")
    width = tokens.shape[2]
    shard = w_in.shape[1]
    w_all = lax.all_gather(jnp.stack([w_in.T, w_out]), both, axis=1, tiled=True)
    vectors = jnp.concatenate([b_in, gain_one, shift_one, gain_two, shift_two, b_out])
    vectors = lax.all_gather(vectors, both, axis=0, tiled=False).astype(f32)
    bias_in = vectors[:, :shard].reshape(-1)
    vec = vectors[:, shard:].reshape(vectors.shape[0], 5, -1)
    vec = jnp.moveaxis(vec, 1, 0).reshape(5, width)
    vec = jnp.concatenate([vec, jnp.zeros((3, width), f32)], axis=0)
    out, gtok, _, dw, small, bsum = layer_call(tokens, cotangent, w_all, vec, bias_in, parts)
    dw = lax.psum_scatter(dw, both, scatter_dimension=1, tiled=True)
    devices = vectors.shape[0]
    small = small.sum(1).reshape(5, devices, -1)
    small = jnp.moveaxis(small, 1, 0).reshape(devices, -1)
    bsum = bsum.sum(1).reshape(devices, -1)
    rest = lax.psum_scatter(jnp.concatenate([bsum, small], axis=1), both, scatter_dimension=0, tiled=False)
    grads = rest[shard:].reshape(5, -1)
    return (out, gtok, dw[0].T, rest[:shard], dw[1], grads[4], grads[0], grads[1], grads[2], grads[3])


def hidden_table(extent):
    idx_all = jnp.arange(extent, dtype=jnp.int32)
    angles = (idx_all[:, None] * idx_all[None, :] % extent).astype(jnp.float32) * (
        2.0 * math.pi / extent
    )
    factor = 1.0 / math.sqrt(extent)
    return jnp.concatenate([jnp.cos(angles) * factor, jnp.sin(angles) * factor], axis=1).astype(
        jnp.bfloat16
    )


def sequence_table(length):
    block_rows = min(512, length)
    block_count = length // block_rows
    col_ids = jnp.arange(length, dtype=jnp.int32)
    factor = 1.0 / math.sqrt(length)

    def table_rows(block_index):
        row_ids = block_index * block_rows + jnp.arange(block_rows, dtype=jnp.int32)
        angles = (row_ids[:, None] * col_ids[None, :] % length).astype(jnp.float32) * (
            2.0 * math.pi / length
        )
        return (jnp.stack([jnp.cos(angles), -jnp.sin(angles)]) * factor).astype(jnp.bfloat16)

    blocks = lax.map(table_rows, jnp.arange(block_count, dtype=jnp.int32))
    return jnp.moveaxis(blocks, 1, 0).reshape(2, length, length)


def normalize(values, gain, shift):
    center = values - jnp.mean(values, axis=-1, keepdims=True)
    inv_std = lax.rsqrt(jnp.mean(center * center, axis=-1, keepdims=True) + epsilon)
    normed = center * inv_std
    return (normed * gain + shift, normed, inv_std)


def norm_back(grad_out, normed, inv_std, gain):
    scaled = grad_out * gain
    centered = scaled - jnp.mean(scaled, axis=-1, keepdims=True)
    return inv_std * (centered - normed * jnp.mean(scaled * normed, axis=-1, keepdims=True))


def local(tokens, w_in, b_in, w_out, b_out, gain_one, shift_one, gain_two, shift_two, cotangent):
    batch_rows, seq_part, model_width = tokens.shape
    length = seq_part * lax.axis_size("seq")
    w_in_all, b_in_all, w_out_all, b_out_all, g_one_all, s_one_all, g_two_all, s_two_all = (
        lax.all_gather(w_in, ("seq", "batch"), axis=1, tiled=True),
        lax.all_gather(b_in, ("seq", "batch"), axis=0, tiled=True),
        lax.all_gather(w_out, ("seq", "batch"), axis=0, tiled=True),
        lax.all_gather(b_out, ("seq", "batch"), axis=0, tiled=True),
        lax.all_gather(gain_one, ("seq", "batch"), axis=0, tiled=True),
        lax.all_gather(shift_one, ("seq", "batch"), axis=0, tiled=True),
        lax.all_gather(gain_two, ("seq", "batch"), axis=0, tiled=True),
        lax.all_gather(shift_two, ("seq", "batch"), axis=0, tiled=True),
    )
    h_table = hidden_table(model_width)
    s_table = sequence_table(length)
    flat_tokens = tokens.reshape(-1, model_width)
    spectra = jnp.dot(flat_tokens, h_table, preferred_element_type=jnp.float32).astype(jnp.bfloat16)
    spectra = spectra.reshape(batch_rows, seq_part, 2, model_width)
    mixed_cols = jnp.einsum(
        "plm,bmpc->blc",
        s_table,
        lax.all_to_all(spectra, "seq", split_axis=3, concat_axis=1, tiled=True),
        preferred_element_type=jnp.float32,
    ).astype(jnp.bfloat16)
    mixed = lax.all_to_all(mixed_cols, "seq", split_axis=1, concat_axis=2, tiled=True)
    resid_one = flat_tokens.astype(jnp.float32) + mixed.reshape(-1, model_width).astype(jnp.float32)
    act_one, normed_one, inv_one = normalize(
        resid_one, g_one_all.astype(jnp.float32), s_one_all.astype(jnp.float32)
    )
    act_low = act_one.astype(jnp.bfloat16)
    pre_act = jnp.dot(act_low, w_in_all, preferred_element_type=jnp.float32) + b_in_all.astype(
        jnp.float32
    )
    activ, gelu_back = jax.vjp(partial(jax.nn.gelu, approximate=True), pre_act)
    hidden_low = activ.astype(jnp.bfloat16)
    branch = jnp.dot(hidden_low, w_out_all, preferred_element_type=jnp.float32) + b_out_all.astype(
        jnp.float32
    )
    resid_two = act_one + branch
    result, normed_two, inv_two = normalize(
        resid_two, g_two_all.astype(jnp.float32), s_two_all.astype(jnp.float32)
    )
    grad_out = cotangent.reshape(-1, model_width).astype(jnp.float32)
    grad_g_two = jnp.sum(grad_out * normed_two, axis=0)
    grad_s_two = jnp.sum(grad_out, axis=0)
    grad_r_two = norm_back(grad_out, normed_two, inv_two, g_two_all.astype(jnp.float32))
    grad_branch = grad_r_two.astype(jnp.bfloat16)
    grad_b_out = jnp.sum(grad_branch.astype(jnp.float32), axis=0)
    grad_w_out = jnp.einsum(
        "tf,td->fd", hidden_low, grad_branch, preferred_element_type=jnp.float32
    )
    grad_hidden = jnp.einsum(
        "td,fd->tf", grad_branch, w_out_all, preferred_element_type=jnp.float32
    )
    grad_pre = gelu_back(grad_hidden)[0].astype(jnp.bfloat16)
    grad_b_in = jnp.sum(grad_pre.astype(jnp.float32), axis=0)
    grad_w_in = jnp.einsum("td,tf->df", act_low, grad_pre, preferred_element_type=jnp.float32)
    grad_a_one = grad_r_two + jnp.einsum(
        "tf,df->td", grad_pre, w_in_all, preferred_element_type=jnp.float32
    )
    grad_g_one = jnp.sum(grad_a_one * normed_one, axis=0)
    grad_s_one = jnp.sum(grad_a_one, axis=0)
    grad_r_one = norm_back(grad_a_one, normed_one, inv_one, g_one_all.astype(jnp.float32))
    grad_mix = grad_r_one.astype(jnp.bfloat16).reshape(batch_rows, seq_part, model_width)
    spec_grad = jnp.einsum(
        "plm,blc->bmpc",
        s_table,
        lax.all_to_all(grad_mix, "seq", split_axis=2, concat_axis=1, tiled=True),
        preferred_element_type=jnp.float32,
    ).astype(jnp.bfloat16)
    grad_spec = lax.all_to_all(spec_grad, "seq", split_axis=1, concat_axis=3, tiled=True)
    grad_flat = grad_r_one + jnp.einsum(
        "te,de->td",
        grad_spec.reshape(-1, 2 * model_width),
        h_table,
        preferred_element_type=jnp.float32,
    )
    sum_w_in, sum_b_in, sum_w_out, sum_b_out, sum_g_one, sum_s_one, sum_g_two, sum_s_two = (
        lax.psum_scatter(grad_w_in, ("seq", "batch"), scatter_dimension=1, tiled=True),
        lax.psum_scatter(grad_b_in, ("seq", "batch"), scatter_dimension=0, tiled=True),
        lax.psum_scatter(grad_w_out, ("seq", "batch"), scatter_dimension=0, tiled=True),
        lax.psum_scatter(grad_b_out, ("seq", "batch"), scatter_dimension=0, tiled=True),
        lax.psum_scatter(grad_g_one, ("seq", "batch"), scatter_dimension=0, tiled=True),
        lax.psum_scatter(grad_s_one, ("seq", "batch"), scatter_dimension=0, tiled=True),
        lax.psum_scatter(grad_g_two, ("seq", "batch"), scatter_dimension=0, tiled=True),
        lax.psum_scatter(grad_s_two, ("seq", "batch"), scatter_dimension=0, tiled=True),
    )
    output = result.astype(jnp.bfloat16).reshape(batch_rows, seq_part, model_width)
    grad_tokens = grad_flat.astype(jnp.bfloat16).reshape(batch_rows, seq_part, model_width)
    return (
        output,
        grad_tokens,
        sum_w_in,
        sum_b_in,
        sum_w_out,
        sum_b_out,
        sum_g_one,
        sum_s_one,
        sum_g_two,
        sum_s_two,
    )


def solution(mesh):
    every = P(("seq", "batch"))

    def whole(tokens, w_in, *rest):
        parts = mesh.shape["seq"]
        fits = (
            parts == 8
            and tokens.shape[1] == 512 * parts
            and tokens.shape[2] % (32 * parts) == 0
            and w_in.shape[1] % (3 * 128) == 0
            and tokens.shape[0] == 4 * mesh.shape["batch"]
        )
        return jax.shard_map(
            local_fast if fits else local,
            mesh=mesh,
            in_specs=(
                P("batch", "seq", None),
                P(None, ("seq", "batch")),
                every,
                P(("seq", "batch"), None),
                every,
                every,
                every,
                every,
                every,
                P("batch", "seq", None),
            ),
            out_specs=(
                P("batch", "seq", None),
                P("batch", "seq", None),
                P(None, ("seq", "batch")),
                every,
                P(("seq", "batch"), None),
                every,
                every,
                every,
                every,
                every,
            ),
            check_vma=False,
        )(tokens, w_in, *rest)

    return whole
```

```python
from functools import partial
import math

import jax
import jax.numpy as jnp
import ml_dtypes
import numpy as np
from jax import lax
from jax.experimental import pallas as pl
from jax.experimental.pallas import tpu as pltpu
from jax.sharding import PartitionSpec as P

epsilon = 1e-05
f32, bf16 = jnp.float32, jnp.bfloat16
MESH = pl.DeviceIdType.MESH


def dot_nn(a, b):
    return lax.dot_general(a, b, (((1,), (0,)), ((), ())), preferred_element_type=f32)


def dot_nt(a, b):
    return lax.dot_general(a, b, (((1,), (1,)), ((), ())), preferred_element_type=f32)


def dot_tn(a, b):
    return lax.dot_general(a, b, (((0,), (0,)), ((), ())), preferred_element_type=f32)


def plan_columns(width, parts):
    pairs = width // 2 // parts
    r = np.arange(width)
    dev, kind, i = r // (2 * pairs), (r // pairs) % 2, r % pairs
    j = dev * pairs + i
    first = (kind == 1) & (j == 0)
    return j, kind, first


def packed_hidden(width, parts):
    j, kind, first = plan_columns(width, parts)
    k = np.arange(width)
    angle = (j[:, None] * k[None, :] % width) * (2.0 * math.pi / width)
    table = np.where(kind[:, None] == 0, np.cos(angle), np.sin(angle))
    nyquist = np.cos(np.pi * (k % 2))
    table = np.where(first[:, None], nyquist[None, :], table) / math.sqrt(width)
    return table.astype(np.float32).astype(ml_dtypes.bfloat16)


def column_order(width, parts):
    j, kind, first = plan_columns(width, parts)
    col = np.where(kind == 0, j, np.where(first, width // 2, (width - j) % width))
    return (col[:, None] == np.arange(width)[None, :]).astype(ml_dtypes.bfloat16)


def inner_table(span, length):
    a = np.arange(span)
    angle = (a[:, None] * a[None, :] % span) * (2.0 * math.pi / span)
    table = np.concatenate([np.cos(angle), np.sin(angle)], axis=0)
    return (table / math.sqrt(length)).astype(np.float32).astype(ml_dtypes.bfloat16)


def twiddles(parts, span):
    b = np.arange(parts)[:, None]
    angle = b * np.arange(span)[None, :] * (2.0 * math.pi / (parts * span))
    return np.concatenate([np.cos(angle), np.sin(angle)], axis=0).astype(np.float32)


def add(a, b):
    return (a[0] + b[0], a[1] + b[1])


def sub(a, b):
    return (a[0] - b[0], a[1] - b[1])


def minus_i(a):
    return (a[1], -a[0])


def dft4(x0, x1, x2, x3):
    t0, t1, t2, t3 = add(x0, x2), sub(x0, x2), add(x1, x3), sub(x1, x3)
    r = minus_i(t3)
    return add(t0, t2), add(t1, r), sub(t0, t2), sub(t1, r)


def dft8(x):
    e = dft4(x[0], x[2], x[4], x[6])
    o = dft4(x[1], x[3], x[5], x[7])
    h = math.sqrt(0.5)
    o1 = (h * (o[1][0] + o[1][1]), h * (o[1][1] - o[1][0]))
    o2 = minus_i(o[2])
    o3 = (h * (o[3][1] - o[3][0]), -h * (o[3][0] + o[3][1]))
    o = (o[0], o1, o2, o3)
    return [add(e[k], o[k]) for k in range(4)] + [sub(e[k], o[k]) for k in range(4)]


def radix_step(rec, tw, t_ref, parts, pairs, span):
    groups = pairs // 16
    count = 2 * parts * pairs

    def tile(u, carry):
        lanes = pl.ds(pl.multiple_of(u * 128, 128), 128)
        lanes_im = pl.ds(pl.multiple_of(span + u * 128, 128), 128)
        extra = [jnp.zeros((16, 128), f32), jnp.zeros((16, 128), f32)]
        row = lax.broadcasted_iota(jnp.int32, (16, 128), 0)
        for g in range(groups):
            x = []
            for s in range(parts):
                re = rec[s, g * 16:g * 16 + 16, lanes].astype(f32)
                im = rec[s, pairs + g * 16:pairs + g * 16 + 16, lanes].astype(f32)
                x.append((re, -im))
            y = dft8(x)
            for b in range(parts):
                c, s = tw[b:b + 1, lanes], tw[parts + b:parts + b + 1, lanes]
                conj = y[(parts - b) % parts]
                for kind, (zr, zi) in enumerate((y[b], (conj[0], -conj[1]))):
                    tr = c * zr + s * zi
                    ti = c * zi - s * zr
                    base = (kind * parts + b) * pairs + g * 16
                    t_ref[base:base + 16, lanes] = tr.astype(bf16)
                    t_ref[base:base + 16, lanes_im] = ti.astype(bf16)
                    if g == 0:
                        hit = row == kind * parts + b
                        extra[0] = jnp.where(hit, jnp.broadcast_to(-ti[0:1], (16, 128)), extra[0])
                        extra[1] = jnp.where(hit, jnp.broadcast_to(tr[0:1], (16, 128)), extra[1])
        t_ref[count:count + 16, lanes] = extra[0].astype(bf16)
        t_ref[count:count + 16, lanes_im] = extra[1].astype(bf16)
        return carry

    lax.fori_loop(0, span // 128, tile, 0)


def spread_step(o_ref, put, me, parts, pairs, span, u):
    count = 2 * parts * pairs
    lanes = pl.ds(pl.multiple_of(u * 128, 128), 128)
    low = lax.broadcasted_iota(jnp.int32, (16, 128), 1) < 64
    row = lax.broadcasted_iota(jnp.int32, (16, 128), 0)
    special = (row == 0) & (jnp.zeros((16, 128), jnp.int32) + me == 0)
    extra = o_ref[count:count + 16, lanes]
    for p in range(parts // 2):
        for g in range(pairs // 16):
            v = [[None, None], [None, None]]
            for kind in range(2):
                for h in range(2):
                    base = (kind * parts + 2 * p + h) * pairs + g * 16
                    v[kind][h] = o_ref[base:base + 16, lanes]
            if g == 0:
                for h in range(2):
                    b = 2 * p + h
                    even = 0.5 * (v[0][h] + v[1][h])
                    odd = jnp.broadcast_to(0.5 * (extra[b:b + 1] - extra[parts + b:parts + b + 1]), (16, 128))
                    v[0][h] = jnp.where(special, even, v[0][h])
                    v[1][h] = jnp.where(special, odd, v[1][h])
            for kind in range(2):
                v0, v1 = v[kind]
                rows = pl.ds(kind * pairs + g * 16, 16)
                cols = pl.ds(p * 128, 128)
                put(2 * u, rows, cols, jnp.where(low, v0, pltpu.roll(v1, 64, 1)).astype(bf16))
                put(2 * u + 1, rows, cols, jnp.where(low, pltpu.roll(v0, 64, 1), v1).astype(bf16))


def fold(v):
    total = v[0:8]
    for k in range(8, v.shape[0], 8):
        total = total + v[k:k + 8]
    return total


def rows_of(ref, at):
    return jnp.concatenate([ref[c, at, :] for c in range(ref.shape[0])], axis=1)


def set_rows(ref, at, value):
    for c in range(ref.shape[0]):
        ref[c, at, :] = value[:, c * 128:(c + 1) * 128]


def mean_of(v):
    return jnp.mean(v, axis=-1, keepdims=True)


def gelu_pair(x):
    k = math.sqrt(2.0 / math.pi)
    c = 0.044715
    x2 = x * x
    half = 0.5 + 0.5 * jnp.tanh(x * (k + (k * c) * x2))
    value = x * half
    slope = half + value * (1.0 - half) * (2.0 * k + (6.0 * k * c) * x2)
    return value, slope


def ffn_forward(x_get, nbuf, sbuf, alow, hid, slope, acc, w, vec, bias_in, chunk, rows_step):
    rows = nbuf.shape[1]

    def first(r, carry):
        at = pl.ds(pl.multiple_of(r * rows_step, rows_step), rows_step)
        v = x_get(at).astype(f32) + rows_of(nbuf, at)
        center = v - mean_of(v)
        inv = lax.rsqrt(mean_of(center * center) + epsilon)
        n = center * inv
        set_rows(nbuf, at, n)
        sbuf[at, :] = jnp.broadcast_to(inv, (rows_step, 128))
        alow[at, :] = (n * vec[0:1] + vec[1:2]).astype(bf16)
        return carry

    lax.fori_loop(0, rows // rows_step, first, 0)

    def step(c, carry):
        at = pl.ds(pl.multiple_of(c * chunk, chunk), chunk)
        pre = dot_nt(alow[...], w[0, at, :]) + bias_in[c]
        value, back = gelu_pair(pre)
        low = value.astype(bf16)
        hid[c] = low
        slope[c] = back.astype(bf16)
        part = dot_nn(low, w[1, at, :])

        @pl.when(c == 0)
        def _():
            acc[...] = part

        @pl.when(c > 0)
        def _():
            acc[...] += part

        return carry

    lax.fori_loop(0, hid.shape[0], step, 0)


def ffn_middle(nbuf, acc, glow, cot, outv, vec, sums, rows_step):
    rows = nbuf.shape[1]

    def second(r, carry):
        at = pl.ds(pl.multiple_of(r * rows_step, rows_step), rows_step)
        v = rows_of(nbuf, at) * vec[0:1] + vec[1:2] + (acc[at, :] + vec[4:5])
        center = v - mean_of(v)
        inv = lax.rsqrt(mean_of(center * center) + epsilon)
        n = center * inv
        outv[at, :] = (n * vec[2:3] + vec[3:4]).astype(bf16)
        g = cot[at, :].astype(f32)
        q = g * vec[2:3]
        gr = inv * (q - mean_of(q) - n * mean_of(q * n))
        acc[at, :] = gr
        low = gr.astype(bf16)
        glow[at, :] = low
        sums[2] += fold(g * n)
        sums[3] += fold(g)
        sums[4] += fold(low.astype(f32))
        return carry

    lax.fori_loop(0, rows // rows_step, second, 0)


def ffn_backward(nbuf, sbuf, alow, hid, slope, acc, glow, w, dw, bsum, vec, sums, chunk, rows_step, put):
    rows = nbuf.shape[1]

    def step(c, carry):
        at = pl.ds(pl.multiple_of(c * chunk, chunk), chunk)
        gh = dot_nt(glow[...], w[1, at, :])
        pre32 = gh * slope[c].astype(f32)
        gpre = pre32.astype(bf16)
        bsum[c] += fold(gpre.astype(f32))
        dw[1, at, :] += dot_tn(hid[c], glow[...])
        dw[0, at, :] += dot_tn(gpre, alow[...])
        acc[...] += dot_nn(gpre, w[0, at, :])
        return carry

    lax.fori_loop(0, hid.shape[0], step, 0)

    def last(r, carry):
        at = pl.ds(pl.multiple_of(r * rows_step, rows_step), rows_step)
        ga = acc[at, :]
        n = rows_of(nbuf, at)
        sums[0] += fold(ga * n)
        sums[1] += fold(ga)
        q = ga * vec[0:1]
        put(at, sbuf[at, 0:1] * (q - mean_of(q) - n * mean_of(q * n)))
        return carry

    lax.fori_loop(0, rows // rows_step, last, 0)


def layer_kernel(geo, tok, cot, w_all, hp_all, wd_all, cp_all, tw, vec, bias_in,
                 out, gtok, grow, dw_own, small,
                 tokv, cotv, outv, w, hp, wd, cp, dw, send1, recv1, send2, recv2, t_ref, o_ref,
                 nbuf, sbuf, alow, hid, slope, acc, glow, sums, bsum, rz, sv, rv,
                 ss1, rs1, ss2, rs2, free1, free2, load, io,
                 s_core, r_core, s_first, r_first, s_next, r_next, s_z, r_z, s_vec, r_vec, ready):
    parts, pairs, span, width, jobs, chunk, rows_step, planes = geo
    shard = dw.shape[1] // (parts * planes)
    me = lax.axis_index("seq")
    plane = lax.axis_index("batch")

    def peer(d):
        return lax.rem(me + d, parts)

    def load_of(k):
        if k < jobs:
            return pltpu.make_async_copy(tok.at[k], tokv.at[k], load.at[k])
        a, b = ((hp_all, hp), (wd_all, wd), (cp_all, cp))[k - jobs]
        return pltpu.make_async_copy(a, b, load.at[k])

    for k in (jobs, 0, 1, jobs + 1, 2, 3, jobs + 2):
        load_of(k).start()

    def weights(o, carry):
        for m in range(2):
            pltpu.make_async_copy(
                w_all.at[o, pl.ds(m * shard, shard)], w.at[m, pl.ds(pl.multiple_of(o * shard, shard), shard)],
                load.at[jobs + 3]).start()
        return carry

    lax.fori_loop(0, parts * planes, weights, 0)

    barrier = pltpu.get_barrier_semaphore()

    def greet(d, carry):
        pl.semaphore_signal(barrier, inc=1, device_id=(peer(d), plane), device_id_type=MESH)
        return carry

    def greet_z(d, carry):
        pl.semaphore_signal(barrier, inc=1, device_id=(me, lax.rem(plane + d, planes)), device_id_type=MESH)
        return carry

    lax.fori_loop(1, parts, greet, 0)
    lax.fori_loop(1, planes, greet_z, 0)
    pl.semaphore_wait(barrier, parts - 1 + planes - 1)

    def remote(send, recv, ss, rs, k, d):
        p = peer(d)
        return pltpu.make_async_remote_copy(
            src_ref=send.at[lax.rem(k, 2), p], dst_ref=recv.at[lax.rem(k, jobs), me],
            send_sem=ss.at[lax.rem(k, 2), d], recv_sem=rs.at[lax.rem(k, jobs), d],
            device_id=(p, plane), device_id_type=MESH)

    def own(send, recv, rs, k):
        return pltpu.make_async_copy(
            send.at[lax.rem(k, 2), me], recv.at[lax.rem(k, jobs), me], rs.at[lax.rem(k, jobs), 0])

    def wait_sends(send, recv, ss, rs, k):
        def one(d, carry):
            remote(send, recv, ss, rs, k, d).wait_send()
            return carry

        lax.fori_loop(1, parts, one, 0)

    def wait_recvs(send, recv, ss, rs, k):
        own(send, recv, rs, k).wait()

        def one(d, carry):
            source = lax.rem(me + parts - d, parts)
            slot = lax.rem(k, jobs)
            pltpu.make_async_remote_copy(
                src_ref=send.at[0, 0], dst_ref=recv.at[slot, source],
                send_sem=ss.at[0, d], recv_sem=rs.at[slot, d],
                device_id=(source, plane), device_id_type=MESH).wait_recv()
            return carry

        lax.fori_loop(1, parts, one, 0)

    def tell(sem, slot):
        def one(d, carry):
            pl.semaphore_signal(sem.at[slot], inc=1, device_id=(peer(d), plane), device_id_type=MESH)
            return carry

        lax.fori_loop(1, parts, one, 0)

    one_way = (send1, recv1, ss1, rs1)
    way_back = (send2, recv2, ss2, rs2)

    def hidden_job(k):
        table = dot_nt(hp[...], tokv[lax.rem(k, jobs)]).astype(bf16)
        send1[lax.rem(k, 2)] = table.reshape(parts, 2 * pairs, span)
        own(send1, recv1, rs1, k).start()

        def one(d, carry):
            remote(*one_way, k, d).start()
            return carry

        lax.fori_loop(1, parts, one, 0)

    def sequence_job(k, before_send):
        wait_recvs(*one_way, k)
        radix_step(recv1.at[lax.rem(k, jobs)], tw, t_ref, parts, pairs, span)
        o_ref[...] = dot_nn(t_ref[...], wd[...])
        before_send()
        slot = lax.rem(k, 2)

        def one(u, carry):
            def put(p, rows, cols, value):
                send2[slot, p, rows, cols] = value

            spread_step(o_ref, put, me, parts, pairs, span, u)
            for h in range(2):
                d = lax.rem(2 * u + h - me + parts, parts)

                @pl.when(d > 0)
                def _():
                    remote(*way_back, k, d).start()

                @pl.when(d == 0)
                def _():
                    own(send2, recv2, rs2, k).start()
            return carry

        lax.fori_loop(0, parts // 2, one, 0)

    def mixed_job(k):
        wait_recvs(*way_back, k)
        blocks = recv2[lax.rem(k, jobs)].reshape(width, span)
        natural = dot_tn(blocks, cp[...])
        step = span // parts
        for b in range(parts):
            for c in range(width // 128):
                nbuf[c, pl.ds(b, step, stride=parts), :] = natural[b * step:(b + 1) * step, c * 128:(c + 1) * 128]

    load_of(jobs).wait()
    for k in range(2):
        load_of(k).wait()

    def lead(k, carry):
        hidden_job(k)
        return carry

    lax.fori_loop(0, 2, lead, 0)
    dw[...] = jnp.zeros_like(dw)
    sums[...] = jnp.zeros_like(sums)
    bsum[...] = jnp.zeros_like(bsum)
    for k in (2, 3, jobs + 1, jobs + 2):
        load_of(k).wait()

    def fill(k, carry):
        sequence_job(k, lambda: None)
        tell(free1, k)
        wait_sends(*one_way, k)
        hidden_job(k + 2)
        return carry

    lax.fori_loop(0, 2, fill, 0)
    pltpu.make_async_copy(w, w, load.at[jobs + 3]).wait()

    def out_copy(i):
        return pltpu.make_async_copy(outv, out.at[i], io.at[0])

    def cot_copy(i):
        return pltpu.make_async_copy(cot.at[i], cotv, io.at[1])

    def row_copy(i):
        return pltpu.make_async_copy(acc, grow.at[i], io.at[2])

    def main(i, carry):
        cot_copy(i).start()
        mixed_job(i)
        tell(free2, i)
        ffn_forward(lambda at: tokv[i, at, :], nbuf, sbuf, alow, hid, slope, acc, w, vec, bias_in, chunk, rows_step)

        def before():
            wait_sends(*way_back, i)

            @pl.when(i >= 2)
            def _():
                pl.semaphore_wait(free2.at[lax.rem(i + 2, jobs)], parts - 1)

        sequence_job(i + 2, before)

        @pl.when(i < 2)
        def _():
            tell(free1, lax.rem(i + 2, jobs))

        cot_copy(i).wait()

        @pl.when(i > 0)
        def _():
            out_copy(i - 1).wait()

        ffn_middle(nbuf, acc, glow, cotv, outv, vec, sums, rows_step)
        out_copy(i).start()

        def put(at, value):
            acc[at, :] = value
            tokv[i, at, :] = value.astype(bf16)

        ffn_backward(nbuf, sbuf, alow, hid, slope, acc, glow, w, dw, bsum, vec, sums, chunk, rows_step, put)
        row_copy(i).start()
        wait_sends(*one_way, i + 2)
        pl.semaphore_wait(free1.at[i], parts - 1)
        hidden_job(i + jobs)
        row_copy(i).wait()
        return carry

    lax.fori_loop(0, jobs, main, 0)

    core, quad = lax.rem(me, 2), me // 2
    x, y = lax.rem(quad, 2), quad // 2
    partner = (me + 1 - 2 * core, plane)
    x_peer = (me + 2 - 4 * x, plane)
    y_peer = (me + 4 - 8 * y, plane)
    quads = parts // 2
    group = 2 * quads * shard

    def rows_at(start, count=shard):
        return pl.ds(pl.multiple_of(start, shard), count)

    def target(v):
        return lax.rem(plane + 1 + v, planes)

    def owned(q, c, v):
        return rows_at(((2 * q + c) * planes + target(v)) * shard)

    def send(src, dst, s, r, to):
        return pltpu.make_async_remote_copy(
            src_ref=src, dst_ref=dst, send_sem=s, recv_sem=r, device_id=to, device_id_type=MESH)

    def core_copy(v):
        at = rows_at(v * group, group)
        return send(w.at[0, at], w.at[1, at], s_core.at[v], r_core.at[v], partner)

    def first_copy(v, m):
        return send(w.at[0, rows_at((planes + v) * quads * shard + 2 * m * shard, 2 * shard)],
                    w.at[0, rows_at(v * quads * shard + 2 * m * shard, 2 * shard)],
                    s_first.at[v, m], r_first.at[v, m], (x_peer, y_peer)[m])

    def next_copy(v, m):
        return send(w.at[1, rows_at((2 * v + m) * shard)], (alow, glow)[m].at[rows_at(v * shard)],
                    s_next.at[v, m], r_next.at[v, m], (y_peer, x_peer)[m])

    def z_copy(v):
        return send(w.at[1, rows_at((2 * planes + 2 * v) * shard, 2 * shard)], rz.at[v],
                    s_z.at[v], r_z.at[v], (me, target(v)))

    def vec_copy(k):
        to = (partner, x_peer, y_peer)[k] if k < 3 else (me, target(k - 3))
        return send(sv.at[min(k, 3)], rv.at[k], s_vec.at[k], r_vec.at[k], to)

    def core_step(v, carry):
        for q in range(quads):
            for m in range(2):
                w[0, rows_at(v * group + (2 * q + m) * shard)] = dw[m, owned(q, 1 - core, v)].astype(bf16)
        core_copy(v).start()
        return carry

    def first_step(v, carry):
        core_copy(v).wait_recv()
        for q in range(quads):
            for m in range(2):
                at = owned(q, core, v)
                dw[m, at] += w[1, rows_at(v * group + (2 * q + m) * shard)].astype(f32)
        for k in range(2):
            for m in range(2):
                q = 2 * k + 1 - x if m == 0 else 2 * (1 - y) + k
                at = rows_at((planes + v) * quads * shard + (2 * m + k) * shard)
                w[0, at] = dw[m, owned(q, core, v)].astype(bf16)
        for m in range(2):
            first_copy(v, m).start()
        return carry

    def next_step(v, carry):
        for m in range(2):
            first_copy(v, m).wait_recv()
        for k in range(2):
            for m in range(2):
                q = 2 * k + x if m == 0 else 2 * y + k
                dw[m, owned(q, core, v)] += w[0, rows_at(v * quads * shard + (2 * m + k) * shard)].astype(f32)
        for m in range(2):
            q = 2 * (1 - y) + x if m == 0 else 2 * y + 1 - x
            w[1, rows_at((2 * v + m) * shard)] = dw[m, owned(q, core, v)].astype(bf16)
            next_copy(v, m).start()
        return carry

    def z_step(v, carry):
        for m in range(2):
            next_copy(v, m).wait_recv()
            dw[m, owned(quad, core, v)] += (alow, glow)[m][rows_at(v * shard)].astype(f32)

        @pl.when(v < planes - 1)
        def _():
            for m in range(2):
                at = rows_at((2 * planes + 2 * v + m) * shard)
                w[1, at] = dw[m, owned(quad, core, v)].astype(bf16)
            z_copy(v).start()

        return carry

    def vec_step(k):
        if k == 0:
            sv[0] = jnp.zeros_like(sv[0])
            for j in range(5):
                sv[0, j:j + 1] = jnp.sum(sums[j], axis=0, keepdims=True)
            piece = math.gcd(width, chunk)
            for f in range(0, bsum.shape[0] * chunk, piece):
                sv[0, 5 + f // width:6 + f // width, f % width:f % width + piece] = jnp.sum(
                    bsum[f // chunk, :, f % chunk:f % chunk + piece], axis=0, keepdims=True)
        else:
            vec_copy(k - 1).wait_recv()
            sv[k] = sv[k - 1] + rv[k - 1]
        for j in ((k,) if k < 3 else range(3, 2 + planes)):
            vec_copy(j).start()

    def gt_copy(i):
        return pltpu.make_async_copy(tokv.at[i], gtok.at[i], io.at[4 + i])

    def final(i):
        back = pltpu.make_async_copy(grow.at[i], acc, io.at[2])
        back.start()
        mixed_job(i + jobs)
        back.wait()
        for c in range(width // 128):
            tokv[i, :, c * 128:(c + 1) * 128] = (nbuf[c] + acc[:, c * 128:(c + 1) * 128]).astype(bf16)
        gt_copy(i).start()

    def drain(i, carry):
        final(i)

        def before():
            wait_sends(*way_back, i + 4)
            pl.semaphore_wait(free2.at[i + 2], parts - 1)

        sequence_job(i + 6, before)

        @pl.when(i == 0)
        def _():
            lax.fori_loop(0, planes, first_step, 0)

        return carry

    def finish(i, carry):
        final(i + 2)
        wait_sends(*way_back, i + 6)
        wait_sends(*one_way, i + 6)

        @pl.when(i == 0)
        def _():
            lax.fori_loop(0, planes, z_step, 0)

        return carry

    pl.semaphore_signal(ready.at[0], inc=1, device_id=partner, device_id_type=MESH)
    pl.semaphore_wait(ready.at[0], 1)
    lax.fori_loop(0, planes, core_step, 0)
    vec_step(0)

    def core_sent(v, carry):
        core_copy(v).wait_send()
        return carry

    lax.fori_loop(0, planes, core_sent, 0)
    pl.semaphore_signal(ready.at[1], inc=1, device_id=x_peer, device_id_type=MESH)
    pl.semaphore_signal(ready.at[2], inc=1, device_id=y_peer, device_id_type=MESH)
    vec_step(1)
    pl.semaphore_wait(ready.at[1], 1)
    pl.semaphore_wait(ready.at[2], 1)
    lax.fori_loop(0, 2, drain, 0)
    vec_step(2)
    lax.fori_loop(0, planes, next_step, 0)
    vec_step(3)
    lax.fori_loop(0, 2, finish, 0)
    own_rows = owned(quad, core, planes - 1)
    for m in range(2):
        dw_own[m] = dw[m, own_rows]
    for v in range(planes - 1):
        z_copy(v).wait_recv()
        for m in range(2):
            dw_own[m] += rz[v, m * shard:(m + 1) * shard].astype(f32)
    total = sv[3]
    for k in range(3, 2 + planes):
        vec_copy(k).wait_recv()
        total = total + rv[k]
    small[...] = total

    def sent(v, carry):
        for m in range(2):
            first_copy(v, m).wait_send()
            next_copy(v, m).wait_send()
        return carry

    lax.fori_loop(0, planes, sent, 0)
    for v in range(planes - 1):
        z_copy(v).wait_send()
    for k in range(2 + planes):
        vec_copy(k).wait_send()
    out_copy(jobs - 1).wait()
    for i in range(jobs):
        gt_copy(i).wait()


def layer_call(tok, cot, w_all, vec, bias_in, parts, planes):
    jobs, span, width = tok.shape
    ff = bias_in.size
    shard = ff // (parts * planes)
    pairs = width // 2 // parts
    chunk, rows_step = ff // 3, span // 2
    steps = ff // chunk
    length = span * parts
    geo = (parts, pairs, span, width, jobs, chunk, rows_step, planes)
    tables = (
        jnp.asarray(packed_hidden(width, parts)),
        jnp.asarray(inner_table(span, length)),
        jnp.asarray(column_order(width, parts)),
        jnp.asarray(twiddles(parts, span)),
    )
    hbm, vmem, dma = pl.BlockSpec(memory_space=pl.ANY), pl.BlockSpec(memory_space=pltpu.VMEM), pltpu.SemaphoreType.DMA
    block = (parts, 2 * pairs, span)
    scratch = [
        pltpu.VMEM((jobs, span, width), bf16),
        pltpu.VMEM((span, width), bf16),
        pltpu.VMEM((span, width), bf16),
        pltpu.VMEM((2, ff, width), bf16),
        pltpu.VMEM((width, width), bf16),
        pltpu.VMEM((2 * span, span), bf16),
        pltpu.VMEM((width, width), bf16),
        pltpu.VMEM((2, ff, width), f32),
        pltpu.VMEM((2,) + block, bf16),
        pltpu.VMEM((jobs,) + block, bf16),
        pltpu.VMEM((2,) + block, bf16),
        pltpu.VMEM((jobs,) + block, bf16),
        pltpu.VMEM((2 * parts * pairs + 16, 2 * span), bf16),
        pltpu.VMEM((2 * parts * pairs + 16, span), f32),
        pltpu.VMEM((width // 128, span, 128), f32),
        pltpu.VMEM((span, 128), f32),
        pltpu.VMEM((span, width), bf16),
        pltpu.VMEM((steps, span, chunk), bf16),
        pltpu.VMEM((steps, span, chunk), bf16),
        pltpu.VMEM((span, width), f32),
        pltpu.VMEM((span, width), bf16),
        pltpu.VMEM((5, 8, width), f32),
        pltpu.VMEM((steps, 8, chunk), f32),
        pltpu.VMEM((planes - 1, 2 * shard, width), bf16),
        pltpu.VMEM((4, 16, width), f32),
        pltpu.VMEM((2 + planes, 16, width), f32),
        dma((2, parts)), dma((jobs, parts)), dma((2, parts)), dma((jobs, parts)),
        pltpu.SemaphoreType.REGULAR((jobs,)), pltpu.SemaphoreType.REGULAR((jobs,)),
        dma((jobs + 4,)), dma((4 + jobs,)),
        dma((planes,)), dma((planes,)), dma((planes, 2)), dma((planes, 2)), dma((planes, 2)), dma((planes, 2)),
        dma((planes - 1,)), dma((planes - 1,)), dma((2 + planes,)), dma((2 + planes,)),
        pltpu.SemaphoreType.REGULAR((3,)),
    ]
    shape = jax.ShapeDtypeStruct
    return pl.pallas_call(
        partial(layer_kernel, geo),
        out_shape=(
            shape(tok.shape, bf16),
            shape(tok.shape, bf16),
            shape(tok.shape, f32),
            shape((2, shard, width), f32),
            shape((16, width), f32),
        ),
        in_specs=[hbm] * 6 + [vmem] * 3,
        out_specs=(hbm,) * 3 + (vmem,) * 2,
        scratch_shapes=scratch,
        compiler_params=pltpu.CompilerParams(
            collective_id=1, has_side_effects=True, vmem_limit_bytes=64 * 1024 * 1024 - 256 * 1024),
        name="encoder_layer",
    )(tok, cot, w_all, tables[0], tables[1], tables[2], tables[3], vec, bias_in.reshape(steps, 1, chunk))


def local_fast(tokens, w_in, b_in, w_out, b_out, gain_one, shift_one, gain_two, shift_two, cotangent):
    both = ("seq", "batch")
    parts = lax.axis_size("seq")
    width = tokens.shape[2]
    shard = w_in.shape[1]
    planes = lax.axis_size("batch")
    pad = 16 * width - shard - 5 * b_out.shape[0]
    vectors = jnp.concatenate([b_in, gain_one, shift_one, gain_two, shift_two, b_out, jnp.zeros((pad,), bf16)])
    packed = jnp.concatenate([w_in.T, w_out, vectors.reshape(16, width)], axis=0)
    w_all = lax.all_gather(packed, both, axis=0, tiled=False)
    vectors = w_all[:, 2 * shard].astype(f32)
    bias_in = vectors[:, :shard].reshape(-1)
    vec = vectors[:, shard:shard + 5 * b_out.shape[0]].reshape(vectors.shape[0], 5, -1)
    vec = jnp.moveaxis(vec, 1, 0).reshape(5, width)
    vec = jnp.concatenate([vec, jnp.zeros((3, width), f32)], axis=0)
    out, gtok, _, dw, small = layer_call(tokens, cotangent, w_all, vec, bias_in, parts, planes)
    owner = lax.axis_index("seq") * planes + lax.axis_index("batch")
    grad_b_in = lax.dynamic_slice(small[5:9].reshape(-1), (owner * shard,), (shard,))
    part = b_out.shape[0]
    rest = lax.dynamic_slice(small[:5], (0, owner * part), (5, part))
    return (out, gtok, dw[0].T, grad_b_in, dw[1], rest[4], rest[0], rest[1], rest[2], rest[3])


def hidden_table(extent):
    idx_all = jnp.arange(extent, dtype=jnp.int32)
    angles = (idx_all[:, None] * idx_all[None, :] % extent).astype(jnp.float32) * (
        2.0 * math.pi / extent
    )
    factor = 1.0 / math.sqrt(extent)
    return jnp.concatenate([jnp.cos(angles) * factor, jnp.sin(angles) * factor], axis=1).astype(
        jnp.bfloat16
    )


def sequence_table(length):
    block_rows = min(512, length)
    block_count = length // block_rows
    col_ids = jnp.arange(length, dtype=jnp.int32)
    factor = 1.0 / math.sqrt(length)

    def table_rows(block_index):
        row_ids = block_index * block_rows + jnp.arange(block_rows, dtype=jnp.int32)
        angles = (row_ids[:, None] * col_ids[None, :] % length).astype(jnp.float32) * (
            2.0 * math.pi / length
        )
        return (jnp.stack([jnp.cos(angles), -jnp.sin(angles)]) * factor).astype(jnp.bfloat16)

    blocks = lax.map(table_rows, jnp.arange(block_count, dtype=jnp.int32))
    return jnp.moveaxis(blocks, 1, 0).reshape(2, length, length)


def normalize(values, gain, shift):
    center = values - jnp.mean(values, axis=-1, keepdims=True)
    inv_std = lax.rsqrt(jnp.mean(center * center, axis=-1, keepdims=True) + epsilon)
    normed = center * inv_std
    return (normed * gain + shift, normed, inv_std)


def norm_back(grad_out, normed, inv_std, gain):
    scaled = grad_out * gain
    centered = scaled - jnp.mean(scaled, axis=-1, keepdims=True)
    return inv_std * (centered - normed * jnp.mean(scaled * normed, axis=-1, keepdims=True))


def local(tokens, w_in, b_in, w_out, b_out, gain_one, shift_one, gain_two, shift_two, cotangent):
    batch_rows, seq_part, model_width = tokens.shape
    length = seq_part * lax.axis_size("seq")
    w_in_all, b_in_all, w_out_all, b_out_all, g_one_all, s_one_all, g_two_all, s_two_all = (
        lax.all_gather(w_in, ("seq", "batch"), axis=1, tiled=True),
        lax.all_gather(b_in, ("seq", "batch"), axis=0, tiled=True),
        lax.all_gather(w_out, ("seq", "batch"), axis=0, tiled=True),
        lax.all_gather(b_out, ("seq", "batch"), axis=0, tiled=True),
        lax.all_gather(gain_one, ("seq", "batch"), axis=0, tiled=True),
        lax.all_gather(shift_one, ("seq", "batch"), axis=0, tiled=True),
        lax.all_gather(gain_two, ("seq", "batch"), axis=0, tiled=True),
        lax.all_gather(shift_two, ("seq", "batch"), axis=0, tiled=True),
    )
    h_table = hidden_table(model_width)
    s_table = sequence_table(length)
    flat_tokens = tokens.reshape(-1, model_width)
    spectra = jnp.dot(flat_tokens, h_table, preferred_element_type=jnp.float32).astype(jnp.bfloat16)
    spectra = spectra.reshape(batch_rows, seq_part, 2, model_width)
    mixed_cols = jnp.einsum(
        "plm,bmpc->blc",
        s_table,
        lax.all_to_all(spectra, "seq", split_axis=3, concat_axis=1, tiled=True),
        preferred_element_type=jnp.float32,
    ).astype(jnp.bfloat16)
    mixed = lax.all_to_all(mixed_cols, "seq", split_axis=1, concat_axis=2, tiled=True)
    resid_one = flat_tokens.astype(jnp.float32) + mixed.reshape(-1, model_width).astype(jnp.float32)
    act_one, normed_one, inv_one = normalize(
        resid_one, g_one_all.astype(jnp.float32), s_one_all.astype(jnp.float32)
    )
    act_low = act_one.astype(jnp.bfloat16)
    pre_act = jnp.dot(act_low, w_in_all, preferred_element_type=jnp.float32) + b_in_all.astype(
        jnp.float32
    )
    activ, gelu_back = jax.vjp(partial(jax.nn.gelu, approximate=True), pre_act)
    hidden_low = activ.astype(jnp.bfloat16)
    branch = jnp.dot(hidden_low, w_out_all, preferred_element_type=jnp.float32) + b_out_all.astype(
        jnp.float32
    )
    resid_two = act_one + branch
    result, normed_two, inv_two = normalize(
        resid_two, g_two_all.astype(jnp.float32), s_two_all.astype(jnp.float32)
    )
    grad_out = cotangent.reshape(-1, model_width).astype(jnp.float32)
    grad_g_two = jnp.sum(grad_out * normed_two, axis=0)
    grad_s_two = jnp.sum(grad_out, axis=0)
    grad_r_two = norm_back(grad_out, normed_two, inv_two, g_two_all.astype(jnp.float32))
    grad_branch = grad_r_two.astype(jnp.bfloat16)
    grad_b_out = jnp.sum(grad_branch.astype(jnp.float32), axis=0)
    grad_w_out = jnp.einsum(
        "tf,td->fd", hidden_low, grad_branch, preferred_element_type=jnp.float32
    )
    grad_hidden = jnp.einsum(
        "td,fd->tf", grad_branch, w_out_all, preferred_element_type=jnp.float32
    )
    grad_pre = gelu_back(grad_hidden)[0].astype(jnp.bfloat16)
    grad_b_in = jnp.sum(grad_pre.astype(jnp.float32), axis=0)
    grad_w_in = jnp.einsum("td,tf->df", act_low, grad_pre, preferred_element_type=jnp.float32)
    grad_a_one = grad_r_two + jnp.einsum(
        "tf,df->td", grad_pre, w_in_all, preferred_element_type=jnp.float32
    )
    grad_g_one = jnp.sum(grad_a_one * normed_one, axis=0)
    grad_s_one = jnp.sum(grad_a_one, axis=0)
    grad_r_one = norm_back(grad_a_one, normed_one, inv_one, g_one_all.astype(jnp.float32))
    grad_mix = grad_r_one.astype(jnp.bfloat16).reshape(batch_rows, seq_part, model_width)
    spec_grad = jnp.einsum(
        "plm,blc->bmpc",
        s_table,
        lax.all_to_all(grad_mix, "seq", split_axis=2, concat_axis=1, tiled=True),
        preferred_element_type=jnp.float32,
    ).astype(jnp.bfloat16)
    grad_spec = lax.all_to_all(spec_grad, "seq", split_axis=1, concat_axis=3, tiled=True)
    grad_flat = grad_r_one + jnp.einsum(
        "te,de->td",
        grad_spec.reshape(-1, 2 * model_width),
        h_table,
        preferred_element_type=jnp.float32,
    )
    sum_w_in, sum_b_in, sum_w_out, sum_b_out, sum_g_one, sum_s_one, sum_g_two, sum_s_two = (
        lax.psum_scatter(grad_w_in, ("seq", "batch"), scatter_dimension=1, tiled=True),
        lax.psum_scatter(grad_b_in, ("seq", "batch"), scatter_dimension=0, tiled=True),
        lax.psum_scatter(grad_w_out, ("seq", "batch"), scatter_dimension=0, tiled=True),
        lax.psum_scatter(grad_b_out, ("seq", "batch"), scatter_dimension=0, tiled=True),
        lax.psum_scatter(grad_g_one, ("seq", "batch"), scatter_dimension=0, tiled=True),
        lax.psum_scatter(grad_s_one, ("seq", "batch"), scatter_dimension=0, tiled=True),
        lax.psum_scatter(grad_g_two, ("seq", "batch"), scatter_dimension=0, tiled=True),
        lax.psum_scatter(grad_s_two, ("seq", "batch"), scatter_dimension=0, tiled=True),
    )
    output = result.astype(jnp.bfloat16).reshape(batch_rows, seq_part, model_width)
    grad_tokens = grad_flat.astype(jnp.bfloat16).reshape(batch_rows, seq_part, model_width)
    return (
        output,
        grad_tokens,
        sum_w_in,
        sum_b_in,
        sum_w_out,
        sum_b_out,
        sum_g_one,
        sum_s_one,
        sum_g_two,
        sum_s_two,
    )


def solution(mesh):
    every = P(("seq", "batch"))

    def whole(tokens, w_in, *rest):
        parts = mesh.shape["seq"]
        fits = (
            parts == 8
            and tokens.shape[1] == 512 * parts
            and tokens.shape[2] % (32 * parts) == 0
            and w_in.shape[1] % (3 * 128) == 0
            and tokens.shape[0] == 4 * mesh.shape["batch"]
        )
        return jax.shard_map(
            local_fast if fits else local,
            mesh=mesh,
            in_specs=(
                P("batch", "seq", None),
                P(None, ("seq", "batch")),
                every,
                P(("seq", "batch"), None),
                every,
                every,
                every,
                every,
                every,
                P("batch", "seq", None),
            ),
            out_specs=(
                P("batch", "seq", None),
                P("batch", "seq", None),
                P(None, ("seq", "batch")),
                every,
                P(("seq", "batch"), None),
                every,
                every,
                every,
                every,
                every,
            ),
            check_vma=False,
        )(tokens, w_in, *rest)

    return whole
```

```python
from functools import partial
import math

import jax
import jax.numpy as jnp
import ml_dtypes
import numpy as np
from jax import lax
from jax.experimental import pallas as pl
from jax.experimental.pallas import tpu as pltpu
from jax.sharding import PartitionSpec as P

epsilon = 1e-05
f32, bf16 = jnp.float32, jnp.bfloat16
MESH = pl.DeviceIdType.MESH


def dot_nn(a, b):
    return lax.dot_general(a, b, (((1,), (0,)), ((), ())), preferred_element_type=f32)


def dot_nt(a, b):
    return lax.dot_general(a, b, (((1,), (1,)), ((), ())), preferred_element_type=f32)


def dot_tn(a, b):
    return lax.dot_general(a, b, (((0,), (0,)), ((), ())), preferred_element_type=f32)


def plan_columns(width, parts):
    pairs = width // 2 // parts
    r = np.arange(width)
    dev, kind, i = r // (2 * pairs), (r // pairs) % 2, r % pairs
    j = dev * pairs + i
    first = (kind == 1) & (j == 0)
    return j, kind, first


def packed_hidden(width, parts):
    j, kind, first = plan_columns(width, parts)
    k = np.arange(width)
    angle = (j[:, None] * k[None, :] % width) * (2.0 * math.pi / width)
    table = np.where(kind[:, None] == 0, np.cos(angle), np.sin(angle))
    nyquist = np.cos(np.pi * (k % 2))
    table = np.where(first[:, None], nyquist[None, :], table) / math.sqrt(width)
    return table.astype(np.float32).astype(ml_dtypes.bfloat16)


def column_order(width, parts):
    j, kind, first = plan_columns(width, parts)
    col = np.where(kind == 0, j, np.where(first, width // 2, (width - j) % width))
    return (col[:, None] == np.arange(width)[None, :]).astype(ml_dtypes.bfloat16)


def inner_table(span, length):
    a = np.arange(span)
    angle = (a[:, None] * a[None, :] % span) * (2.0 * math.pi / span)
    table = np.concatenate([np.cos(angle), np.sin(angle)], axis=0)
    return (table / math.sqrt(length)).astype(np.float32).astype(ml_dtypes.bfloat16)


def twiddles(parts, span):
    b = np.arange(parts)[:, None]
    angle = b * np.arange(span)[None, :] * (2.0 * math.pi / (parts * span))
    return np.concatenate([np.cos(angle), np.sin(angle)], axis=0).astype(np.float32)


def add(a, b):
    return (a[0] + b[0], a[1] + b[1])


def sub(a, b):
    return (a[0] - b[0], a[1] - b[1])


def minus_i(a):
    return (a[1], -a[0])


def dft4(x0, x1, x2, x3):
    t0, t1, t2, t3 = add(x0, x2), sub(x0, x2), add(x1, x3), sub(x1, x3)
    r = minus_i(t3)
    return add(t0, t2), add(t1, r), sub(t0, t2), sub(t1, r)


def dft8(x):
    e = dft4(x[0], x[2], x[4], x[6])
    o = dft4(x[1], x[3], x[5], x[7])
    h = math.sqrt(0.5)
    o1 = (h * (o[1][0] + o[1][1]), h * (o[1][1] - o[1][0]))
    o2 = minus_i(o[2])
    o3 = (h * (o[3][1] - o[3][0]), -h * (o[3][0] + o[3][1]))
    o = (o[0], o1, o2, o3)
    return [add(e[k], o[k]) for k in range(4)] + [sub(e[k], o[k]) for k in range(4)]


def radix_step(rec, tw, t_ref, parts, pairs, span):
    groups = pairs // 16
    count = 2 * parts * pairs

    def tile(u, carry):
        lanes = pl.ds(pl.multiple_of(u * 128, 128), 128)
        lanes_im = pl.ds(pl.multiple_of(span + u * 128, 128), 128)
        extra = [jnp.zeros((16, 128), f32), jnp.zeros((16, 128), f32)]
        row = lax.broadcasted_iota(jnp.int32, (16, 128), 0)
        for g in range(groups):
            x = []
            for s in range(parts):
                re = rec[s, g * 16:g * 16 + 16, lanes].astype(f32)
                im = rec[s, pairs + g * 16:pairs + g * 16 + 16, lanes].astype(f32)
                x.append((re, -im))
            y = dft8(x)
            for b in range(parts):
                c, s = tw[b:b + 1, lanes], tw[parts + b:parts + b + 1, lanes]
                conj = y[(parts - b) % parts]
                for kind, (zr, zi) in enumerate((y[b], (conj[0], -conj[1]))):
                    tr = c * zr + s * zi
                    ti = c * zi - s * zr
                    base = (kind * parts + b) * pairs + g * 16
                    t_ref[base:base + 16, lanes] = tr.astype(bf16)
                    t_ref[base:base + 16, lanes_im] = ti.astype(bf16)
                    if g == 0:
                        hit = row == kind * parts + b
                        extra[0] = jnp.where(hit, jnp.broadcast_to(-ti[0:1], (16, 128)), extra[0])
                        extra[1] = jnp.where(hit, jnp.broadcast_to(tr[0:1], (16, 128)), extra[1])
        t_ref[count:count + 16, lanes] = extra[0].astype(bf16)
        t_ref[count:count + 16, lanes_im] = extra[1].astype(bf16)
        return carry

    lax.fori_loop(0, span // 128, tile, 0)


def spread_step(o_ref, put, me, parts, pairs, u, half):
    count = 2 * parts * pairs
    lanes = pl.ds(pl.multiple_of((u - half * parts // 4) * 128, 128), 128)
    low = lax.broadcasted_iota(jnp.int32, (16, 128), 1) < 64
    row = lax.broadcasted_iota(jnp.int32, (16, 128), 0)
    special = (row == 0) & (jnp.zeros((16, 128), jnp.int32) + me == 0)
    extra = o_ref[count:count + 16, lanes]
    for p in range(parts // 2):
        for g in range(pairs // 16):
            v = [[None, None], [None, None]]
            for kind in range(2):
                for h in range(2):
                    base = (kind * parts + 2 * p + h) * pairs + g * 16
                    v[kind][h] = o_ref[base:base + 16, lanes]
            if g == 0:
                for h in range(2):
                    b = 2 * p + h
                    even = 0.5 * (v[0][h] + v[1][h])
                    odd = jnp.broadcast_to(0.5 * (extra[b:b + 1] - extra[parts + b:parts + b + 1]), (16, 128))
                    v[0][h] = jnp.where(special, even, v[0][h])
                    v[1][h] = jnp.where(special, odd, v[1][h])
            for kind in range(2):
                v0, v1 = v[kind]
                rows = pl.ds(kind * pairs + g * 16, 16)
                cols = pl.ds(p * 128, 128)
                put(2 * u, rows, cols, jnp.where(low, v0, pltpu.roll(v1, 64, 1)).astype(bf16))
                put(2 * u + 1, rows, cols, jnp.where(low, pltpu.roll(v0, 64, 1), v1).astype(bf16))


def fold(v):
    total = v[0:8]
    for k in range(8, v.shape[0], 8):
        total = total + v[k:k + 8]
    return total


def rows_of(ref, at):
    return jnp.concatenate([ref[c, at, :] for c in range(ref.shape[0])], axis=1)


def set_rows(ref, at, value):
    for c in range(ref.shape[0]):
        ref[c, at, :] = value[:, c * 128:(c + 1) * 128]


def mean_of(v):
    return jnp.mean(v, axis=-1, keepdims=True)


def gelu_pair(x):
    k = math.sqrt(2.0 / math.pi)
    c = 0.044715
    x2 = x * x
    half = 0.5 + 0.5 * jnp.tanh(x * (k + (k * c) * x2))
    value = x * half
    slope = half + value * (1.0 - half) * (2.0 * k + (6.0 * k * c) * x2)
    return value, slope


def ffn_forward(x_get, nbuf, sbuf, alow, hid, slope, acc, weight, vec, bias_in, rows_step):
    rows = nbuf.shape[1]

    def first(r, carry):
        at = pl.ds(pl.multiple_of(r * rows_step, rows_step), rows_step)
        v = x_get(at).astype(f32) + rows_of(nbuf, at)
        center = v - mean_of(v)
        inv = lax.rsqrt(mean_of(center * center) + epsilon)
        n = center * inv
        set_rows(nbuf, at, n)
        sbuf[at, :] = jnp.broadcast_to(inv, (rows_step, 128))
        alow[at, :] = (n * vec[0:1] + vec[1:2]).astype(bf16)
        return carry

    lax.fori_loop(0, rows // rows_step, first, 0)

    def step(c, carry):
        pre = dot_nt(alow[...], weight(0, c)) + bias_in[c]
        value, back = gelu_pair(pre)
        low = value.astype(bf16)
        hid[c] = low
        slope[c] = back.astype(bf16)
        part = dot_nn(low, weight(1, c))

        @pl.when(c == 0)
        def _():
            acc[...] = part

        @pl.when(c > 0)
        def _():
            acc[...] += part

        return carry

    lax.fori_loop(0, hid.shape[0], step, 0)


def ffn_middle(nbuf, acc, glow, cot, outv, vec, sums, rows_step):
    rows = nbuf.shape[1]

    def second(r, carry):
        at = pl.ds(pl.multiple_of(r * rows_step, rows_step), rows_step)
        v = rows_of(nbuf, at) * vec[0:1] + vec[1:2] + (acc[at, :] + vec[4:5])
        center = v - mean_of(v)
        inv = lax.rsqrt(mean_of(center * center) + epsilon)
        n = center * inv
        outv[at, :] = (n * vec[2:3] + vec[3:4]).astype(bf16)
        g = cot[at, :].astype(f32)
        q = g * vec[2:3]
        gr = inv * (q - mean_of(q) - n * mean_of(q * n))
        acc[at, :] = gr
        low = gr.astype(bf16)
        glow[at, :] = low
        sums[2] += fold(g * n)
        sums[3] += fold(g)
        sums[4] += fold(low.astype(f32))
        return carry

    lax.fori_loop(0, rows // rows_step, second, 0)


def ffn_backward(nbuf, sbuf, alow, hid, slope, acc, glow, weight, dw, bsum, vec, sums, chunk, rows_step, put):
    rows = nbuf.shape[1]

    def step(c, carry):
        at = pl.ds(pl.multiple_of(c * chunk, chunk), chunk)
        gh = dot_nt(glow[...], weight(1, c))
        pre32 = gh * slope[c].astype(f32)
        gpre = pre32.astype(bf16)
        bsum[c] += fold(gpre.astype(f32))
        dw[1, at, :] += dot_tn(hid[c], glow[...])
        dw[0, at, :] += dot_tn(gpre, alow[...])
        acc[...] += dot_nn(gpre, weight(0, c))
        return carry

    lax.fori_loop(0, hid.shape[0], step, 0)

    def last(r, carry):
        at = pl.ds(pl.multiple_of(r * rows_step, rows_step), rows_step)
        ga = acc[at, :]
        n = rows_of(nbuf, at)
        sums[0] += fold(ga * n)
        sums[1] += fold(ga)
        q = ga * vec[0:1]
        put(at, sbuf[at, 0:1] * (q - mean_of(q) - n * mean_of(q * n)))
        return carry

    lax.fori_loop(0, rows // rows_step, last, 0)


def layer_kernel(geo, tok, cot, win_own, wout_own, vec_own, hp_all, wd_all, cp_all, tw,
                 out, gtok, grow, dw_own, small,
                 tokv, cotv, outv, w0, w1, hp, wd, cp, dw, send1, recv1, send2, recv2, t_ref, o_ref,
                 nbuf, sbuf, alow, hid, slope, acc, glow, sums, bsum, rz, sv, rv, vec, bias_in,
                 ss1, rs1, ss2, rs2, free1, free2, load, io,
                 s_core, r_core, s_first, r_first, s_next, r_next, s_z, r_z, s_vec, r_vec, ready,
                 s_spread, r_spread, s_relay, r_relay, s_pair, r_pair):
    parts, pairs, span, width, jobs, slots, chunk, rows_step, planes = geo
    shard = dw.shape[1] // (parts * planes)
    me = lax.axis_index("seq")
    plane = lax.axis_index("batch")

    def peer(d):
        return lax.rem(me + d, parts)

    def load_of(k):
        if k < jobs:
            return pltpu.make_async_copy(tok.at[k], tokv.at[k], load.at[k])
        a, b = ((hp_all, hp), (wd_all, wd), (cp_all, cp))[k - jobs]
        return pltpu.make_async_copy(a, b, load.at[k])

    for k in (jobs, 0, 1, jobs + 1, 2, 3, jobs + 2):
        load_of(k).start()

    core, quad = lax.rem(me, 2), me // 2
    quads = parts // 2
    partner = (me + 1 - 2 * core, plane)
    last = planes - 1

    def send(src, dst, s, r, to):
        return pltpu.make_async_remote_copy(
            src_ref=src, dst_ref=dst, send_sem=s, recv_sem=r, device_id=to, device_id_type=MESH)

    own_loads = (
        pltpu.make_async_copy(win_own, w0.at[quad, core, plane, pl.ds(0, shard)], load.at[jobs + 3]),
        pltpu.make_async_copy(vec_own, w0.at[quad, core, plane, pl.ds(shard, 16)], load.at[jobs + 4]),
        pltpu.make_async_copy(wout_own, w1.at[quad, core, plane], load.at[jobs + 5]),
    )
    for copy in own_loads:
        copy.start()

    barrier = pltpu.get_barrier_semaphore()

    def greet(d, carry):
        pl.semaphore_signal(barrier, inc=1, device_id=(peer(d), plane), device_id_type=MESH)
        return carry

    def greet_z(d, carry):
        pl.semaphore_signal(barrier, inc=1, device_id=(me, lax.rem(plane + d, planes)), device_id_type=MESH)
        return carry

    lax.fori_loop(1, parts, greet, 0)
    lax.fori_loop(1, planes, greet_z, 0)
    pl.semaphore_wait(barrier, parts - 1 + planes - 1)

    def remote(send, recv, ss, rs, k, d):
        p = peer(d)
        return pltpu.make_async_remote_copy(
            src_ref=send.at[lax.rem(k, 2), p], dst_ref=recv.at[lax.rem(k, slots), me],
            send_sem=ss.at[lax.rem(k, 2), d], recv_sem=rs.at[lax.rem(k, slots), d],
            device_id=(p, plane), device_id_type=MESH)

    def own(send, recv, rs, k):
        return pltpu.make_async_copy(
            send.at[lax.rem(k, 2), me], recv.at[lax.rem(k, slots), me], rs.at[lax.rem(k, slots), 0])

    def wait_sends(send, recv, ss, rs, k):
        def one(d, carry):
            remote(send, recv, ss, rs, k, d).wait_send()
            return carry

        lax.fori_loop(1, parts, one, 0)

    def wait_recvs(send, recv, ss, rs, k):
        own(send, recv, rs, k).wait()

        def one(d, carry):
            source = lax.rem(me + parts - d, parts)
            slot = lax.rem(k, slots)
            pltpu.make_async_remote_copy(
                src_ref=send.at[0, 0], dst_ref=recv.at[slot, source],
                send_sem=ss.at[0, d], recv_sem=rs.at[slot, d],
                device_id=(source, plane), device_id_type=MESH).wait_recv()
            return carry

        lax.fori_loop(1, parts, one, 0)

    def tell(sem, k):
        def one(d, carry):
            pl.semaphore_signal(sem.at[lax.rem(k, slots)], inc=1, device_id=(peer(d), plane), device_id_type=MESH)
            return carry

        lax.fori_loop(1, parts, one, 0)

    def in_plane(d):
        return 2 * lax.rem(quad + d, quads) + core

    def along(d):
        return lax.rem(plane + d, planes)

    def spread_z(d):
        block = w0.at[quad, core, plane]
        return send(block, block, s_spread.at[0, d], r_spread.at[0, d], (me, along(d)))

    def spread_out(d):
        block = w1.at[quad, core, plane]
        return send(block, block, s_spread.at[1, d], r_spread.at[1, d], (in_plane(d), plane))

    def spread_in(d):
        block = w0.at[quad, core]
        return send(block, block, s_spread.at[2, d], r_spread.at[2, d], (in_plane(d), plane))

    def relay(origin, up):
        block = w1.at[:, core, origin]
        return send(block, block, s_relay.at[up, origin], r_relay.at[origin], (me, plane + 2 * up - 1))

    def pair_in(q):
        block = w0.at[q, core]
        return send(block, block, s_pair.at[0, q], r_pair.at[0, q], partner)

    def pair_out(origin):
        block = w1.at[:, core, origin]
        return send(block, block, s_pair.at[1, origin], r_pair.at[1, origin], partner)

    def relay_step(j):
        below, above = plane - 1 - j, plane + 1 + j

        @pl.when(below >= 0)
        def _():
            relay(below, 1).wait_recv()

            @pl.when(plane < last)
            def _():
                relay(below, 1).start()

            pair_out(below).start()

        @pl.when(above <= last)
        def _():
            relay(above, 0).wait_recv()

            @pl.when(plane > 0)
            def _():
                relay(above, 0).start()

            pair_out(above).start()

    def gather_start():
        for copy in own_loads:
            copy.wait()
        for d in range(1, planes):
            spread_z(d).start()
        for d in range(1, quads):
            spread_out(d).start()

    def gather_out():
        for d in range(1, quads):
            spread_out(d).wait_recv()

        @pl.when(plane < last)
        def _():
            relay(plane, 1).start()

        @pl.when(plane > 0)
        def _():
            relay(plane, 0).start()

        pair_out(plane).start()

    def gather_in():
        for d in range(1, planes):
            spread_z(d).wait_recv()
        for d in range(1, quads):
            spread_in(d).start()
        pair_in(quad).start()

    def gather_pass():
        for d in range(1, quads):
            spread_in(d).wait_recv()
            pair_in(lax.rem(quad + quads - d, quads)).start()

    def gather_end():
        for q in range(quads):
            pair_in(q).wait_recv()
        for origin in range(planes):
            pair_out(origin).wait_recv()

        def one(o, carry):
            rest = lax.rem(o, 2 * planes)
            block = w0[o // (2 * planes), rest // planes, lax.rem(rest, planes), shard:shard + 16, :]
            return carry + block.astype(f32)

        total = lax.fori_loop(0, parts * planes, one, jnp.zeros((16, width), f32))
        vec[...] = total[0:8]
        for f in range(0, bsum.shape[0] * chunk, width):
            bias_in[f // chunk, 0:1, f % chunk:f % chunk + width] = total[5 + f // width:6 + f // width]

    def gather_sent():
        for d in range(1, planes):
            spread_z(d).wait_send()
        for d in range(1, quads):
            spread_out(d).wait_send()
            spread_in(d).wait_send()
        for q in range(quads):
            pair_in(q).wait_send()
        for origin in range(planes):
            pair_out(origin).wait_send()

            @pl.when((plane < last) & (origin <= plane))
            def _():
                relay(origin, 1).wait_send()

            @pl.when((plane > 0) & (origin >= plane))
            def _():
                relay(origin, 0).wait_send()

    def weight(m, c):
        n = chunk // (2 * planes * shard)
        at = pl.ds(c * n, n)
        block = w0[at, :, :, 0:shard, :] if m == 0 else w1[at]
        return block.reshape(chunk, width)

    def told(sem, k):
        pl.semaphore_wait(sem.at[lax.rem(k, slots)], parts - 1)

    one_way = (send1, recv1, ss1, rs1)
    way_back = (send2, recv2, ss2, rs2)

    def hidden_job(k):
        table = dot_nt(hp[...], tokv[lax.rem(k, jobs)]).astype(bf16)
        send1[lax.rem(k, 2)] = table.reshape(parts, 2 * pairs, span)
        own(send1, recv1, rs1, k).start()

        def one(d, carry):
            remote(*one_way, k, d).start()
            return carry

        lax.fori_loop(1, parts, one, 0)

    def sequence_job(k, before_send):
        wait_recvs(*one_way, k)
        radix_step(recv1.at[lax.rem(k, slots)], tw, t_ref, parts, pairs, span)
        slot = lax.rem(k, 2)
        half = span // 2

        def one(u, base, carry):
            def put(p, rows, cols, value):
                send2[slot, p, rows, cols] = value

            spread_step(o_ref, put, me, parts, pairs, u, base)
            for h in range(2):
                d = lax.rem(2 * u + h - me + parts, parts)

                @pl.when(d > 0)
                def _():
                    remote(*way_back, k, d).start()

                @pl.when(d == 0)
                def _():
                    own(send2, recv2, rs2, k).start()
            return carry

        for base in range(2):
            o_ref[...] = dot_nn(t_ref[...], wd[:, base * half:(base + 1) * half])
            if base == 0:
                before_send()
            lax.fori_loop(base * parts // 4, (base + 1) * parts // 4, partial(lambda b, u, c: one(u, b, c), base), 0)

    def mixed_job(k):
        wait_recvs(*way_back, k)
        blocks = recv2[lax.rem(k, slots)].reshape(width, span)
        natural = dot_tn(blocks, cp[...])
        step = span // parts
        for b in range(parts):
            for c in range(width // 128):
                nbuf[c, pl.ds(b, step, stride=parts), :] = natural[b * step:(b + 1) * step, c * 128:(c + 1) * 128]

    gather_start()
    load_of(jobs).wait()
    load_of(0).wait()
    hidden_job(0)
    dw[...] = jnp.zeros_like(dw)
    sums[...] = jnp.zeros_like(sums)
    bsum[...] = jnp.zeros_like(bsum)
    gather_out()
    gather_in()
    for k in (1, 2, 3, jobs + 1, jobs + 2):
        load_of(k).wait()

    def fill(k, carry):
        sequence_job(k, lambda: None)
        tell(free1, k)

        @pl.when(k == 0)
        def _():
            relay_step(0)
            gather_pass()

        @pl.when(k == 1)
        def _():
            wait_sends(*one_way, 0)

        hidden_job(k + 1)
        return carry

    lax.fori_loop(0, 2, fill, 0)
    relay_step(1)
    wait_sends(*one_way, 1)
    told(free1, 0)
    hidden_job(3)
    relay_step(2)
    gather_end()
    gather_sent()

    def out_copy(i):
        return pltpu.make_async_copy(outv, out.at[i], io.at[0])

    def cot_copy(i):
        return pltpu.make_async_copy(cot.at[i], cotv, io.at[1])

    def row_copy(i):
        return pltpu.make_async_copy(acc, grow.at[i], io.at[2])

    def main(i, carry):
        cot_copy(i).start()
        mixed_job(i)
        tell(free2, i)
        ffn_forward(lambda at: tokv[i, at, :], nbuf, sbuf, alow, hid, slope, acc, weight, vec, bias_in, rows_step)

        def before():
            wait_sends(*way_back, i)

            @pl.when(i >= 1)
            def _():
                told(free2, i + 2)

        sequence_job(i + 2, before)

        @pl.when(i < 3)
        def _():
            tell(free1, i + 2)

        cot_copy(i).wait()

        @pl.when(i > 0)
        def _():
            out_copy(i - 1).wait()

        ffn_middle(nbuf, acc, glow, cotv, outv, vec, sums, rows_step)
        out_copy(i).start()

        def put(at, value):
            acc[at, :] = value
            tokv[i, at, :] = value.astype(bf16)

        ffn_backward(nbuf, sbuf, alow, hid, slope, acc, glow, weight, dw, bsum, vec, sums, chunk, rows_step, put)
        row_copy(i).start()
        wait_sends(*one_way, i + 2)
        told(free1, i + jobs)
        hidden_job(i + jobs)
        row_copy(i).wait()
        return carry

    lax.fori_loop(0, jobs, main, 0)

    x, y = lax.rem(quad, 2), quad // 2
    x_peer = (me + 2 - 4 * x, plane)
    y_peer = (me + 4 - 8 * y, plane)
    def rows_at(start, count=shard):
        return pl.ds(pl.multiple_of(start, shard), count)

    def target(v):
        return lax.rem(plane + 1 + v, planes)

    def owned(q, c, v):
        return rows_at(((2 * q + c) * planes + target(v)) * shard)

    keep = pl.ds(0, shard)

    def core_copy(v):
        return send(w1.at[v], w0.at[v, :, :, keep], s_core.at[v], r_core.at[v], partner)

    def first_copy(v, m):
        return send(w1.at[2 + v // 2, lax.rem(v, 2), pl.ds(2 * m, 2)], w1.at[v // 2, lax.rem(v, 2), pl.ds(2 * m, 2)],
                    s_first.at[v, m], r_first.at[v, m], (x_peer, y_peer)[m])

    def next_copy(v, m):
        return send(w0.at[0, v // 2, 2 * lax.rem(v, 2) + m, keep], (alow, glow)[m].at[rows_at(v * shard)],
                    s_next.at[v, m], r_next.at[v, m], (y_peer, x_peer)[m])

    def z_copy(v):
        return send(w0.at[1, v // 2, pl.ds(2 * lax.rem(v, 2), 2), keep], rz.at[v],
                    s_z.at[v], r_z.at[v], (me, target(v)))

    def vec_copy(k):
        to = (partner, x_peer, y_peer)[k] if k < 3 else (me, target(k - 3))
        return send(sv.at[min(k, 3)], rv.at[k], s_vec.at[k], r_vec.at[k], to)

    def core_step(v, carry):
        for q in range(quads):
            for m in range(2):
                w1[v, q // 2, 2 * (q % 2) + m] = dw[m, owned(q, 1 - core, v)].astype(bf16)
        core_copy(v).start()
        return carry

    def first_step(v, carry):
        core_copy(v).wait_recv()
        for q in range(quads):
            for m in range(2):
                at = owned(q, core, v)
                dw[m, at] += w0[v, q // 2, 2 * (q % 2) + m, 0:shard, :].astype(f32)
        for k in range(2):
            for m in range(2):
                q = 2 * k + 1 - x if m == 0 else 2 * (1 - y) + k
                w1[2 + v // 2, lax.rem(v, 2), 2 * m + k] = dw[m, owned(q, core, v)].astype(bf16)
        for m in range(2):
            first_copy(v, m).start()
        return carry

    def next_step(v, carry):
        for m in range(2):
            first_copy(v, m).wait_recv()
        for k in range(2):
            for m in range(2):
                q = 2 * k + x if m == 0 else 2 * y + k
                dw[m, owned(q, core, v)] += w1[v // 2, lax.rem(v, 2), 2 * m + k].astype(f32)
        for m in range(2):
            q = 2 * (1 - y) + x if m == 0 else 2 * y + 1 - x
            w0[0, v // 2, 2 * lax.rem(v, 2) + m, 0:shard, :] = dw[m, owned(q, core, v)].astype(bf16)
            next_copy(v, m).start()
        return carry

    def z_step(v, carry):
        for m in range(2):
            next_copy(v, m).wait_recv()
            dw[m, owned(quad, core, v)] += (alow, glow)[m][rows_at(v * shard)].astype(f32)

        @pl.when(v < planes - 1)
        def _():
            for m in range(2):
                w0[1, v // 2, 2 * lax.rem(v, 2) + m, 0:shard, :] = dw[m, owned(quad, core, v)].astype(bf16)
            z_copy(v).start()

        return carry

    def vec_step(k):
        if k == 0:
            sv[0] = jnp.zeros_like(sv[0])
            for j in range(5):
                sv[0, j:j + 1] = jnp.sum(sums[j], axis=0, keepdims=True)
            piece = math.gcd(width, chunk)
            for f in range(0, bsum.shape[0] * chunk, piece):
                sv[0, 5 + f // width:6 + f // width, f % width:f % width + piece] = jnp.sum(
                    bsum[f // chunk, :, f % chunk:f % chunk + piece], axis=0, keepdims=True)
        else:
            vec_copy(k - 1).wait_recv()
            sv[k] = sv[k - 1] + rv[k - 1]
        for j in ((k,) if k < 3 else range(3, 2 + planes)):
            vec_copy(j).start()

    def gt_copy(i):
        return pltpu.make_async_copy(tokv.at[i], gtok.at[i], io.at[4 + i])

    def final(i):
        back = pltpu.make_async_copy(grow.at[i], acc, io.at[2])
        back.start()
        mixed_job(i + jobs)
        back.wait()
        for c in range(width // 128):
            tokv[i, :, c * 128:(c + 1) * 128] = (nbuf[c] + acc[:, c * 128:(c + 1) * 128]).astype(bf16)
        gt_copy(i).start()

    def drain(i, carry):
        final(i)

        @pl.when(i == 0)
        def _():
            tell(free2, jobs)

        def before():
            wait_sends(*way_back, i + 4)
            told(free2, i + 6)

        sequence_job(i + 6, before)

        @pl.when(i == 0)
        def _():
            lax.fori_loop(0, planes, first_step, 0)

        return carry

    def finish(i, carry):
        final(i + 2)
        wait_sends(*way_back, i + 6)
        wait_sends(*one_way, i + 6)

        @pl.when(i == 0)
        def _():
            lax.fori_loop(0, planes, z_step, 0)

        return carry

    pl.semaphore_signal(ready.at[0], inc=1, device_id=partner, device_id_type=MESH)
    pl.semaphore_wait(ready.at[0], 1)
    lax.fori_loop(0, planes, core_step, 0)
    vec_step(0)

    def core_sent(v, carry):
        core_copy(v).wait_send()
        return carry

    lax.fori_loop(0, planes, core_sent, 0)
    pl.semaphore_signal(ready.at[1], inc=1, device_id=x_peer, device_id_type=MESH)
    pl.semaphore_signal(ready.at[2], inc=1, device_id=y_peer, device_id_type=MESH)
    vec_step(1)
    pl.semaphore_wait(ready.at[1], 1)
    pl.semaphore_wait(ready.at[2], 1)
    lax.fori_loop(0, 2, drain, 0)
    vec_step(2)
    lax.fori_loop(0, planes, next_step, 0)
    vec_step(3)
    lax.fori_loop(0, 2, finish, 0)
    own_rows = owned(quad, core, planes - 1)
    for m in range(2):
        dw_own[m] = dw[m, own_rows]
    for v in range(planes - 1):
        z_copy(v).wait_recv()
        for m in range(2):
            dw_own[m] += rz[v, m].astype(f32)
    total = sv[3]
    for k in range(3, 2 + planes):
        vec_copy(k).wait_recv()
        total = total + rv[k]
    small[...] = total

    def sent(v, carry):
        for m in range(2):
            first_copy(v, m).wait_send()
            next_copy(v, m).wait_send()
        return carry

    lax.fori_loop(0, planes, sent, 0)
    for v in range(planes - 1):
        z_copy(v).wait_send()
    for k in range(2 + planes):
        vec_copy(k).wait_send()
    out_copy(jobs - 1).wait()
    for i in range(jobs):
        gt_copy(i).wait()


def layer_call(tok, cot, win_own, wout_own, vec_own, parts, planes):
    jobs, span, width = tok.shape
    shard = wout_own.shape[0]
    ff = shard * parts * planes
    pairs = width // 2 // parts
    chunk, rows_step = ff // 2, span // 2
    steps = ff // chunk
    length = span * parts
    slots = 3
    geo = (parts, pairs, span, width, jobs, slots, chunk, rows_step, planes)
    tables = (
        jnp.asarray(packed_hidden(width, parts)),
        jnp.asarray(inner_table(span, length)),
        jnp.asarray(column_order(width, parts)),
        jnp.asarray(twiddles(parts, span)),
    )
    hbm, vmem, dma = pl.BlockSpec(memory_space=pl.ANY), pl.BlockSpec(memory_space=pltpu.VMEM), pltpu.SemaphoreType.DMA
    block = (parts, 2 * pairs, span)
    scratch = [
        pltpu.VMEM((jobs, span, width), bf16),
        pltpu.VMEM((span, width), bf16),
        pltpu.VMEM((span, width), bf16),
        pltpu.VMEM((parts // 2, 2, planes, shard + 16, width), bf16),
        pltpu.VMEM((parts // 2, 2, planes, shard, width), bf16),
        pltpu.VMEM((width, width), bf16),
        pltpu.VMEM((2 * span, span), bf16),
        pltpu.VMEM((width, width), bf16),
        pltpu.VMEM((2, ff, width), f32),
        pltpu.VMEM((2,) + block, bf16),
        pltpu.VMEM((slots,) + block, bf16),
        pltpu.VMEM((2,) + block, bf16),
        pltpu.VMEM((slots,) + block, bf16),
        pltpu.VMEM((2 * parts * pairs + 16, 2 * span), bf16),
        pltpu.VMEM((2 * parts * pairs + 16, span // 2), f32),
        pltpu.VMEM((width // 128, span, 128), f32),
        pltpu.VMEM((span, 128), f32),
        pltpu.VMEM((span, width), bf16),
        pltpu.VMEM((steps, span, chunk), bf16),
        pltpu.VMEM((steps, span, chunk), bf16),
        pltpu.VMEM((span, width), f32),
        pltpu.VMEM((span, width), bf16),
        pltpu.VMEM((5, 8, width), f32),
        pltpu.VMEM((steps, 8, chunk), f32),
        pltpu.VMEM((planes - 1, 2, shard, width), bf16),
        pltpu.VMEM((4, 16, width), f32),
        pltpu.VMEM((2 + planes, 16, width), f32),
        pltpu.VMEM((8, width), f32),
        pltpu.VMEM((steps, 1, chunk), f32),
        dma((2, parts)), dma((slots, parts)), dma((2, parts)), dma((slots, parts)),
        pltpu.SemaphoreType.REGULAR((slots,)), pltpu.SemaphoreType.REGULAR((slots,)),
        dma((jobs + 6,)), dma((4 + jobs,)),
        dma((planes,)), dma((planes,)), dma((planes, 2)), dma((planes, 2)), dma((planes, 2)), dma((planes, 2)),
        dma((planes - 1,)), dma((planes - 1,)), dma((2 + planes,)), dma((2 + planes,)),
        pltpu.SemaphoreType.REGULAR((3,)),
        dma((3, max(parts // 2, planes))), dma((3, max(parts // 2, planes))), dma((2, planes)), dma((planes,)),
        dma((2, max(parts // 2, planes))), dma((2, max(parts // 2, planes))),
    ]
    shape = jax.ShapeDtypeStruct
    return pl.pallas_call(
        partial(layer_kernel, geo),
        out_shape=(
            shape(tok.shape, bf16),
            shape(tok.shape, bf16),
            shape(tok.shape, f32),
            shape((2, shard, width), f32),
            shape((16, width), f32),
        ),
        in_specs=[hbm] * 8 + [vmem],
        out_specs=(hbm,) * 3 + (vmem,) * 2,
        scratch_shapes=scratch,
        compiler_params=pltpu.CompilerParams(
            collective_id=1, has_side_effects=True, vmem_limit_bytes=64 * 1024 * 1024 - 256 * 1024),
        name="encoder_layer",
    )(tok, cot, win_own, wout_own, vec_own, *tables)


def local_fast(tokens, w_in, b_in, w_out, b_out, gain_one, shift_one, gain_two, shift_two, cotangent):
    both = ("seq", "batch")
    parts = lax.axis_size("seq")
    width = tokens.shape[2]
    shard = w_in.shape[1]
    planes = lax.axis_size("batch")
    owner = lax.axis_index("seq") * planes + lax.axis_index("batch")
    part = b_out.shape[0]
    vectors = jnp.zeros((5, width), bf16)
    mine = jnp.stack([gain_one, shift_one, gain_two, shift_two, b_out])
    vectors = lax.dynamic_update_slice(vectors, mine, (0, owner * part))
    bias = lax.dynamic_update_slice(jnp.zeros((parts * planes * shard,), bf16), b_in, (owner * shard,))
    bias = bias.reshape(-1, width)
    vectors = jnp.concatenate([vectors, bias, jnp.zeros((11 - bias.shape[0], width), bf16)])
    out, gtok, _, dw, small = layer_call(tokens, cotangent, w_in.T, w_out, vectors, parts, planes)
    grad_b_in = lax.dynamic_slice(small[5:9].reshape(-1), (owner * shard,), (shard,))
    rest = lax.dynamic_slice(small[:5], (0, owner * part), (5, part))
    return (out, gtok, dw[0].T, grad_b_in, dw[1], rest[4], rest[0], rest[1], rest[2], rest[3])


def hidden_table(extent):
    idx_all = jnp.arange(extent, dtype=jnp.int32)
    angles = (idx_all[:, None] * idx_all[None, :] % extent).astype(jnp.float32) * (
        2.0 * math.pi / extent
    )
    factor = 1.0 / math.sqrt(extent)
    return jnp.concatenate([jnp.cos(angles) * factor, jnp.sin(angles) * factor], axis=1).astype(
        jnp.bfloat16
    )


def sequence_table(length):
    block_rows = min(512, length)
    block_count = length // block_rows
    col_ids = jnp.arange(length, dtype=jnp.int32)
    factor = 1.0 / math.sqrt(length)

    def table_rows(block_index):
        row_ids = block_index * block_rows + jnp.arange(block_rows, dtype=jnp.int32)
        angles = (row_ids[:, None] * col_ids[None, :] % length).astype(jnp.float32) * (
            2.0 * math.pi / length
        )
        return (jnp.stack([jnp.cos(angles), -jnp.sin(angles)]) * factor).astype(jnp.bfloat16)

    blocks = lax.map(table_rows, jnp.arange(block_count, dtype=jnp.int32))
    return jnp.moveaxis(blocks, 1, 0).reshape(2, length, length)


def normalize(values, gain, shift):
    center = values - jnp.mean(values, axis=-1, keepdims=True)
    inv_std = lax.rsqrt(jnp.mean(center * center, axis=-1, keepdims=True) + epsilon)
    normed = center * inv_std
    return (normed * gain + shift, normed, inv_std)


def norm_back(grad_out, normed, inv_std, gain):
    scaled = grad_out * gain
    centered = scaled - jnp.mean(scaled, axis=-1, keepdims=True)
    return inv_std * (centered - normed * jnp.mean(scaled * normed, axis=-1, keepdims=True))


def local(tokens, w_in, b_in, w_out, b_out, gain_one, shift_one, gain_two, shift_two, cotangent):
    batch_rows, seq_part, model_width = tokens.shape
    length = seq_part * lax.axis_size("seq")
    w_in_all, b_in_all, w_out_all, b_out_all, g_one_all, s_one_all, g_two_all, s_two_all = (
        lax.all_gather(w_in, ("seq", "batch"), axis=1, tiled=True),
        lax.all_gather(b_in, ("seq", "batch"), axis=0, tiled=True),
        lax.all_gather(w_out, ("seq", "batch"), axis=0, tiled=True),
        lax.all_gather(b_out, ("seq", "batch"), axis=0, tiled=True),
        lax.all_gather(gain_one, ("seq", "batch"), axis=0, tiled=True),
        lax.all_gather(shift_one, ("seq", "batch"), axis=0, tiled=True),
        lax.all_gather(gain_two, ("seq", "batch"), axis=0, tiled=True),
        lax.all_gather(shift_two, ("seq", "batch"), axis=0, tiled=True),
    )
    h_table = hidden_table(model_width)
    s_table = sequence_table(length)
    flat_tokens = tokens.reshape(-1, model_width)
    spectra = jnp.dot(flat_tokens, h_table, preferred_element_type=jnp.float32).astype(jnp.bfloat16)
    spectra = spectra.reshape(batch_rows, seq_part, 2, model_width)
    mixed_cols = jnp.einsum(
        "plm,bmpc->blc",
        s_table,
        lax.all_to_all(spectra, "seq", split_axis=3, concat_axis=1, tiled=True),
        preferred_element_type=jnp.float32,
    ).astype(jnp.bfloat16)
    mixed = lax.all_to_all(mixed_cols, "seq", split_axis=1, concat_axis=2, tiled=True)
    resid_one = flat_tokens.astype(jnp.float32) + mixed.reshape(-1, model_width).astype(jnp.float32)
    act_one, normed_one, inv_one = normalize(
        resid_one, g_one_all.astype(jnp.float32), s_one_all.astype(jnp.float32)
    )
    act_low = act_one.astype(jnp.bfloat16)
    pre_act = jnp.dot(act_low, w_in_all, preferred_element_type=jnp.float32) + b_in_all.astype(
        jnp.float32
    )
    activ, gelu_back = jax.vjp(partial(jax.nn.gelu, approximate=True), pre_act)
    hidden_low = activ.astype(jnp.bfloat16)
    branch = jnp.dot(hidden_low, w_out_all, preferred_element_type=jnp.float32) + b_out_all.astype(
        jnp.float32
    )
    resid_two = act_one + branch
    result, normed_two, inv_two = normalize(
        resid_two, g_two_all.astype(jnp.float32), s_two_all.astype(jnp.float32)
    )
    grad_out = cotangent.reshape(-1, model_width).astype(jnp.float32)
    grad_g_two = jnp.sum(grad_out * normed_two, axis=0)
    grad_s_two = jnp.sum(grad_out, axis=0)
    grad_r_two = norm_back(grad_out, normed_two, inv_two, g_two_all.astype(jnp.float32))
    grad_branch = grad_r_two.astype(jnp.bfloat16)
    grad_b_out = jnp.sum(grad_branch.astype(jnp.float32), axis=0)
    grad_w_out = jnp.einsum(
        "tf,td->fd", hidden_low, grad_branch, preferred_element_type=jnp.float32
    )
    grad_hidden = jnp.einsum(
        "td,fd->tf", grad_branch, w_out_all, preferred_element_type=jnp.float32
    )
    grad_pre = gelu_back(grad_hidden)[0].astype(jnp.bfloat16)
    grad_b_in = jnp.sum(grad_pre.astype(jnp.float32), axis=0)
    grad_w_in = jnp.einsum("td,tf->df", act_low, grad_pre, preferred_element_type=jnp.float32)
    grad_a_one = grad_r_two + jnp.einsum(
        "tf,df->td", grad_pre, w_in_all, preferred_element_type=jnp.float32
    )
    grad_g_one = jnp.sum(grad_a_one * normed_one, axis=0)
    grad_s_one = jnp.sum(grad_a_one, axis=0)
    grad_r_one = norm_back(grad_a_one, normed_one, inv_one, g_one_all.astype(jnp.float32))
    grad_mix = grad_r_one.astype(jnp.bfloat16).reshape(batch_rows, seq_part, model_width)
    spec_grad = jnp.einsum(
        "plm,blc->bmpc",
        s_table,
        lax.all_to_all(grad_mix, "seq", split_axis=2, concat_axis=1, tiled=True),
        preferred_element_type=jnp.float32,
    ).astype(jnp.bfloat16)
    grad_spec = lax.all_to_all(spec_grad, "seq", split_axis=1, concat_axis=3, tiled=True)
    grad_flat = grad_r_one + jnp.einsum(
        "te,de->td",
        grad_spec.reshape(-1, 2 * model_width),
        h_table,
        preferred_element_type=jnp.float32,
    )
    sum_w_in, sum_b_in, sum_w_out, sum_b_out, sum_g_one, sum_s_one, sum_g_two, sum_s_two = (
        lax.psum_scatter(grad_w_in, ("seq", "batch"), scatter_dimension=1, tiled=True),
        lax.psum_scatter(grad_b_in, ("seq", "batch"), scatter_dimension=0, tiled=True),
        lax.psum_scatter(grad_w_out, ("seq", "batch"), scatter_dimension=0, tiled=True),
        lax.psum_scatter(grad_b_out, ("seq", "batch"), scatter_dimension=0, tiled=True),
        lax.psum_scatter(grad_g_one, ("seq", "batch"), scatter_dimension=0, tiled=True),
        lax.psum_scatter(grad_s_one, ("seq", "batch"), scatter_dimension=0, tiled=True),
        lax.psum_scatter(grad_g_two, ("seq", "batch"), scatter_dimension=0, tiled=True),
        lax.psum_scatter(grad_s_two, ("seq", "batch"), scatter_dimension=0, tiled=True),
    )
    output = result.astype(jnp.bfloat16).reshape(batch_rows, seq_part, model_width)
    grad_tokens = grad_flat.astype(jnp.bfloat16).reshape(batch_rows, seq_part, model_width)
    return (
        output,
        grad_tokens,
        sum_w_in,
        sum_b_in,
        sum_w_out,
        sum_b_out,
        sum_g_one,
        sum_s_one,
        sum_g_two,
        sum_s_two,
    )


def solution(mesh):
    every = P(("seq", "batch"))

    def whole(tokens, w_in, *rest):
        parts = mesh.shape["seq"]
        fits = (
            parts == 8
            and tokens.shape[1] == 512 * parts
            and tokens.shape[2] % (32 * parts) == 0
            and w_in.shape[1] % (3 * 128) == 0
            and tokens.shape[0] == 4 * mesh.shape["batch"]
        )
        return jax.shard_map(
            local_fast if fits else local,
            mesh=mesh,
            in_specs=(
                P("batch", "seq", None),
                P(None, ("seq", "batch")),
                every,
                P(("seq", "batch"), None),
                every,
                every,
                every,
                every,
                every,
                P("batch", "seq", None),
            ),
            out_specs=(
                P("batch", "seq", None),
                P("batch", "seq", None),
                P(None, ("seq", "batch")),
                every,
                P(("seq", "batch"), None),
                every,
                every,
                every,
                every,
                every,
            ),
            check_vma=False,
        )(tokens, w_in, *rest)

    return whole
```

```python
from functools import partial
import math

import jax
import jax.numpy as jnp
import ml_dtypes
import numpy as np
from jax import lax
from jax.experimental import pallas as pl
from jax.experimental.pallas import tpu as pltpu
from jax.sharding import PartitionSpec as P

epsilon = 1e-05
f32, bf16 = jnp.float32, jnp.bfloat16
MESH = pl.DeviceIdType.MESH


def dot_nn(a, b):
    return lax.dot_general(a, b, (((1,), (0,)), ((), ())), preferred_element_type=f32)


def dot_nt(a, b):
    return lax.dot_general(a, b, (((1,), (1,)), ((), ())), preferred_element_type=f32)


def dot_tn(a, b):
    return lax.dot_general(a, b, (((0,), (0,)), ((), ())), preferred_element_type=f32)


def plan_columns(width, parts):
    pairs = width // 2 // parts
    r = np.arange(width)
    dev, kind, i = r // (2 * pairs), (r // pairs) % 2, r % pairs
    j = dev * pairs + i
    first = (kind == 1) & (j == 0)
    return j, kind, first


def packed_hidden(width, parts):
    j, kind, first = plan_columns(width, parts)
    k = np.arange(width)
    angle = (j[:, None] * k[None, :] % width) * (2.0 * math.pi / width)
    table = np.where(kind[:, None] == 0, np.cos(angle), np.sin(angle))
    nyquist = np.cos(np.pi * (k % 2))
    table = np.where(first[:, None], nyquist[None, :], table) / math.sqrt(width)
    return table.astype(np.float32).astype(ml_dtypes.bfloat16)


def column_order(width, parts):
    j, kind, first = plan_columns(width, parts)
    col = np.where(kind == 0, j, np.where(first, width // 2, (width - j) % width))
    return (col[:, None] == np.arange(width)[None, :]).astype(ml_dtypes.bfloat16)


def inner_table(span, length):
    a = np.arange(span)
    angle = (a[:, None] * a[None, :] % span) * (2.0 * math.pi / span)
    table = np.concatenate([np.cos(angle), np.sin(angle)], axis=0)
    return (table / math.sqrt(length)).astype(np.float32).astype(ml_dtypes.bfloat16)


def twiddles(parts, span):
    b = np.arange(parts)[:, None]
    angle = b * np.arange(span)[None, :] * (2.0 * math.pi / (parts * span))
    return np.concatenate([np.cos(angle), np.sin(angle)], axis=0).astype(np.float32)


def add(a, b):
    return (a[0] + b[0], a[1] + b[1])


def sub(a, b):
    return (a[0] - b[0], a[1] - b[1])


def minus_i(a):
    return (a[1], -a[0])


def dft4(x0, x1, x2, x3):
    t0, t1, t2, t3 = add(x0, x2), sub(x0, x2), add(x1, x3), sub(x1, x3)
    r = minus_i(t3)
    return add(t0, t2), add(t1, r), sub(t0, t2), sub(t1, r)


def dft8(x):
    e = dft4(x[0], x[2], x[4], x[6])
    o = dft4(x[1], x[3], x[5], x[7])
    h = math.sqrt(0.5)
    o1 = (h * (o[1][0] + o[1][1]), h * (o[1][1] - o[1][0]))
    o2 = minus_i(o[2])
    o3 = (h * (o[3][1] - o[3][0]), -h * (o[3][0] + o[3][1]))
    o = (o[0], o1, o2, o3)
    return [add(e[k], o[k]) for k in range(4)] + [sub(e[k], o[k]) for k in range(4)]


def radix_step(rec, tw, t_ref, parts, pairs, span):
    groups = pairs // 16
    count = 2 * parts * pairs

    def tile(u, carry):
        lanes = pl.ds(pl.multiple_of(u * 128, 128), 128)
        lanes_im = pl.ds(pl.multiple_of(span + u * 128, 128), 128)
        extra = [jnp.zeros((16, 128), f32), jnp.zeros((16, 128), f32)]
        row = lax.broadcasted_iota(jnp.int32, (16, 128), 0)
        for g in range(groups):
            x = []
            for s in range(parts):
                re = rec[s, g * 16:g * 16 + 16, lanes].astype(f32)
                im = rec[s, pairs + g * 16:pairs + g * 16 + 16, lanes].astype(f32)
                x.append((re, -im))
            y = dft8(x)
            for b in range(parts):
                c, s = tw[b:b + 1, lanes], tw[parts + b:parts + b + 1, lanes]
                conj = y[(parts - b) % parts]
                for kind, (zr, zi) in enumerate((y[b], (conj[0], -conj[1]))):
                    tr = c * zr + s * zi
                    ti = c * zi - s * zr
                    base = (kind * parts + b) * pairs + g * 16
                    t_ref[base:base + 16, lanes] = tr.astype(bf16)
                    t_ref[base:base + 16, lanes_im] = ti.astype(bf16)
                    if g == 0:
                        hit = row == kind * parts + b
                        extra[0] = jnp.where(hit, jnp.broadcast_to(-ti[0:1], (16, 128)), extra[0])
                        extra[1] = jnp.where(hit, jnp.broadcast_to(tr[0:1], (16, 128)), extra[1])
        t_ref[count:count + 16, lanes] = extra[0].astype(bf16)
        t_ref[count:count + 16, lanes_im] = extra[1].astype(bf16)
        return carry

    lax.fori_loop(0, span // 128, tile, 0)


def spread_step(o_ref, put, me, parts, pairs, u, half):
    count = 2 * parts * pairs
    lanes = pl.ds(pl.multiple_of((u - half * parts // 4) * 128, 128), 128)
    low = lax.broadcasted_iota(jnp.int32, (16, 128), 1) < 64
    row = lax.broadcasted_iota(jnp.int32, (16, 128), 0)
    special = (row == 0) & (jnp.zeros((16, 128), jnp.int32) + me == 0)
    extra = o_ref[count:count + 16, lanes]
    for p in range(parts // 2):
        for g in range(pairs // 16):
            v = [[None, None], [None, None]]
            for kind in range(2):
                for h in range(2):
                    base = (kind * parts + 2 * p + h) * pairs + g * 16
                    v[kind][h] = o_ref[base:base + 16, lanes]
            if g == 0:
                for h in range(2):
                    b = 2 * p + h
                    even = 0.5 * (v[0][h] + v[1][h])
                    odd = jnp.broadcast_to(0.5 * (extra[b:b + 1] - extra[parts + b:parts + b + 1]), (16, 128))
                    v[0][h] = jnp.where(special, even, v[0][h])
                    v[1][h] = jnp.where(special, odd, v[1][h])
            for kind in range(2):
                v0, v1 = v[kind]
                rows = pl.ds(kind * pairs + g * 16, 16)
                cols = pl.ds(p * 128, 128)
                put(2 * u, rows, cols, jnp.where(low, v0, pltpu.roll(v1, 64, 1)).astype(bf16))
                put(2 * u + 1, rows, cols, jnp.where(low, pltpu.roll(v0, 64, 1), v1).astype(bf16))


def fold(v):
    total = v[0:8]
    for k in range(8, v.shape[0], 8):
        total = total + v[k:k + 8]
    return total


def rows_of(ref, at):
    return jnp.concatenate([ref[c, at, :] for c in range(ref.shape[0])], axis=1)


def set_rows(ref, at, value):
    for c in range(ref.shape[0]):
        ref[c, at, :] = value[:, c * 128:(c + 1) * 128]


def mean_of(v):
    return jnp.mean(v, axis=-1, keepdims=True)


def gelu_pair(x):
    k = math.sqrt(2.0 / math.pi)
    c = 0.044715
    x2 = x * x
    half = 0.5 + 0.5 * jnp.tanh(x * (k + (k * c) * x2))
    value = x * half
    slope = half + value * (1.0 - half) * (2.0 * k + (6.0 * k * c) * x2)
    return value, slope


def ffn_hidden(x_get, nbuf, sbuf, alow, hid, slope, weight, vec, bias_in, rows_step):
    rows = nbuf.shape[1]

    def first(r, carry):
        at = pl.ds(pl.multiple_of(r * rows_step, rows_step), rows_step)
        v = x_get(at).astype(f32) + rows_of(nbuf, at)
        center = v - mean_of(v)
        inv = lax.rsqrt(mean_of(center * center) + epsilon)
        n = center * inv
        set_rows(nbuf, at, n)
        sbuf[at, :] = jnp.broadcast_to(inv, (rows_step, 128))
        alow[at, :] = (n * vec[0:1] + vec[1:2]).astype(bf16)
        return carry

    lax.fori_loop(0, rows // rows_step, first, 0)

    def step(c, carry):
        pre = dot_nt(alow[...], weight(0, c)) + bias_in[c]
        value, back = gelu_pair(pre)
        hid[c] = value.astype(bf16)
        slope[c] = back.astype(bf16)
        return carry

    lax.fori_loop(0, hid.shape[0], step, 0)


def ffn_branch(hid, acc, weight):
    steps = hid.shape[0]
    every = jnp.concatenate([hid[c] for c in range(steps)], axis=1)
    acc[...] = dot_nn(every, weight(1, 0, steps))


def ffn_middle(nbuf, acc, glow, cot, outv, vec, sums, rows_step):
    rows = nbuf.shape[1]

    def second(r, carry):
        at = pl.ds(pl.multiple_of(r * rows_step, rows_step), rows_step)
        v = rows_of(nbuf, at) * vec[0:1] + vec[1:2] + (acc[at, :] + vec[4:5])
        center = v - mean_of(v)
        inv = lax.rsqrt(mean_of(center * center) + epsilon)
        n = center * inv
        outv[at, :] = (n * vec[2:3] + vec[3:4]).astype(bf16)
        g = cot[at, :].astype(f32)
        q = g * vec[2:3]
        gr = inv * (q - mean_of(q) - n * mean_of(q * n))
        acc[at, :] = gr
        low = gr.astype(bf16)
        glow[at, :] = low
        sums[2] += fold(g * n)
        sums[3] += fold(g)
        sums[4] += fold(low.astype(f32))
        return carry

    lax.fori_loop(0, rows // rows_step, second, 0)


def ffn_backward(nbuf, sbuf, alow, hid, slope, acc, glow, weight, dw, bsum, vec, sums, chunk, rows_step, put, after):
    rows = nbuf.shape[1]

    def step(c, carry):
        gh = dot_nt(glow[...], weight(1, c))
        gpre = (gh * slope[c].astype(f32)).astype(bf16)
        slope[c] = gpre
        bsum[c] += fold(gpre.astype(f32))
        acc[...] += dot_nn(gpre, weight(0, c))
        return carry

    lax.fori_loop(0, hid.shape[0], step, 0)

    def last(r, carry):
        at = pl.ds(pl.multiple_of(r * rows_step, rows_step), rows_step)
        ga = acc[at, :]
        n = rows_of(nbuf, at)
        sums[0] += fold(ga * n)
        sums[1] += fold(ga)
        q = ga * vec[0:1]
        put(at, sbuf[at, 0:1] * (q - mean_of(q) - n * mean_of(q * n)))
        return carry

    lax.fori_loop(0, rows // rows_step, last, 0)
    after()

    def grads(c, carry):
        at = pl.ds(pl.multiple_of(c * chunk, chunk), chunk)
        dw[1, at, :] += dot_tn(hid[c], glow[...])
        dw[0, at, :] += dot_tn(slope[c], alow[...])
        return carry

    lax.fori_loop(0, hid.shape[0], grads, 0)


def layer_kernel(geo, tok, cot, win_own, wout_own, vec_own, hp_all, wd_all, cp_all, tw,
                 out, gtok, grow, dw_own, small,
                 tokv, cotv, outv, w0, w1, hp, wd, cp, dw, send1, recv1, send2, recv2, t_ref, o_ref,
                 nbuf, sbuf, alow, hid, slope, acc, glow, sums, bsum, rz, rze, rzl, sv, rv, vec, bias_in,
                 ss1, rs1, ss2, rs2, free1, free2, load, io,
                 s_core, r_core, s_first, r_first, s_next, r_next, s_z, r_z, s_vec, r_vec, ready,
                 s_spread, r_spread, s_relay, r_relay, s_pair, r_pair, s_early, r_early, s_late, r_late):
    parts, pairs, span, width, jobs, slots, chunk, rows_step, planes = geo
    shard = dw.shape[1] // (parts * planes)
    me = lax.axis_index("seq")
    plane = lax.axis_index("batch")

    def peer(d):
        return lax.rem(me + d, parts)

    def load_of(k):
        if k < jobs:
            return pltpu.make_async_copy(tok.at[k], tokv.at[k], load.at[k])
        a, b = ((hp_all, hp), (wd_all, wd), (cp_all, cp))[k - jobs]
        return pltpu.make_async_copy(a, b, load.at[k])

    for k in (jobs, 0, 1, jobs + 1, 2, 3, jobs + 2):
        load_of(k).start()

    core, quad = lax.rem(me, 2), me // 2
    quads = parts // 2
    x, y = lax.rem(quad, 2), quad // 2
    partner = (me + 1 - 2 * core, plane)
    x_peer = (me + 2 - 4 * x, plane)
    y_peer = (me + 4 - 8 * y, plane)
    quad_x, quad_y = quad + 1 - 2 * x, quad + 2 - 4 * y
    last = planes - 1

    def send(src, dst, s, r, to):
        return pltpu.make_async_remote_copy(
            src_ref=src, dst_ref=dst, send_sem=s, recv_sem=r, device_id=to, device_id_type=MESH)

    own_loads = (
        pltpu.make_async_copy(win_own, w0.at[quad, core, plane, pl.ds(0, shard)], load.at[jobs + 3]),
        pltpu.make_async_copy(vec_own, w0.at[quad, core, plane, pl.ds(shard, 16)], load.at[jobs + 4]),
        pltpu.make_async_copy(wout_own, w1.at[quad, core, plane], load.at[jobs + 5]),
    )
    for copy in own_loads:
        copy.start()

    barrier = pltpu.get_barrier_semaphore()

    def greet(d, carry):
        pl.semaphore_signal(barrier, inc=1, device_id=(peer(d), plane), device_id_type=MESH)
        return carry

    def greet_z(d, carry):
        pl.semaphore_signal(barrier, inc=1, device_id=(me, lax.rem(plane + d, planes)), device_id_type=MESH)
        return carry

    lax.fori_loop(1, parts, greet, 0)
    lax.fori_loop(1, planes, greet_z, 0)
    pl.semaphore_wait(barrier, parts - 1 + planes - 1)

    def remote(send, recv, ss, rs, k, d):
        p = peer(d)
        return pltpu.make_async_remote_copy(
            src_ref=send.at[lax.rem(k, 2), p], dst_ref=recv.at[lax.rem(k, slots), me],
            send_sem=ss.at[lax.rem(k, 2), d], recv_sem=rs.at[lax.rem(k, slots), d],
            device_id=(p, plane), device_id_type=MESH)

    def wait_sends(send, recv, ss, rs, k):
        def one(d, carry):
            remote(send, recv, ss, rs, k, d).wait_send()
            return carry

        lax.fori_loop(1, parts, one, 0)

    def wait_recvs(send, recv, ss, rs, k):
        def one(d, carry):
            source = lax.rem(me + parts - d, parts)
            slot = lax.rem(k, slots)
            pltpu.make_async_remote_copy(
                src_ref=send.at[0, 0], dst_ref=recv.at[slot, source],
                send_sem=ss.at[0, d], recv_sem=rs.at[slot, d],
                device_id=(source, plane), device_id_type=MESH).wait_recv()
            return carry

        lax.fori_loop(1, parts, one, 0)

    def tell(sem, k):
        def one(d, carry):
            pl.semaphore_signal(sem.at[lax.rem(k, slots)], inc=1, device_id=(peer(d), plane), device_id_type=MESH)
            return carry

        lax.fori_loop(1, parts, one, 0)

    def in_plane(d):
        return 2 * lax.rem(quad + d, quads) + core

    def along(d):
        return lax.rem(plane + d, planes)

    def spread_z(d):
        block = w0.at[quad, core, plane]
        return send(block, block, s_spread.at[0, d], r_spread.at[0, d], (me, along(d)))

    def spread_out(d):
        block = w1.at[quad, core, plane]
        return send(block, block, s_spread.at[1, d], r_spread.at[1, d], (in_plane(d), plane))

    def spread_in(n):
        block = w0.at[quad, core]
        return send(block, block, s_spread.at[2, n], r_spread.at[2, n], (x_peer, y_peer)[n])

    def pass_in(n):
        block = w0.at[quad_x if n == 0 else quad_y, core, pl.ds(n * planes // 2, planes // 2)]
        return send(block, block, s_spread.at[2, 2 + n], r_spread.at[2, 2 + n], (y_peer, x_peer)[n])

    def relay(origin, up):
        block = w1.at[:, core, origin]
        return send(block, block, s_relay.at[up, origin], r_relay.at[origin], (me, plane + 2 * up - 1))

    def pair_in(q):
        block = w0.at[q, core]
        return send(block, block, s_pair.at[0, q], r_pair.at[0, q], partner)

    def pair_out(origin):
        block = w1.at[:, core, origin]
        return send(block, block, s_pair.at[1, origin], r_pair.at[1, origin], partner)

    def relay_step(j):
        below, above = plane - 1 - j, plane + 1 + j

        @pl.when(below >= 0)
        def _():
            relay(below, 1).wait_recv()

            @pl.when(plane < last)
            def _():
                relay(below, 1).start()

            pair_out(below).start()

        @pl.when(above <= last)
        def _():
            relay(above, 0).wait_recv()

            @pl.when(plane > 0)
            def _():
                relay(above, 0).start()

            pair_out(above).start()

    def gather_start():
        for copy in own_loads:
            copy.wait()
        for d in range(1, planes):
            spread_z(d).start()
        for d in range(1, quads):
            spread_out(d).start()

    def gather_out():
        for d in range(1, quads):
            spread_out(d).wait_recv()

        @pl.when(plane < last)
        def _():
            relay(plane, 1).start()

        @pl.when(plane > 0)
        def _():
            relay(plane, 0).start()

        pair_out(plane).start()

    def gather_in():
        for d in range(1, planes):
            spread_z(d).wait_recv()
        for n in range(2):
            spread_in(n).start()
        pair_in(quad).start()

    def gather_pass():
        for n in range(2):
            spread_in(n).wait_recv()
        for n in range(2):
            pass_in(n).start()
        pair_in(quad_x).start()
        pair_in(quad_y).start()

    def gather_diagonal():
        for n in range(2):
            pass_in(n).wait_recv()
        pair_in(quads - 1 - quad).start()

    def gather_end_out():
        for origin in range(planes):
            pair_out(origin).wait_recv()

    def gather_end_in():
        for q in range(quads):
            pair_in(q).wait_recv()

        def one(o, carry):
            rest = lax.rem(o, 2 * planes)
            block = w0[o // (2 * planes), rest // planes, lax.rem(rest, planes), shard:shard + 16, :]
            return carry + block.astype(f32)

        total = lax.fori_loop(0, parts * planes, one, jnp.zeros((16, width), f32))
        vec[...] = total[0:8]
        for f in range(0, bsum.shape[0] * chunk, width):
            bias_in[f // chunk, 0:1, f % chunk:f % chunk + width] = total[5 + f // width:6 + f // width]

    def gather_sent():
        for d in range(1, planes):
            spread_z(d).wait_send()
        for d in range(1, quads):
            spread_out(d).wait_send()
        for n in range(2):
            spread_in(n).wait_send()
            pass_in(n).wait_send()
        for q in range(quads):
            pair_in(q).wait_send()
        for origin in range(planes):
            pair_out(origin).wait_send()

            @pl.when((plane < last) & (origin <= plane))
            def _():
                relay(origin, 1).wait_send()

            @pl.when((plane > 0) & (origin >= plane))
            def _():
                relay(origin, 0).wait_send()

    def weight(m, c, count=1):
        n = chunk // (2 * planes * shard)
        at = pl.ds(c * n, count * n)
        block = w0[at, :, :, 0:shard, :] if m == 0 else w1[at]
        return block.reshape(count * chunk, width)

    def told(sem, k):
        pl.semaphore_wait(sem.at[lax.rem(k, slots)], parts - 1)

    one_way = (send1, recv1, ss1, rs1)
    way_back = (send2, recv2, ss2, rs2)

    def hidden_job(k):
        @pl.when(k >= 2)
        def _():
            wait_sends(*one_way, k - 2)

        @pl.when(k >= slots)
        def _():
            told(free1, k)

        table = dot_nt(hp[...], tokv[lax.rem(k, jobs)]).astype(bf16)
        send1[lax.rem(k, 2)] = table.reshape(parts, 2 * pairs, span)
        recv1[lax.rem(k, slots), me] = send1[lax.rem(k, 2), me]

        def one(d, carry):
            remote(*one_way, k, d).start()
            return carry

        lax.fori_loop(1, parts, one, 0)

    def sequence_job(k, carry):
        wait_recvs(*one_way, k)
        radix_step(recv1.at[lax.rem(k, slots)], tw, t_ref, parts, pairs, span)

        @pl.when(k < 2 * jobs - slots)
        def _():
            tell(free1, k)

        slot = lax.rem(k, 2)
        half = span // 2

        def one(u, base, carry):
            def put(p, rows, cols, value):
                send2[slot, p, rows, cols] = value

            spread_step(o_ref, put, me, parts, pairs, u, base)
            for h in range(2):
                d = lax.rem(2 * u + h - me + parts, parts)

                @pl.when(d > 0)
                def _():
                    remote(*way_back, k, d).start()

                @pl.when(d == 0)
                def _():
                    recv2[lax.rem(k, slots), me] = send2[slot, me]
            return carry

        for base in range(2):
            o_ref[...] = dot_nn(t_ref[...], wd[:, base * half:(base + 1) * half])
            if base == 0:

                @pl.when(k >= 2)
                def _():
                    wait_sends(*way_back, k - 2)

                @pl.when(k >= slots)
                def _():
                    told(free2, k)

            lax.fori_loop(base * parts // 4, (base + 1) * parts // 4, partial(lambda b, u, c: one(u, b, c), base), 0)
        return carry

    def mixed_job(k):
        wait_recvs(*way_back, k)
        blocks = recv2[lax.rem(k, slots)].reshape(width, span)
        natural = dot_tn(blocks, cp[...])
        step = span // parts
        for b in range(parts):
            for c in range(width // 128):
                nbuf[c, pl.ds(b, step, stride=parts), :] = natural[b * step:(b + 1) * step, c * 128:(c + 1) * 128]

    gather_start()
    load_of(jobs).wait()
    load_of(0).wait()
    hidden_job(0)
    dw[...] = jnp.zeros_like(dw)
    sums[...] = jnp.zeros_like(sums)
    bsum[...] = jnp.zeros_like(bsum)
    gather_out()
    gather_in()
    for k in (1, 2, 3, jobs + 1, jobs + 2):
        load_of(k).wait()

    sequence_job(0, 0)
    relay_step(0)
    gather_pass()
    hidden_job(1)
    relay_step(1)
    hidden_job(2)
    gather_diagonal()
    hidden_job(3)
    gather_end_in()

    def out_copy(i):
        return pltpu.make_async_copy(outv, out.at[i], io.at[0])

    def cot_copy(i):
        return pltpu.make_async_copy(cot.at[i], cotv, io.at[1])

    def row_copy(i):
        return pltpu.make_async_copy(acc, grow.at[i], io.at[2])

    def after(i):
        row_copy(i).start()
        hidden_job(i + jobs)

    def main(i, carry):
        cot_copy(i).start()
        mixed_job(i)
        tell(free2, i)
        ffn_hidden(lambda at: tokv[i, at, :], nbuf, sbuf, alow, hid, slope, weight, vec, bias_in, rows_step)
        lax.fori_loop(i + 1 + i // 3, i + 2 + i // 2 + i // 3, sequence_job, 0)

        @pl.when(i == 0)
        def _():
            relay_step(2)
            gather_end_out()

        ffn_branch(hid, acc, weight)
        cot_copy(i).wait()

        @pl.when(i > 0)
        def _():
            out_copy(i - 1).wait()

        ffn_middle(nbuf, acc, glow, cotv, outv, vec, sums, rows_step)
        out_copy(i).start()

        def put(at, value):
            acc[at, :] = value
            tokv[i, at, :] = value.astype(bf16)

        ffn_backward(nbuf, sbuf, alow, hid, slope, acc, glow, weight, dw, bsum, vec, sums, chunk, rows_step, put,
                     lambda: after(i))
        row_copy(i).wait()
        return carry

    lax.fori_loop(0, jobs, main, 0)

    most = shard - 16

    def rows_at(start, count=shard):
        return pl.ds(pl.multiple_of(start, shard), count)

    def target(v):
        return lax.rem(plane + 1 + v, planes)

    def owned(q, c, v):
        return rows_at(((2 * q + c) * planes + target(v)) * shard)

    keep, head, tail = pl.ds(0, shard), pl.ds(0, most), pl.ds(shard, 16)

    def core_copy(v):
        return send(w1.at[v], w0.at[v, :, :, keep], s_core.at[v], r_core.at[v], partner)

    def first_copy(v, m):
        at = pl.ds(2 * m, 2)
        return send(w1.at[2 + v // 2, lax.rem(v, 2), at, head], w1.at[v // 2, lax.rem(v, 2), at, head],
                    s_first.at[v, m], r_first.at[v, m], (x_peer, y_peer)[m])

    def next_copy(v, m):
        return send(w0.at[0, v // 2, 2 * lax.rem(v, 2) + m, head],
                    (alow, glow)[m].at[pl.ds(pl.multiple_of(v * most, most), most)],
                    s_next.at[v, m], r_next.at[v, m], (y_peer, x_peer)[m])

    def z_copy(v):
        return send(w0.at[1, v // 2, pl.ds(2 * lax.rem(v, 2), 2), head], rz.at[v],
                    s_z.at[v], r_z.at[v], (me, target(v)))

    def early_copy(v):
        return send(w0.at[v, :, :, tail], rze.at[v], s_early.at[v], r_early.at[v], (me, target(v)))

    def late_copy(d):
        q = lax.rem(quad + d, quads)
        return send(w0.at[quads - 1, q // 2, pl.ds(2 * lax.rem(q, 2), 2), tail], rzl.at[d - 1],
                    s_late.at[d - 1], r_late.at[d - 1], (in_plane(d), plane))

    def vec_copy(k):
        to = (partner, x_peer, y_peer)[k] if k < 3 else (me, target(k - 3))
        return send(sv.at[min(k, 3)], rv.at[k], s_vec.at[k], r_vec.at[k], to)

    def core_step(v, carry):
        for q in range(quads):
            for m in range(2):
                w1[v, q // 2, 2 * (q % 2) + m] = dw[m, owned(q, 1 - core, v)].astype(bf16)
        core_copy(v).start()
        return carry

    def owned_most(q, v):
        return rows_at(((2 * q + core) * planes + target(v)) * shard, most)

    def owned_rest(q, v):
        return pl.ds(pl.multiple_of(((2 * q + core) * planes + target(v)) * shard + most, 16), 16)

    def first_step(v, carry):
        core_copy(v).wait_recv()
        for q in range(quads):
            for m in range(2):
                at = owned(q, core, v)
                dw[m, at] += w0[v, q // 2, 2 * (q % 2) + m, 0:shard, :].astype(f32)

        @pl.when(v < last)
        def _():
            for q in range(quads):
                for m in range(2):
                    w0[v, q // 2, 2 * (q % 2) + m, shard:shard + 16, :] = dw[m, owned_rest(q, v)].astype(bf16)
            early_copy(v).start()

        for k in range(2):
            for m in range(2):
                q = 2 * k + 1 - x if m == 0 else 2 * (1 - y) + k
                w1[2 + v // 2, lax.rem(v, 2), 2 * m + k, 0:most, :] = dw[m, owned_most(q, v)].astype(bf16)
        for m in range(2):
            first_copy(v, m).start()
        return carry

    def next_step(v, carry):
        for m in range(2):
            first_copy(v, m).wait_recv()
        for k in range(2):
            for m in range(2):
                q = 2 * k + x if m == 0 else 2 * y + k
                dw[m, owned_most(q, v)] += w1[v // 2, lax.rem(v, 2), 2 * m + k, 0:most, :].astype(f32)
        for m in range(2):
            q = 2 * (1 - y) + x if m == 0 else 2 * y + 1 - x
            w0[0, v // 2, 2 * lax.rem(v, 2) + m, 0:most, :] = dw[m, owned_most(q, v)].astype(bf16)
            next_copy(v, m).start()
        return carry

    def z_step(v, carry):
        for m in range(2):
            next_copy(v, m).wait_recv()
            dw[m, owned_most(quad, v)] += (alow, glow)[m][pl.ds(pl.multiple_of(v * most, most), most)].astype(f32)

        @pl.when(v < last)
        def _():
            for m in range(2):
                w0[1, v // 2, 2 * lax.rem(v, 2) + m, 0:most, :] = dw[m, owned_most(quad, v)].astype(bf16)
            z_copy(v).start()

        return carry

    def late_step():
        for v in range(last):
            early_copy(v).wait_recv()
        for q in range(quads):
            for m in range(2):
                at = owned_rest(q, last)
                total = dw[m, at]
                for v in range(last):
                    total = total + rze[v, q // 2, 2 * (q % 2) + m].astype(f32)
                dw[m, at] = total
                w0[quads - 1, q // 2, 2 * (q % 2) + m, shard:shard + 16, :] = total.astype(bf16)
        for d in range(1, quads):
            late_copy(d).start()

    def vec_step(k):
        if k == 0:
            sv[0] = jnp.zeros_like(sv[0])
            for j in range(5):
                sv[0, j:j + 1] = jnp.sum(sums[j], axis=0, keepdims=True)
            piece = math.gcd(width, chunk)
            for f in range(0, bsum.shape[0] * chunk, piece):
                sv[0, 5 + f // width:6 + f // width, f % width:f % width + piece] = jnp.sum(
                    bsum[f // chunk, :, f % chunk:f % chunk + piece], axis=0, keepdims=True)
        else:
            vec_copy(k - 1).wait_recv()
            sv[k] = sv[k - 1] + rv[k - 1]
        for j in ((k,) if k < 3 else range(3, 2 + planes)):
            vec_copy(j).start()

    def gt_copy(i):
        return pltpu.make_async_copy(tokv.at[i], gtok.at[i], io.at[4 + i])

    def final(i, carry):
        back = pltpu.make_async_copy(grow.at[i], acc, io.at[2])
        back.start()
        mixed_job(i + jobs)
        back.wait()
        for c in range(width // 128):
            tokv[i, :, c * 128:(c + 1) * 128] = (nbuf[c] + acc[:, c * 128:(c + 1) * 128]).astype(bf16)
        gt_copy(i).start()
        return carry

    gather_sent()
    pl.semaphore_signal(ready.at[0], inc=1, device_id=partner, device_id_type=MESH)
    pl.semaphore_wait(ready.at[0], 1)
    lax.fori_loop(0, planes, core_step, 0)
    vec_step(0)

    def core_sent(v, carry):
        core_copy(v).wait_send()
        return carry

    lax.fori_loop(0, planes, core_sent, 0)
    pl.semaphore_signal(ready.at[1], inc=1, device_id=x_peer, device_id_type=MESH)
    pl.semaphore_signal(ready.at[2], inc=1, device_id=y_peer, device_id_type=MESH)
    vec_step(1)
    pl.semaphore_wait(ready.at[1], 1)
    pl.semaphore_wait(ready.at[2], 1)
    lax.fori_loop(0, planes, first_step, 0)
    final(0, 0)
    tell(free2, jobs)
    vec_step(2)
    lax.fori_loop(0, planes // 2, next_step, 0)
    sequence_job(2 * jobs - 1, 0)
    final(1, 0)
    lax.fori_loop(planes // 2, planes, next_step, 0)
    vec_step(3)
    final(2, 0)
    lax.fori_loop(0, planes, z_step, 0)
    late_step()
    final(3, 0)
    own_most, own_rest = owned_most(quad, last), owned_rest(quad, last)
    for v in range(last):
        z_copy(v).wait_recv()
    for d in range(1, quads):
        late_copy(d).wait_recv()
    for m in range(2):
        total = dw[m, own_most]
        for v in range(last):
            total = total + rz[v, m].astype(f32)
        dw_own[m, 0:most] = total
        total = dw[m, own_rest]
        for d in range(1, quads):
            total = total + rzl[d - 1, m].astype(f32)
        dw_own[m, most:shard] = total
    total = sv[3]
    for k in range(3, 2 + planes):
        vec_copy(k).wait_recv()
        total = total + rv[k]
    small[...] = total

    def sent(v, carry):
        for m in range(2):
            first_copy(v, m).wait_send()
            next_copy(v, m).wait_send()
        return carry

    lax.fori_loop(0, planes, sent, 0)
    for k in range(2 * jobs - 2, 2 * jobs):
        wait_sends(*way_back, k)
        wait_sends(*one_way, k)
    for v in range(last):
        z_copy(v).wait_send()
        early_copy(v).wait_send()
    for d in range(1, quads):
        late_copy(d).wait_send()
    for k in range(2 + planes):
        vec_copy(k).wait_send()
    out_copy(jobs - 1).wait()
    for i in range(jobs):
        gt_copy(i).wait()


def layer_call(tok, cot, win_own, wout_own, vec_own, parts, planes):
    jobs, span, width = tok.shape
    shard = wout_own.shape[0]
    ff = shard * parts * planes
    pairs = width // 2 // parts
    chunk, rows_step = ff // 2, span // 2
    steps = ff // chunk
    length = span * parts
    slots = 3
    geo = (parts, pairs, span, width, jobs, slots, chunk, rows_step, planes)
    tables = (
        jnp.asarray(packed_hidden(width, parts)),
        jnp.asarray(inner_table(span, length)),
        jnp.asarray(column_order(width, parts)),
        jnp.asarray(twiddles(parts, span)),
    )
    hbm, vmem, dma = pl.BlockSpec(memory_space=pl.ANY), pl.BlockSpec(memory_space=pltpu.VMEM), pltpu.SemaphoreType.DMA
    block = (parts, 2 * pairs, span)
    scratch = [
        pltpu.VMEM((jobs, span, width), bf16),
        pltpu.VMEM((span, width), bf16),
        pltpu.VMEM((span, width), bf16),
        pltpu.VMEM((parts // 2, 2, planes, shard + 16, width), bf16),
        pltpu.VMEM((parts // 2, 2, planes, shard, width), bf16),
        pltpu.VMEM((width, width), bf16),
        pltpu.VMEM((2 * span, span), bf16),
        pltpu.VMEM((width, width), bf16),
        pltpu.VMEM((2, ff, width), f32),
        pltpu.VMEM((2,) + block, bf16),
        pltpu.VMEM((slots,) + block, bf16),
        pltpu.VMEM((2,) + block, bf16),
        pltpu.VMEM((slots,) + block, bf16),
        pltpu.VMEM((2 * parts * pairs + 16, 2 * span), bf16),
        pltpu.VMEM((2 * parts * pairs + 16, span // 2), f32),
        pltpu.VMEM((width // 128, span, 128), f32),
        pltpu.VMEM((span, 128), f32),
        pltpu.VMEM((span, width), bf16),
        pltpu.VMEM((steps, span, chunk), bf16),
        pltpu.VMEM((steps, span, chunk), bf16),
        pltpu.VMEM((span, width), f32),
        pltpu.VMEM((span, width), bf16),
        pltpu.VMEM((5, 8, width), f32),
        pltpu.VMEM((steps, 8, chunk), f32),
        pltpu.VMEM((planes - 1, 2, shard - 16, width), bf16),
        pltpu.VMEM((planes - 1, 2, parts // 2, 16, width), bf16),
        pltpu.VMEM((parts // 2 - 1, 2, 16, width), bf16),
        pltpu.VMEM((4, 16, width), f32),
        pltpu.VMEM((2 + planes, 16, width), f32),
        pltpu.VMEM((8, width), f32),
        pltpu.VMEM((steps, 1, chunk), f32),
        dma((2, parts)), dma((slots, parts)), dma((2, parts)), dma((slots, parts)),
        pltpu.SemaphoreType.REGULAR((slots,)), pltpu.SemaphoreType.REGULAR((slots,)),
        dma((jobs + 6,)), dma((4 + jobs,)),
        dma((planes,)), dma((planes,)), dma((planes, 2)), dma((planes, 2)), dma((planes, 2)), dma((planes, 2)),
        dma((planes - 1,)), dma((planes - 1,)), dma((2 + planes,)), dma((2 + planes,)),
        pltpu.SemaphoreType.REGULAR((3,)),
        dma((3, max(parts // 2, planes))), dma((3, max(parts // 2, planes))), dma((2, planes)), dma((planes,)),
        dma((2, max(parts // 2, planes))), dma((2, max(parts // 2, planes))),
        dma((planes - 1,)), dma((planes - 1,)), dma((parts // 2 - 1,)), dma((parts // 2 - 1,)),
    ]
    shape = jax.ShapeDtypeStruct
    return pl.pallas_call(
        partial(layer_kernel, geo),
        out_shape=(
            shape(tok.shape, bf16),
            shape(tok.shape, bf16),
            shape(tok.shape, f32),
            shape((2, shard, width), f32),
            shape((16, width), f32),
        ),
        in_specs=[hbm] * 8 + [vmem],
        out_specs=(hbm,) * 3 + (vmem,) * 2,
        scratch_shapes=scratch,
        compiler_params=pltpu.CompilerParams(
            collective_id=1, has_side_effects=True, vmem_limit_bytes=64 * 1024 * 1024 - 256 * 1024),
        name="encoder_layer",
    )(tok, cot, win_own, wout_own, vec_own, *tables)


def local_fast(tokens, w_in, b_in, w_out, b_out, gain_one, shift_one, gain_two, shift_two, cotangent):
    both = ("seq", "batch")
    parts = lax.axis_size("seq")
    width = tokens.shape[2]
    shard = w_in.shape[1]
    planes = lax.axis_size("batch")
    owner = lax.axis_index("seq") * planes + lax.axis_index("batch")
    part = b_out.shape[0]
    vectors = jnp.zeros((5, width), bf16)
    mine = jnp.stack([gain_one, shift_one, gain_two, shift_two, b_out])
    vectors = lax.dynamic_update_slice(vectors, mine, (0, owner * part))
    bias = lax.dynamic_update_slice(jnp.zeros((parts * planes * shard,), bf16), b_in, (owner * shard,))
    bias = bias.reshape(-1, width)
    vectors = jnp.concatenate([vectors, bias, jnp.zeros((11 - bias.shape[0], width), bf16)])
    out, gtok, _, dw, small = layer_call(tokens, cotangent, w_in.T, w_out, vectors, parts, planes)
    grad_b_in = lax.dynamic_slice(small[5:9].reshape(-1), (owner * shard,), (shard,))
    rest = lax.dynamic_slice(small[:5], (0, owner * part), (5, part))
    return (out, gtok, dw[0].T, grad_b_in, dw[1], rest[4], rest[0], rest[1], rest[2], rest[3])


def hidden_table(extent):
    idx_all = jnp.arange(extent, dtype=jnp.int32)
    angles = (idx_all[:, None] * idx_all[None, :] % extent).astype(jnp.float32) * (
        2.0 * math.pi / extent
    )
    factor = 1.0 / math.sqrt(extent)
    return jnp.concatenate([jnp.cos(angles) * factor, jnp.sin(angles) * factor], axis=1).astype(
        jnp.bfloat16
    )


def sequence_table(length):
    block_rows = min(512, length)
    block_count = length // block_rows
    col_ids = jnp.arange(length, dtype=jnp.int32)
    factor = 1.0 / math.sqrt(length)

    def table_rows(block_index):
        row_ids = block_index * block_rows + jnp.arange(block_rows, dtype=jnp.int32)
        angles = (row_ids[:, None] * col_ids[None, :] % length).astype(jnp.float32) * (
            2.0 * math.pi / length
        )
        return (jnp.stack([jnp.cos(angles), -jnp.sin(angles)]) * factor).astype(jnp.bfloat16)

    blocks = lax.map(table_rows, jnp.arange(block_count, dtype=jnp.int32))
    return jnp.moveaxis(blocks, 1, 0).reshape(2, length, length)


def normalize(values, gain, shift):
    center = values - jnp.mean(values, axis=-1, keepdims=True)
    inv_std = lax.rsqrt(jnp.mean(center * center, axis=-1, keepdims=True) + epsilon)
    normed = center * inv_std
    return (normed * gain + shift, normed, inv_std)


def norm_back(grad_out, normed, inv_std, gain):
    scaled = grad_out * gain
    centered = scaled - jnp.mean(scaled, axis=-1, keepdims=True)
    return inv_std * (centered - normed * jnp.mean(scaled * normed, axis=-1, keepdims=True))


def local(tokens, w_in, b_in, w_out, b_out, gain_one, shift_one, gain_two, shift_two, cotangent):
    batch_rows, seq_part, model_width = tokens.shape
    length = seq_part * lax.axis_size("seq")
    w_in_all, b_in_all, w_out_all, b_out_all, g_one_all, s_one_all, g_two_all, s_two_all = (
        lax.all_gather(w_in, ("seq", "batch"), axis=1, tiled=True),
        lax.all_gather(b_in, ("seq", "batch"), axis=0, tiled=True),
        lax.all_gather(w_out, ("seq", "batch"), axis=0, tiled=True),
        lax.all_gather(b_out, ("seq", "batch"), axis=0, tiled=True),
        lax.all_gather(gain_one, ("seq", "batch"), axis=0, tiled=True),
        lax.all_gather(shift_one, ("seq", "batch"), axis=0, tiled=True),
        lax.all_gather(gain_two, ("seq", "batch"), axis=0, tiled=True),
        lax.all_gather(shift_two, ("seq", "batch"), axis=0, tiled=True),
    )
    h_table = hidden_table(model_width)
    s_table = sequence_table(length)
    flat_tokens = tokens.reshape(-1, model_width)
    spectra = jnp.dot(flat_tokens, h_table, preferred_element_type=jnp.float32).astype(jnp.bfloat16)
    spectra = spectra.reshape(batch_rows, seq_part, 2, model_width)
    mixed_cols = jnp.einsum(
        "plm,bmpc->blc",
        s_table,
        lax.all_to_all(spectra, "seq", split_axis=3, concat_axis=1, tiled=True),
        preferred_element_type=jnp.float32,
    ).astype(jnp.bfloat16)
    mixed = lax.all_to_all(mixed_cols, "seq", split_axis=1, concat_axis=2, tiled=True)
    resid_one = flat_tokens.astype(jnp.float32) + mixed.reshape(-1, model_width).astype(jnp.float32)
    act_one, normed_one, inv_one = normalize(
        resid_one, g_one_all.astype(jnp.float32), s_one_all.astype(jnp.float32)
    )
    act_low = act_one.astype(jnp.bfloat16)
    pre_act = jnp.dot(act_low, w_in_all, preferred_element_type=jnp.float32) + b_in_all.astype(
        jnp.float32
    )
    activ, gelu_back = jax.vjp(partial(jax.nn.gelu, approximate=True), pre_act)
    hidden_low = activ.astype(jnp.bfloat16)
    branch = jnp.dot(hidden_low, w_out_all, preferred_element_type=jnp.float32) + b_out_all.astype(
        jnp.float32
    )
    resid_two = act_one + branch
    result, normed_two, inv_two = normalize(
        resid_two, g_two_all.astype(jnp.float32), s_two_all.astype(jnp.float32)
    )
    grad_out = cotangent.reshape(-1, model_width).astype(jnp.float32)
    grad_g_two = jnp.sum(grad_out * normed_two, axis=0)
    grad_s_two = jnp.sum(grad_out, axis=0)
    grad_r_two = norm_back(grad_out, normed_two, inv_two, g_two_all.astype(jnp.float32))
    grad_branch = grad_r_two.astype(jnp.bfloat16)
    grad_b_out = jnp.sum(grad_branch.astype(jnp.float32), axis=0)
    grad_w_out = jnp.einsum(
        "tf,td->fd", hidden_low, grad_branch, preferred_element_type=jnp.float32
    )
    grad_hidden = jnp.einsum(
        "td,fd->tf", grad_branch, w_out_all, preferred_element_type=jnp.float32
    )
    grad_pre = gelu_back(grad_hidden)[0].astype(jnp.bfloat16)
    grad_b_in = jnp.sum(grad_pre.astype(jnp.float32), axis=0)
    grad_w_in = jnp.einsum("td,tf->df", act_low, grad_pre, preferred_element_type=jnp.float32)
    grad_a_one = grad_r_two + jnp.einsum(
        "tf,df->td", grad_pre, w_in_all, preferred_element_type=jnp.float32
    )
    grad_g_one = jnp.sum(grad_a_one * normed_one, axis=0)
    grad_s_one = jnp.sum(grad_a_one, axis=0)
    grad_r_one = norm_back(grad_a_one, normed_one, inv_one, g_one_all.astype(jnp.float32))
    grad_mix = grad_r_one.astype(jnp.bfloat16).reshape(batch_rows, seq_part, model_width)
    spec_grad = jnp.einsum(
        "plm,blc->bmpc",
        s_table,
        lax.all_to_all(grad_mix, "seq", split_axis=2, concat_axis=1, tiled=True),
        preferred_element_type=jnp.float32,
    ).astype(jnp.bfloat16)
    grad_spec = lax.all_to_all(spec_grad, "seq", split_axis=1, concat_axis=3, tiled=True)
    grad_flat = grad_r_one + jnp.einsum(
        "te,de->td",
        grad_spec.reshape(-1, 2 * model_width),
        h_table,
        preferred_element_type=jnp.float32,
    )
    sum_w_in, sum_b_in, sum_w_out, sum_b_out, sum_g_one, sum_s_one, sum_g_two, sum_s_two = (
        lax.psum_scatter(grad_w_in, ("seq", "batch"), scatter_dimension=1, tiled=True),
        lax.psum_scatter(grad_b_in, ("seq", "batch"), scatter_dimension=0, tiled=True),
        lax.psum_scatter(grad_w_out, ("seq", "batch"), scatter_dimension=0, tiled=True),
        lax.psum_scatter(grad_b_out, ("seq", "batch"), scatter_dimension=0, tiled=True),
        lax.psum_scatter(grad_g_one, ("seq", "batch"), scatter_dimension=0, tiled=True),
        lax.psum_scatter(grad_s_one, ("seq", "batch"), scatter_dimension=0, tiled=True),
        lax.psum_scatter(grad_g_two, ("seq", "batch"), scatter_dimension=0, tiled=True),
        lax.psum_scatter(grad_s_two, ("seq", "batch"), scatter_dimension=0, tiled=True),
    )
    output = result.astype(jnp.bfloat16).reshape(batch_rows, seq_part, model_width)
    grad_tokens = grad_flat.astype(jnp.bfloat16).reshape(batch_rows, seq_part, model_width)
    return (
        output,
        grad_tokens,
        sum_w_in,
        sum_b_in,
        sum_w_out,
        sum_b_out,
        sum_g_one,
        sum_s_one,
        sum_g_two,
        sum_s_two,
    )


def solution(mesh):
    every = P(("seq", "batch"))

    def whole(tokens, w_in, *rest):
        parts = mesh.shape["seq"]
        fits = (
            parts == 8
            and tokens.shape[1] == 512 * parts
            and tokens.shape[2] % (32 * parts) == 0
            and w_in.shape[1] % (3 * 128) == 0
            and tokens.shape[0] == 4 * mesh.shape["batch"]
        )
        return jax.shard_map(
            local_fast if fits else local,
            mesh=mesh,
            in_specs=(
                P("batch", "seq", None),
                P(None, ("seq", "batch")),
                every,
                P(("seq", "batch"), None),
                every,
                every,
                every,
                every,
                every,
                P("batch", "seq", None),
            ),
            out_specs=(
                P("batch", "seq", None),
                P("batch", "seq", None),
                P(None, ("seq", "batch")),
                every,
                P(("seq", "batch"), None),
                every,
                every,
                every,
                every,
                every,
            ),
            check_vma=False,
        )(tokens, w_in, *rest)

    return whole
```

```python
from functools import partial
import math

import jax
import jax.numpy as jnp
import ml_dtypes
import numpy as np
from jax import lax
from jax.experimental import pallas as pl
from jax.experimental.pallas import tpu as pltpu
from jax.sharding import PartitionSpec as P

epsilon = 1e-05
f32, bf16 = jnp.float32, jnp.bfloat16
MESH = pl.DeviceIdType.MESH


def dot_nn(a, b):
    return lax.dot_general(a, b, (((1,), (0,)), ((), ())), preferred_element_type=f32)


def dot_nt(a, b):
    return lax.dot_general(a, b, (((1,), (1,)), ((), ())), preferred_element_type=f32)


def dot_tn(a, b):
    return lax.dot_general(a, b, (((0,), (0,)), ((), ())), preferred_element_type=f32)


def plan_columns(width, parts):
    pairs = width // 2 // parts
    r = np.arange(width)
    dev, kind, i = r // (2 * pairs), (r // pairs) % 2, r % pairs
    j = dev * pairs + i
    first = (kind == 1) & (j == 0)
    return j, kind, first


def packed_hidden(width, parts):
    j, kind, first = plan_columns(width, parts)
    k = np.arange(width)
    angle = (j[:, None] * k[None, :] % width) * (2.0 * math.pi / width)
    table = np.where(kind[:, None] == 0, np.cos(angle), np.sin(angle))
    nyquist = np.cos(np.pi * (k % 2))
    table = np.where(first[:, None], nyquist[None, :], table) / math.sqrt(width)
    return table.astype(np.float32).astype(ml_dtypes.bfloat16)


def column_order(width, parts):
    j, kind, first = plan_columns(width, parts)
    col = np.where(kind == 0, j, np.where(first, width // 2, (width - j) % width))
    return (col[:, None] == np.arange(width)[None, :]).astype(ml_dtypes.bfloat16)


def inner_table(span, length):
    a = np.arange(span)
    angle = (a[:, None] * a[None, :] % span) * (2.0 * math.pi / span)
    table = np.concatenate([np.cos(angle), np.sin(angle)], axis=0)
    return (table / math.sqrt(length)).astype(np.float32).astype(ml_dtypes.bfloat16)


def twiddles(parts, span):
    b = np.arange(parts)[:, None]
    angle = b * np.arange(span)[None, :] * (2.0 * math.pi / (parts * span))
    return np.concatenate([np.cos(angle), np.sin(angle)], axis=0).astype(np.float32)


def add(a, b):
    return (a[0] + b[0], a[1] + b[1])


def sub(a, b):
    return (a[0] - b[0], a[1] - b[1])


def minus_i(a):
    return (a[1], -a[0])


def dft4(x0, x1, x2, x3):
    t0, t1, t2, t3 = add(x0, x2), sub(x0, x2), add(x1, x3), sub(x1, x3)
    r = minus_i(t3)
    return add(t0, t2), add(t1, r), sub(t0, t2), sub(t1, r)


def dft8(x):
    e = dft4(x[0], x[2], x[4], x[6])
    o = dft4(x[1], x[3], x[5], x[7])
    h = math.sqrt(0.5)
    o1 = (h * (o[1][0] + o[1][1]), h * (o[1][1] - o[1][0]))
    o2 = minus_i(o[2])
    o3 = (h * (o[3][1] - o[3][0]), -h * (o[3][0] + o[3][1]))
    o = (o[0], o1, o2, o3)
    return [add(e[k], o[k]) for k in range(4)] + [sub(e[k], o[k]) for k in range(4)]


def radix_step(rec, tw, t_ref, parts, pairs, span):
    groups = pairs // 16
    count = 2 * parts * pairs

    row = lax.broadcasted_iota(jnp.int32, (16, 128), 0)
    for u in range(span // 128):
        lanes = pl.ds(u * 128, 128)
        lanes_im = pl.ds(span + u * 128, 128)
        extra = [jnp.zeros((16, 128), f32), jnp.zeros((16, 128), f32)]
        for g in range(groups):
            x = []
            for s in range(parts):
                re = rec[s, g * 16:g * 16 + 16, lanes].astype(f32)
                im = rec[s, pairs + g * 16:pairs + g * 16 + 16, lanes].astype(f32)
                x.append((re, -im))
            y = dft8(x)
            for b in range(parts):
                c, s = tw[b:b + 1, lanes], tw[parts + b:parts + b + 1, lanes]
                conj = y[(parts - b) % parts]
                for kind, (zr, zi) in enumerate((y[b], (conj[0], -conj[1]))):
                    tr = c * zr + s * zi
                    ti = c * zi - s * zr
                    base = (kind * parts + b) * pairs + g * 16
                    t_ref[base:base + 16, lanes] = tr.astype(bf16)
                    t_ref[base:base + 16, lanes_im] = ti.astype(bf16)
                    if g == 0:
                        hit = row == kind * parts + b
                        extra[0] = jnp.where(hit, jnp.broadcast_to(-ti[0:1], (16, 128)), extra[0])
                        extra[1] = jnp.where(hit, jnp.broadcast_to(tr[0:1], (16, 128)), extra[1])
        t_ref[count:count + 16, lanes] = extra[0].astype(bf16)
        t_ref[count:count + 16, lanes_im] = extra[1].astype(bf16)


def spread_step(o_ref, put, me, parts, pairs, u, half):
    count = 2 * parts * pairs
    lanes = pl.ds((u - half * parts // 4) * 128, 128)
    low = lax.broadcasted_iota(jnp.int32, (16, 128), 1) < 64
    row = lax.broadcasted_iota(jnp.int32, (16, 128), 0)
    special = (row == 0) & (jnp.zeros((16, 128), jnp.int32) + me == 0)
    extra = o_ref[count:count + 16, lanes]
    for p in range(parts // 2):
        for g in range(pairs // 16):
            v = [[None, None], [None, None]]
            for kind in range(2):
                for h in range(2):
                    base = (kind * parts + 2 * p + h) * pairs + g * 16
                    v[kind][h] = o_ref[base:base + 16, lanes]
            if g == 0:
                for h in range(2):
                    b = 2 * p + h
                    even = 0.5 * (v[0][h] + v[1][h])
                    odd = jnp.broadcast_to(0.5 * (extra[b:b + 1] - extra[parts + b:parts + b + 1]), (16, 128))
                    v[0][h] = jnp.where(special, even, v[0][h])
                    v[1][h] = jnp.where(special, odd, v[1][h])
            for kind in range(2):
                v0, v1 = v[kind]
                rows = pl.ds(kind * pairs + g * 16, 16)
                cols = pl.ds(p * 128, 128)
                put(2 * u, rows, cols, jnp.where(low, v0, pltpu.roll(v1, 64, 1)).astype(bf16))
                put(2 * u + 1, rows, cols, jnp.where(low, pltpu.roll(v0, 64, 1), v1).astype(bf16))


def fold(v):
    total = v[0:8]
    for k in range(8, v.shape[0], 8):
        total = total + v[k:k + 8]
    return total


def rows_of(ref, at):
    return jnp.concatenate([ref[c, at, :] for c in range(ref.shape[0])], axis=1)


def set_rows(ref, at, value):
    for c in range(ref.shape[0]):
        ref[c, at, :] = value[:, c * 128:(c + 1) * 128]


def mean_of(v):
    return jnp.mean(v, axis=-1, keepdims=True)


def gelu_pair(x):
    k = math.sqrt(2.0 / math.pi)
    c = 0.044715
    x2 = x * x
    half = 0.5 + 0.5 * jnp.tanh(x * (k + (k * c) * x2))
    value = x * half
    slope = half + value * (1.0 - half) * (2.0 * k + (6.0 * k * c) * x2)
    return value, slope


def ffn_hidden(x_get, nbuf, sbuf, alow, hid, slope, weight, vec, bias_in, rows_step):
    for r in range(0, nbuf.shape[1], rows_step):
        at = pl.ds(r, rows_step)
        v = x_get(at).astype(f32) + rows_of(nbuf, at)
        center = v - mean_of(v)
        inv = lax.rsqrt(mean_of(center * center) + epsilon)
        n = center * inv
        set_rows(nbuf, at, n)
        sbuf[at, :] = jnp.broadcast_to(inv, (rows_step, 128))
        alow[at, :] = (n * vec[0:1] + vec[1:2]).astype(bf16)
    for c in range(hid.shape[0]):
        value, back = gelu_pair(dot_nt(alow[...], weight(0, c)) + bias_in[c])
        hid[c] = value.astype(bf16)
        slope[c] = back.astype(bf16)


def ffn_branch(hid, acc, weight):
    steps = hid.shape[0]
    every = jnp.concatenate([hid[c] for c in range(steps)], axis=1)
    acc[...] = dot_nn(every, weight(1, 0, steps))


def ffn_middle(nbuf, acc, glow, cot, outv, vec, sums, rows_step):
    for r in range(0, nbuf.shape[1], rows_step):
        at = pl.ds(r, rows_step)
        v = rows_of(nbuf, at) * vec[0:1] + vec[1:2] + (acc[at, :] + vec[4:5])
        center = v - mean_of(v)
        inv = lax.rsqrt(mean_of(center * center) + epsilon)
        n = center * inv
        outv[at, :] = (n * vec[2:3] + vec[3:4]).astype(bf16)
        g = cot[at, :].astype(f32)
        q = g * vec[2:3]
        gr = inv * (q - mean_of(q) - n * mean_of(q * n))
        acc[at, :] = gr
        low = gr.astype(bf16)
        glow[at, :] = low
        sums[2] += fold(g * n)
        sums[3] += fold(g)
        sums[4] += fold(low.astype(f32))


def ffn_backward(nbuf, sbuf, hid, slope, acc, glow, weight, bsum, vec, sums, rows_step, put):
    for c in range(hid.shape[0]):
        gh = dot_nt(glow[...], weight(1, c))
        gpre = (gh * slope[c].astype(f32)).astype(bf16)
        slope[c] = gpre
        bsum[c] += fold(gpre.astype(f32))
        acc[...] += dot_nn(gpre, weight(0, c))
    for r in range(0, nbuf.shape[1], rows_step):
        at = pl.ds(r, rows_step)
        ga = acc[at, :]
        n = rows_of(nbuf, at)
        sums[0] += fold(ga * n)
        sums[1] += fold(ga)
        q = ga * vec[0:1]
        put(at, sbuf[at, 0:1] * (q - mean_of(q) - n * mean_of(q * n)))


def ffn_grads(alow, hid, slope, glow, dw):
    chunk = hid.shape[2]
    for c in range(hid.shape[0]):
        at = pl.ds(c * chunk, chunk)
        dw[1, at, :] += dot_tn(hid[c], glow[...])
        dw[0, at, :] += dot_tn(slope[c], alow[...])


def layer_kernel(geo, tok, cot, win_own, wout_own, vec_own, hp_all, wd_all, cp_all, tw,
                 out, gtok, grow, dw_own, small,
                 tokv, cotv, outv, w0, w1, hp, wd, cp, dw, send1, recv1, send2, recv2, t_ref, o_ref,
                 nbuf, sbuf, alow, hid, slope, acc, glow, sums, bsum, rz, rze, rzl, sv, rv, vec, bias_in,
                 ss1, rs1, ss2, rs2, free1, free2, load, io,
                 s_core, r_core, s_first, r_first, s_next, r_next, s_z, r_z, s_vec, r_vec, ready,
                 s_spread, r_spread, s_relay, r_relay, s_pair, r_pair, s_early, r_early, s_late, r_late):
    parts, pairs, span, width, jobs, slots, chunk, rows_step, planes = geo
    shard = dw.shape[1] // (parts * planes)
    me = lax.axis_index("seq")
    plane = lax.axis_index("batch")

    def peer(d):
        return lax.rem(me + d, parts)

    def load_of(k):
        if k < jobs:
            return pltpu.make_async_copy(tok.at[k], tokv.at[k], load.at[k])
        a, b = ((hp_all, hp), (wd_all, wd), (cp_all, cp))[k - jobs]
        return pltpu.make_async_copy(a, b, load.at[k])

    for k in (jobs, 0, 1, jobs + 1, 2, 3, jobs + 2):
        load_of(k).start()

    core, quad = lax.rem(me, 2), me // 2
    quads = parts // 2
    x, y = lax.rem(quad, 2), quad // 2
    partner = (me + 1 - 2 * core, plane)
    x_peer = (me + 2 - 4 * x, plane)
    y_peer = (me + 4 - 8 * y, plane)
    quad_x, quad_y = quad + 1 - 2 * x, quad + 2 - 4 * y
    last = planes - 1

    def send(src, dst, s, r, to):
        return pltpu.make_async_remote_copy(
            src_ref=src, dst_ref=dst, send_sem=s, recv_sem=r, device_id=to, device_id_type=MESH)

    own_loads = (
        pltpu.make_async_copy(win_own, w0.at[quad, core, plane, pl.ds(0, shard)], load.at[jobs + 3]),
        pltpu.make_async_copy(vec_own, w0.at[quad, core, plane, pl.ds(shard, 16)], load.at[jobs + 4]),
        pltpu.make_async_copy(wout_own, w1.at[quad, core, plane], load.at[jobs + 5]),
    )
    for copy in own_loads:
        copy.start()

    barrier = pltpu.get_barrier_semaphore()

    def greet(d, carry):
        pl.semaphore_signal(barrier, inc=1, device_id=(peer(d), plane), device_id_type=MESH)
        return carry

    def greet_z(d, carry):
        pl.semaphore_signal(barrier, inc=1, device_id=(me, lax.rem(plane + d, planes)), device_id_type=MESH)
        return carry

    lax.fori_loop(1, parts, greet, 0)
    lax.fori_loop(1, planes, greet_z, 0)
    pl.semaphore_wait(barrier, parts - 1 + planes - 1)

    def remote(send, recv, ss, rs, k, d):
        p = peer(d)
        return pltpu.make_async_remote_copy(
            src_ref=send.at[lax.rem(k, 2), p], dst_ref=recv.at[lax.rem(k, slots), me],
            send_sem=ss.at[lax.rem(k, 2), d], recv_sem=rs.at[lax.rem(k, slots), d],
            device_id=(p, plane), device_id_type=MESH)

    def wait_sends(send, recv, ss, rs, k):
        def one(d, carry):
            remote(send, recv, ss, rs, k, d).wait_send()
            return carry

        lax.fori_loop(1, parts, one, 0)

    def wait_recvs(send, recv, ss, rs, k):
        def one(d, carry):
            source = lax.rem(me + parts - d, parts)
            slot = lax.rem(k, slots)
            pltpu.make_async_remote_copy(
                src_ref=send.at[0, 0], dst_ref=recv.at[slot, source],
                send_sem=ss.at[0, d], recv_sem=rs.at[slot, d],
                device_id=(source, plane), device_id_type=MESH).wait_recv()
            return carry

        lax.fori_loop(1, parts, one, 0)

    def tell(sem, k):
        def one(d, carry):
            pl.semaphore_signal(sem.at[lax.rem(k, slots)], inc=1, device_id=(peer(d), plane), device_id_type=MESH)
            return carry

        lax.fori_loop(1, parts, one, 0)

    def in_plane(d):
        return 2 * lax.rem(quad + d, quads) + core

    def along(d):
        return lax.rem(plane + d, planes)

    def spread_z(d):
        block = w0.at[quad, core, plane]
        return send(block, block, s_spread.at[0, d], r_spread.at[0, d], (me, along(d)))

    def spread_out(d):
        block = w1.at[quad, core, plane]
        return send(block, block, s_spread.at[1, d], r_spread.at[1, d], (in_plane(d), plane))

    def spread_in(n):
        block = w0.at[quad, core]
        return send(block, block, s_spread.at[2, n], r_spread.at[2, n], (x_peer, y_peer)[n])

    def pass_in(n):
        block = w0.at[quad_x if n == 0 else quad_y, core, pl.ds(n * planes // 2, planes // 2)]
        return send(block, block, s_spread.at[2, 2 + n], r_spread.at[2, 2 + n], (y_peer, x_peer)[n])

    def relay(origin, up):
        block = w1.at[:, core, origin]
        return send(block, block, s_relay.at[up, origin], r_relay.at[origin], (me, plane + 2 * up - 1))

    def pair_in(q):
        block = w0.at[q, core]
        return send(block, block, s_pair.at[0, q], r_pair.at[0, q], partner)

    def pair_out(origin):
        block = w1.at[:, core, origin]
        return send(block, block, s_pair.at[1, origin], r_pair.at[1, origin], partner)

    def relay_step(j):
        below, above = plane - 1 - j, plane + 1 + j

        @pl.when(below >= 0)
        def _():
            relay(below, 1).wait_recv()

            @pl.when(plane < last)
            def _():
                relay(below, 1).start()

            pair_out(below).start()

        @pl.when(above <= last)
        def _():
            relay(above, 0).wait_recv()

            @pl.when(plane > 0)
            def _():
                relay(above, 0).start()

            pair_out(above).start()

    def gather_start():
        for copy in own_loads:
            copy.wait()
        for d in range(1, planes):
            spread_z(d).start()
        for d in range(1, quads):
            spread_out(d).start()

    def gather_out():
        for d in range(1, quads):
            spread_out(d).wait_recv()

        @pl.when(plane < last)
        def _():
            relay(plane, 1).start()

        @pl.when(plane > 0)
        def _():
            relay(plane, 0).start()

        pair_out(plane).start()

    def gather_in():
        for d in range(1, planes):
            spread_z(d).wait_recv()
        for n in range(2):
            spread_in(n).start()
        pair_in(quad).start()

    def gather_pass():
        for n in range(2):
            spread_in(n).wait_recv()
        for n in range(2):
            pass_in(n).start()
        pair_in(quad_x).start()
        pair_in(quad_y).start()

    def gather_diagonal():
        for n in range(2):
            pass_in(n).wait_recv()
        pair_in(quads - 1 - quad).start()

    def gather_end_out():
        for origin in range(planes):
            pair_out(origin).wait_recv()

    def gather_end_in():
        for q in range(quads):
            pair_in(q).wait_recv()

        def one(o, carry):
            rest = lax.rem(o, 2 * planes)
            block = w0[o // (2 * planes), rest // planes, lax.rem(rest, planes), shard:shard + 16, :]
            return carry + block.astype(f32)

        total = lax.fori_loop(0, parts * planes, one, jnp.zeros((16, width), f32))
        vec[...] = total[0:8]
        for f in range(0, bsum.shape[0] * chunk, width):
            bias_in[f // chunk, 0:1, f % chunk:f % chunk + width] = total[5 + f // width:6 + f // width]

    def gather_sent():
        for d in range(1, planes):
            spread_z(d).wait_send()
        for d in range(1, quads):
            spread_out(d).wait_send()
        for n in range(2):
            spread_in(n).wait_send()
            pass_in(n).wait_send()
        for q in range(quads):
            pair_in(q).wait_send()
        for origin in range(planes):
            pair_out(origin).wait_send()

            @pl.when((plane < last) & (origin <= plane))
            def _():
                relay(origin, 1).wait_send()

            @pl.when((plane > 0) & (origin >= plane))
            def _():
                relay(origin, 0).wait_send()

    def weight(m, c, count=1):
        n = chunk // (2 * planes * shard)
        at = pl.ds(c * n, count * n)
        block = w0[at, :, :, 0:shard, :] if m == 0 else w1[at]
        return block.reshape(count * chunk, width)

    def told(sem, k):
        pl.semaphore_wait(sem.at[lax.rem(k, slots)], parts - 1)

    one_way = (send1, recv1, ss1, rs1)
    way_back = (send2, recv2, ss2, rs2)

    def hidden_job(k):
        @pl.when(k >= 2)
        def _():
            wait_sends(*one_way, k - 2)

        @pl.when(k >= slots)
        def _():
            told(free1, k)

        table = dot_nt(hp[...], tokv[lax.rem(k, jobs)]).astype(bf16)
        send1[lax.rem(k, 2)] = table.reshape(parts, 2 * pairs, span)
        recv1[lax.rem(k, slots), me] = send1[lax.rem(k, 2), me]

        def one(d, carry):
            remote(*one_way, k, d).start()
            return carry

        lax.fori_loop(1, parts, one, 0)

    def sequence_job(k, carry):
        wait_recvs(*one_way, k)
        radix_step(recv1.at[lax.rem(k, slots)], tw, t_ref, parts, pairs, span)

        @pl.when(k < 2 * jobs - slots)
        def _():
            tell(free1, k)

        @pl.when(k >= 2)
        def _():
            wait_sends(*way_back, k - 2)

        @pl.when(k >= slots)
        def _():
            told(free2, k)

        slot = lax.rem(k, 2)
        half = span // 2

        def put(p, rows, cols, value):
            send2[slot, p, rows, cols] = value

        for base in range(2):
            o_ref[...] = dot_nn(t_ref[...], wd[:, base * half:(base + 1) * half])
            for u in range(base * parts // 4, (base + 1) * parts // 4):
                spread_step(o_ref, put, me, parts, pairs, u, base)
        recv2[lax.rem(k, slots), me] = send2[slot, me]

        def one(d, carry):
            remote(*way_back, k, d).start()
            return carry

        lax.fori_loop(1, parts, one, 0)
        return carry

    def mixed_job(k):
        wait_recvs(*way_back, k)
        blocks = recv2[lax.rem(k, slots)].reshape(width, span)
        natural = dot_tn(blocks, cp[...])
        step = span // parts
        for b in range(parts):
            for c in range(width // 128):
                nbuf[c, pl.ds(b, step, stride=parts), :] = natural[b * step:(b + 1) * step, c * 128:(c + 1) * 128]

    gather_start()
    load_of(jobs).wait()
    load_of(0).wait()
    hidden_job(0)
    dw[...] = jnp.zeros_like(dw)
    sums[...] = jnp.zeros_like(sums)
    bsum[...] = jnp.zeros_like(bsum)
    gather_out()
    gather_in()
    for k in (1, 2, 3, jobs + 1, jobs + 2):
        load_of(k).wait()

    sequence_job(0, 0)
    relay_step(0)
    gather_pass()
    hidden_job(1)
    relay_step(1)
    hidden_job(2)
    gather_diagonal()
    hidden_job(3)
    gather_end_in()

    def out_copy(i):
        return pltpu.make_async_copy(outv, out.at[i], io.at[0])

    def cot_copy(i):
        return pltpu.make_async_copy(cot.at[i], cotv, io.at[1])

    def row_copy(i):
        return pltpu.make_async_copy(acc, grow.at[i], io.at[2])

    def main(i, carry):
        cot_copy(i).start()
        mixed_job(i)
        tell(free2, i)
        ffn_hidden(lambda at: tokv[i, at, :], nbuf, sbuf, alow, hid, slope, weight, vec, bias_in, rows_step)
        lax.fori_loop(i + 1 + i // 3, i + 2 + i // 2 + i // 3, sequence_job, 0)

        @pl.when(i == 0)
        def _():
            relay_step(2)
            gather_end_out()

        ffn_branch(hid, acc, weight)
        cot_copy(i).wait()

        @pl.when(i > 0)
        def _():
            out_copy(i - 1).wait()

        ffn_middle(nbuf, acc, glow, cotv, outv, vec, sums, rows_step)
        out_copy(i).start()

        def put(at, value):
            acc[at, :] = value
            tokv[i, at, :] = value.astype(bf16)

        ffn_backward(nbuf, sbuf, hid, slope, acc, glow, weight, bsum, vec, sums, rows_step, put)
        row_copy(i).start()
        hidden_job(i + jobs)
        ffn_grads(alow, hid, slope, glow, dw)
        row_copy(i).wait()
        return carry

    lax.fori_loop(0, jobs, main, 0)

    most = shard - 16

    def rows_at(start, count=shard):
        return pl.ds(pl.multiple_of(start, shard), count)

    def target(v):
        return lax.rem(plane + 1 + v, planes)

    def owned(q, c, v):
        return rows_at(((2 * q + c) * planes + target(v)) * shard)

    keep, head, tail = pl.ds(0, shard), pl.ds(0, most), pl.ds(shard, 16)

    def core_copy(v):
        return send(w1.at[v], w0.at[v, :, :, keep], s_core.at[v], r_core.at[v], partner)

    def first_copy(v, m):
        at = pl.ds(2 * m, 2)
        return send(w1.at[2 + v // 2, lax.rem(v, 2), at, head], w1.at[v // 2, lax.rem(v, 2), at, head],
                    s_first.at[v, m], r_first.at[v, m], (x_peer, y_peer)[m])

    def next_copy(v, m):
        return send(w0.at[0, v // 2, 2 * lax.rem(v, 2) + m, head],
                    (alow, glow)[m].at[pl.ds(pl.multiple_of(v * most, most), most)],
                    s_next.at[v, m], r_next.at[v, m], (y_peer, x_peer)[m])

    def z_copy(v):
        return send(w0.at[1, v // 2, pl.ds(2 * lax.rem(v, 2), 2), head], rz.at[v],
                    s_z.at[v], r_z.at[v], (me, target(v)))

    def early_copy(v):
        return send(w0.at[v, :, :, tail], rze.at[v], s_early.at[v], r_early.at[v], (me, target(v)))

    def late_copy(d):
        q = lax.rem(quad + d, quads)
        return send(w0.at[quads - 1, q // 2, pl.ds(2 * lax.rem(q, 2), 2), tail], rzl.at[d - 1],
                    s_late.at[d - 1], r_late.at[d - 1], (in_plane(d), plane))

    def vec_copy(k):
        to = (partner, x_peer, y_peer)[k] if k < 3 else (me, target(k - 3))
        return send(sv.at[min(k, 3)], rv.at[k], s_vec.at[k], r_vec.at[k], to)

    def core_step(v, carry):
        for q in range(quads):
            for m in range(2):
                w1[v, q // 2, 2 * (q % 2) + m] = dw[m, owned(q, 1 - core, v)].astype(bf16)
        core_copy(v).start()
        return carry

    def owned_most(q, v):
        return rows_at(((2 * q + core) * planes + target(v)) * shard, most)

    def owned_rest(q, v):
        return pl.ds(pl.multiple_of(((2 * q + core) * planes + target(v)) * shard + most, 16), 16)

    def first_step(v, carry):
        core_copy(v).wait_recv()
        for q in range(quads):
            for m in range(2):
                at = owned(q, core, v)
                dw[m, at] += w0[v, q // 2, 2 * (q % 2) + m, 0:shard, :].astype(f32)

        @pl.when(v < last)
        def _():
            for q in range(quads):
                for m in range(2):
                    w0[v, q // 2, 2 * (q % 2) + m, shard:shard + 16, :] = dw[m, owned_rest(q, v)].astype(bf16)
            early_copy(v).start()

        for k in range(2):
            for m in range(2):
                q = 2 * k + 1 - x if m == 0 else 2 * (1 - y) + k
                w1[2 + v // 2, lax.rem(v, 2), 2 * m + k, 0:most, :] = dw[m, owned_most(q, v)].astype(bf16)
        for m in range(2):
            first_copy(v, m).start()
        return carry

    def next_step(v, carry):
        for m in range(2):
            first_copy(v, m).wait_recv()
        for k in range(2):
            for m in range(2):
                q = 2 * k + x if m == 0 else 2 * y + k
                dw[m, owned_most(q, v)] += w1[v // 2, lax.rem(v, 2), 2 * m + k, 0:most, :].astype(f32)
        for m in range(2):
            q = 2 * (1 - y) + x if m == 0 else 2 * y + 1 - x
            w0[0, v // 2, 2 * lax.rem(v, 2) + m, 0:most, :] = dw[m, owned_most(q, v)].astype(bf16)
            next_copy(v, m).start()
        return carry

    def z_step(v, carry):
        for m in range(2):
            next_copy(v, m).wait_recv()
            dw[m, owned_most(quad, v)] += (alow, glow)[m][pl.ds(pl.multiple_of(v * most, most), most)].astype(f32)

        @pl.when(v < last)
        def _():
            for m in range(2):
                w0[1, v // 2, 2 * lax.rem(v, 2) + m, 0:most, :] = dw[m, owned_most(quad, v)].astype(bf16)
            z_copy(v).start()

        return carry

    def late_step():
        for v in range(last):
            early_copy(v).wait_recv()
        for q in range(quads):
            for m in range(2):
                at = owned_rest(q, last)
                total = dw[m, at]
                for v in range(last):
                    total = total + rze[v, q // 2, 2 * (q % 2) + m].astype(f32)
                dw[m, at] = total
                w0[quads - 1, q // 2, 2 * (q % 2) + m, shard:shard + 16, :] = total.astype(bf16)
        for d in range(1, quads):
            late_copy(d).start()

    def vec_step(k):
        if k == 0:
            sv[0] = jnp.zeros_like(sv[0])
            for j in range(5):
                sv[0, j:j + 1] = jnp.sum(sums[j], axis=0, keepdims=True)
            piece = math.gcd(width, chunk)
            for f in range(0, bsum.shape[0] * chunk, piece):
                sv[0, 5 + f // width:6 + f // width, f % width:f % width + piece] = jnp.sum(
                    bsum[f // chunk, :, f % chunk:f % chunk + piece], axis=0, keepdims=True)
        else:
            vec_copy(k - 1).wait_recv()
            sv[k] = sv[k - 1] + rv[k - 1]
        for j in ((k,) if k < 3 else range(3, 2 + planes)):
            vec_copy(j).start()

    def gt_copy(i):
        return pltpu.make_async_copy(tokv.at[i], gtok.at[i], io.at[4 + i])

    def final(i, carry):
        back = pltpu.make_async_copy(grow.at[i], acc, io.at[2])
        back.start()
        mixed_job(i + jobs)
        back.wait()
        for c in range(width // 128):
            tokv[i, :, c * 128:(c + 1) * 128] = (nbuf[c] + acc[:, c * 128:(c + 1) * 128]).astype(bf16)
        gt_copy(i).start()
        return carry

    gather_sent()
    pl.semaphore_signal(ready.at[0], inc=1, device_id=partner, device_id_type=MESH)
    pl.semaphore_wait(ready.at[0], 1)
    lax.fori_loop(0, planes, core_step, 0)
    vec_step(0)

    def core_sent(v, carry):
        core_copy(v).wait_send()
        return carry

    lax.fori_loop(0, planes, core_sent, 0)
    pl.semaphore_signal(ready.at[1], inc=1, device_id=x_peer, device_id_type=MESH)
    pl.semaphore_signal(ready.at[2], inc=1, device_id=y_peer, device_id_type=MESH)
    vec_step(1)
    pl.semaphore_wait(ready.at[1], 1)
    pl.semaphore_wait(ready.at[2], 1)
    lax.fori_loop(0, planes, first_step, 0)
    final(0, 0)
    tell(free2, jobs)
    vec_step(2)
    lax.fori_loop(0, planes // 2, next_step, 0)
    sequence_job(2 * jobs - 1, 0)
    final(1, 0)
    lax.fori_loop(planes // 2, planes, next_step, 0)
    vec_step(3)
    final(2, 0)
    lax.fori_loop(0, planes, z_step, 0)
    late_step()
    final(3, 0)
    own_most, own_rest = owned_most(quad, last), owned_rest(quad, last)
    for v in range(last):
        z_copy(v).wait_recv()
    for d in range(1, quads):
        late_copy(d).wait_recv()
    for m in range(2):
        total = dw[m, own_most]
        for v in range(last):
            total = total + rz[v, m].astype(f32)
        dw_own[m, 0:most] = total
        total = dw[m, own_rest]
        for d in range(1, quads):
            total = total + rzl[d - 1, m].astype(f32)
        dw_own[m, most:shard] = total
    total = sv[3]
    for k in range(3, 2 + planes):
        vec_copy(k).wait_recv()
        total = total + rv[k]
    small[...] = total

    def sent(v, carry):
        for m in range(2):
            first_copy(v, m).wait_send()
            next_copy(v, m).wait_send()
        return carry

    lax.fori_loop(0, planes, sent, 0)
    for k in range(2 * jobs - 2, 2 * jobs):
        wait_sends(*way_back, k)
        wait_sends(*one_way, k)
    for v in range(last):
        z_copy(v).wait_send()
        early_copy(v).wait_send()
    for d in range(1, quads):
        late_copy(d).wait_send()
    for k in range(2 + planes):
        vec_copy(k).wait_send()
    out_copy(jobs - 1).wait()
    for i in range(jobs):
        gt_copy(i).wait()


def layer_call(tok, cot, win_own, wout_own, vec_own, parts, planes):
    jobs, span, width = tok.shape
    shard = wout_own.shape[0]
    ff = shard * parts * planes
    pairs = width // 2 // parts
    chunk, rows_step = ff // (parts // 2), span // 4
    steps = ff // chunk
    length = span * parts
    slots = 3
    geo = (parts, pairs, span, width, jobs, slots, chunk, rows_step, planes)
    tables = (
        jnp.asarray(packed_hidden(width, parts)),
        jnp.asarray(inner_table(span, length)),
        jnp.asarray(column_order(width, parts)),
        jnp.asarray(twiddles(parts, span)),
    )
    hbm, vmem, dma = pl.BlockSpec(memory_space=pl.ANY), pl.BlockSpec(memory_space=pltpu.VMEM), pltpu.SemaphoreType.DMA
    block = (parts, 2 * pairs, span)
    scratch = [
        pltpu.VMEM((jobs, span, width), bf16),
        pltpu.VMEM((span, width), bf16),
        pltpu.VMEM((span, width), bf16),
        pltpu.VMEM((parts // 2, 2, planes, shard + 16, width), bf16),
        pltpu.VMEM((parts // 2, 2, planes, shard, width), bf16),
        pltpu.VMEM((width, width), bf16),
        pltpu.VMEM((2 * span, span), bf16),
        pltpu.VMEM((width, width), bf16),
        pltpu.VMEM((2, ff, width), f32),
        pltpu.VMEM((2,) + block, bf16),
        pltpu.VMEM((slots,) + block, bf16),
        pltpu.VMEM((2,) + block, bf16),
        pltpu.VMEM((slots,) + block, bf16),
        pltpu.VMEM((2 * parts * pairs + 16, 2 * span), bf16),
        pltpu.VMEM((2 * parts * pairs + 16, span // 2), f32),
        pltpu.VMEM((width // 128, span, 128), f32),
        pltpu.VMEM((span, 128), f32),
        pltpu.VMEM((span, width), bf16),
        pltpu.VMEM((steps, span, chunk), bf16),
        pltpu.VMEM((steps, span, chunk), bf16),
        pltpu.VMEM((span, width), f32),
        pltpu.VMEM((span, width), bf16),
        pltpu.VMEM((5, 8, width), f32),
        pltpu.VMEM((steps, 8, chunk), f32),
        pltpu.VMEM((planes - 1, 2, shard - 16, width), bf16),
        pltpu.VMEM((planes - 1, 2, parts // 2, 16, width), bf16),
        pltpu.VMEM((parts // 2 - 1, 2, 16, width), bf16),
        pltpu.VMEM((4, 16, width), f32),
        pltpu.VMEM((2 + planes, 16, width), f32),
        pltpu.VMEM((8, width), f32),
        pltpu.VMEM((steps, 1, chunk), f32),
        dma((2, parts)), dma((slots, parts)), dma((2, parts)), dma((slots, parts)),
        pltpu.SemaphoreType.REGULAR((slots,)), pltpu.SemaphoreType.REGULAR((slots,)),
        dma((jobs + 6,)), dma((4 + jobs,)),
        dma((planes,)), dma((planes,)), dma((planes, 2)), dma((planes, 2)), dma((planes, 2)), dma((planes, 2)),
        dma((planes - 1,)), dma((planes - 1,)), dma((2 + planes,)), dma((2 + planes,)),
        pltpu.SemaphoreType.REGULAR((3,)),
        dma((3, max(parts // 2, planes))), dma((3, max(parts // 2, planes))), dma((2, planes)), dma((planes,)),
        dma((2, max(parts // 2, planes))), dma((2, max(parts // 2, planes))),
        dma((planes - 1,)), dma((planes - 1,)), dma((parts // 2 - 1,)), dma((parts // 2 - 1,)),
    ]
    shape = jax.ShapeDtypeStruct
    return pl.pallas_call(
        partial(layer_kernel, geo),
        out_shape=(
            shape(tok.shape, bf16),
            shape(tok.shape, bf16),
            shape(tok.shape, f32),
            shape((2, shard, width), f32),
            shape((16, width), f32),
        ),
        in_specs=[hbm] * 8 + [vmem],
        out_specs=(hbm,) * 3 + (vmem,) * 2,
        scratch_shapes=scratch,
        compiler_params=pltpu.CompilerParams(
            collective_id=1, has_side_effects=True, vmem_limit_bytes=64 * 1024 * 1024 - 256 * 1024),
        name="encoder_layer",
    )(tok, cot, win_own, wout_own, vec_own, *tables)


def local_fast(tokens, w_in, b_in, w_out, b_out, gain_one, shift_one, gain_two, shift_two, cotangent):
    both = ("seq", "batch")
    parts = lax.axis_size("seq")
    width = tokens.shape[2]
    shard = w_in.shape[1]
    planes = lax.axis_size("batch")
    owner = lax.axis_index("seq") * planes + lax.axis_index("batch")
    part = b_out.shape[0]
    vectors = jnp.zeros((5, width), bf16)
    mine = jnp.stack([gain_one, shift_one, gain_two, shift_two, b_out])
    vectors = lax.dynamic_update_slice(vectors, mine, (0, owner * part))
    bias = lax.dynamic_update_slice(jnp.zeros((parts * planes * shard,), bf16), b_in, (owner * shard,))
    bias = bias.reshape(-1, width)
    vectors = jnp.concatenate([vectors, bias, jnp.zeros((11 - bias.shape[0], width), bf16)])
    out, gtok, _, dw, small = layer_call(tokens, cotangent, w_in.T, w_out, vectors, parts, planes)
    grad_b_in = lax.dynamic_slice(small[5:9].reshape(-1), (owner * shard,), (shard,))
    rest = lax.dynamic_slice(small[:5], (0, owner * part), (5, part))
    return (out, gtok, dw[0].T, grad_b_in, dw[1], rest[4], rest[0], rest[1], rest[2], rest[3])


def hidden_table(extent):
    idx_all = jnp.arange(extent, dtype=jnp.int32)
    angles = (idx_all[:, None] * idx_all[None, :] % extent).astype(jnp.float32) * (
        2.0 * math.pi / extent
    )
    factor = 1.0 / math.sqrt(extent)
    return jnp.concatenate([jnp.cos(angles) * factor, jnp.sin(angles) * factor], axis=1).astype(
        jnp.bfloat16
    )


def sequence_table(length):
    block_rows = min(512, length)
    block_count = length // block_rows
    col_ids = jnp.arange(length, dtype=jnp.int32)
    factor = 1.0 / math.sqrt(length)

    def table_rows(block_index):
        row_ids = block_index * block_rows + jnp.arange(block_rows, dtype=jnp.int32)
        angles = (row_ids[:, None] * col_ids[None, :] % length).astype(jnp.float32) * (
            2.0 * math.pi / length
        )
        return (jnp.stack([jnp.cos(angles), -jnp.sin(angles)]) * factor).astype(jnp.bfloat16)

    blocks = lax.map(table_rows, jnp.arange(block_count, dtype=jnp.int32))
    return jnp.moveaxis(blocks, 1, 0).reshape(2, length, length)


def normalize(values, gain, shift):
    center = values - jnp.mean(values, axis=-1, keepdims=True)
    inv_std = lax.rsqrt(jnp.mean(center * center, axis=-1, keepdims=True) + epsilon)
    normed = center * inv_std
    return (normed * gain + shift, normed, inv_std)


def norm_back(grad_out, normed, inv_std, gain):
    scaled = grad_out * gain
    centered = scaled - jnp.mean(scaled, axis=-1, keepdims=True)
    return inv_std * (centered - normed * jnp.mean(scaled * normed, axis=-1, keepdims=True))


def local(tokens, w_in, b_in, w_out, b_out, gain_one, shift_one, gain_two, shift_two, cotangent):
    batch_rows, seq_part, model_width = tokens.shape
    length = seq_part * lax.axis_size("seq")
    w_in_all, b_in_all, w_out_all, b_out_all, g_one_all, s_one_all, g_two_all, s_two_all = (
        lax.all_gather(w_in, ("seq", "batch"), axis=1, tiled=True),
        lax.all_gather(b_in, ("seq", "batch"), axis=0, tiled=True),
        lax.all_gather(w_out, ("seq", "batch"), axis=0, tiled=True),
        lax.all_gather(b_out, ("seq", "batch"), axis=0, tiled=True),
        lax.all_gather(gain_one, ("seq", "batch"), axis=0, tiled=True),
        lax.all_gather(shift_one, ("seq", "batch"), axis=0, tiled=True),
        lax.all_gather(gain_two, ("seq", "batch"), axis=0, tiled=True),
        lax.all_gather(shift_two, ("seq", "batch"), axis=0, tiled=True),
    )
    h_table = hidden_table(model_width)
    s_table = sequence_table(length)
    flat_tokens = tokens.reshape(-1, model_width)
    spectra = jnp.dot(flat_tokens, h_table, preferred_element_type=jnp.float32).astype(jnp.bfloat16)
    spectra = spectra.reshape(batch_rows, seq_part, 2, model_width)
    mixed_cols = jnp.einsum(
        "plm,bmpc->blc",
        s_table,
        lax.all_to_all(spectra, "seq", split_axis=3, concat_axis=1, tiled=True),
        preferred_element_type=jnp.float32,
    ).astype(jnp.bfloat16)
    mixed = lax.all_to_all(mixed_cols, "seq", split_axis=1, concat_axis=2, tiled=True)
    resid_one = flat_tokens.astype(jnp.float32) + mixed.reshape(-1, model_width).astype(jnp.float32)
    act_one, normed_one, inv_one = normalize(
        resid_one, g_one_all.astype(jnp.float32), s_one_all.astype(jnp.float32)
    )
    act_low = act_one.astype(jnp.bfloat16)
    pre_act = jnp.dot(act_low, w_in_all, preferred_element_type=jnp.float32) + b_in_all.astype(
        jnp.float32
    )
    activ, gelu_back = jax.vjp(partial(jax.nn.gelu, approximate=True), pre_act)
    hidden_low = activ.astype(jnp.bfloat16)
    branch = jnp.dot(hidden_low, w_out_all, preferred_element_type=jnp.float32) + b_out_all.astype(
        jnp.float32
    )
    resid_two = act_one + branch
    result, normed_two, inv_two = normalize(
        resid_two, g_two_all.astype(jnp.float32), s_two_all.astype(jnp.float32)
    )
    grad_out = cotangent.reshape(-1, model_width).astype(jnp.float32)
    grad_g_two = jnp.sum(grad_out * normed_two, axis=0)
    grad_s_two = jnp.sum(grad_out, axis=0)
    grad_r_two = norm_back(grad_out, normed_two, inv_two, g_two_all.astype(jnp.float32))
    grad_branch = grad_r_two.astype(jnp.bfloat16)
    grad_b_out = jnp.sum(grad_branch.astype(jnp.float32), axis=0)
    grad_w_out = jnp.einsum(
        "tf,td->fd", hidden_low, grad_branch, preferred_element_type=jnp.float32
    )
    grad_hidden = jnp.einsum(
        "td,fd->tf", grad_branch, w_out_all, preferred_element_type=jnp.float32
    )
    grad_pre = gelu_back(grad_hidden)[0].astype(jnp.bfloat16)
    grad_b_in = jnp.sum(grad_pre.astype(jnp.float32), axis=0)
    grad_w_in = jnp.einsum("td,tf->df", act_low, grad_pre, preferred_element_type=jnp.float32)
    grad_a_one = grad_r_two + jnp.einsum(
        "tf,df->td", grad_pre, w_in_all, preferred_element_type=jnp.float32
    )
    grad_g_one = jnp.sum(grad_a_one * normed_one, axis=0)
    grad_s_one = jnp.sum(grad_a_one, axis=0)
    grad_r_one = norm_back(grad_a_one, normed_one, inv_one, g_one_all.astype(jnp.float32))
    grad_mix = grad_r_one.astype(jnp.bfloat16).reshape(batch_rows, seq_part, model_width)
    spec_grad = jnp.einsum(
        "plm,blc->bmpc",
        s_table,
        lax.all_to_all(grad_mix, "seq", split_axis=2, concat_axis=1, tiled=True),
        preferred_element_type=jnp.float32,
    ).astype(jnp.bfloat16)
    grad_spec = lax.all_to_all(spec_grad, "seq", split_axis=1, concat_axis=3, tiled=True)
    grad_flat = grad_r_one + jnp.einsum(
        "te,de->td",
        grad_spec.reshape(-1, 2 * model_width),
        h_table,
        preferred_element_type=jnp.float32,
    )
    sum_w_in, sum_b_in, sum_w_out, sum_b_out, sum_g_one, sum_s_one, sum_g_two, sum_s_two = (
        lax.psum_scatter(grad_w_in, ("seq", "batch"), scatter_dimension=1, tiled=True),
        lax.psum_scatter(grad_b_in, ("seq", "batch"), scatter_dimension=0, tiled=True),
        lax.psum_scatter(grad_w_out, ("seq", "batch"), scatter_dimension=0, tiled=True),
        lax.psum_scatter(grad_b_out, ("seq", "batch"), scatter_dimension=0, tiled=True),
        lax.psum_scatter(grad_g_one, ("seq", "batch"), scatter_dimension=0, tiled=True),
        lax.psum_scatter(grad_s_one, ("seq", "batch"), scatter_dimension=0, tiled=True),
        lax.psum_scatter(grad_g_two, ("seq", "batch"), scatter_dimension=0, tiled=True),
        lax.psum_scatter(grad_s_two, ("seq", "batch"), scatter_dimension=0, tiled=True),
    )
    output = result.astype(jnp.bfloat16).reshape(batch_rows, seq_part, model_width)
    grad_tokens = grad_flat.astype(jnp.bfloat16).reshape(batch_rows, seq_part, model_width)
    return (
        output,
        grad_tokens,
        sum_w_in,
        sum_b_in,
        sum_w_out,
        sum_b_out,
        sum_g_one,
        sum_s_one,
        sum_g_two,
        sum_s_two,
    )


def solution(mesh):
    every = P(("seq", "batch"))

    def whole(tokens, w_in, *rest):
        parts = mesh.shape["seq"]
        fits = (
            parts == 8
            and tokens.shape[1] == 512 * parts
            and tokens.shape[2] % (32 * parts) == 0
            and w_in.shape[1] % (3 * 128) == 0
            and tokens.shape[0] == 4 * mesh.shape["batch"]
        )
        return jax.shard_map(
            local_fast if fits else local,
            mesh=mesh,
            in_specs=(
                P("batch", "seq", None),
                P(None, ("seq", "batch")),
                every,
                P(("seq", "batch"), None),
                every,
                every,
                every,
                every,
                every,
                P("batch", "seq", None),
            ),
            out_specs=(
                P("batch", "seq", None),
                P("batch", "seq", None),
                P(None, ("seq", "batch")),
                every,
                P(("seq", "batch"), None),
                every,
                every,
                every,
                every,
                every,
            ),
            check_vma=False,
        )(tokens, w_in, *rest)

    return whole
```

```python
from functools import partial
import math

import jax
import jax.numpy as jnp
import ml_dtypes
import numpy as np
from jax import lax
from jax.experimental import pallas as pl
from jax.experimental.pallas import tpu as pltpu
from jax.sharding import PartitionSpec as P

epsilon = 1e-05
f32, bf16 = jnp.float32, jnp.bfloat16
MESH = pl.DeviceIdType.MESH


def dot_nn(a, b):
    return lax.dot_general(a, b, (((1,), (0,)), ((), ())), preferred_element_type=f32)


def dot_nt(a, b):
    return lax.dot_general(a, b, (((1,), (1,)), ((), ())), preferred_element_type=f32)


def dot_tn(a, b):
    return lax.dot_general(a, b, (((0,), (0,)), ((), ())), preferred_element_type=f32)


def plan_columns(width, parts):
    pairs = width // 2 // parts
    r = np.arange(width)
    dev, kind, i = r // (2 * pairs), (r // pairs) % 2, r % pairs
    j = dev * pairs + i
    first = (kind == 1) & (j == 0)
    return j, kind, first


def packed_hidden(width, parts):
    j, kind, first = plan_columns(width, parts)
    k = np.arange(width)
    angle = (j[:, None] * k[None, :] % width) * (2.0 * math.pi / width)
    table = np.where(kind[:, None] == 0, np.cos(angle), np.sin(angle))
    nyquist = np.cos(np.pi * (k % 2))
    table = np.where(first[:, None], nyquist[None, :], table) / math.sqrt(width)
    return table.astype(np.float32).astype(ml_dtypes.bfloat16)


def column_order(width, parts):
    j, kind, first = plan_columns(width, parts)
    col = np.where(kind == 0, j, np.where(first, width // 2, (width - j) % width))
    return (col[:, None] == np.arange(width)[None, :]).astype(ml_dtypes.bfloat16)


def inner_table(span, length):
    a = np.arange(span)
    angle = (a[:, None] * a[None, :] % span) * (2.0 * math.pi / span)
    table = np.concatenate([np.cos(angle), np.sin(angle)], axis=0)
    return (table / math.sqrt(length)).astype(np.float32).astype(ml_dtypes.bfloat16)


def twiddles(parts, span):
    b = np.arange(parts)[:, None]
    angle = b * np.arange(span)[None, :] * (2.0 * math.pi / (parts * span))
    return np.concatenate([np.cos(angle), np.sin(angle)], axis=0).astype(np.float32)


def add(a, b):
    return (a[0] + b[0], a[1] + b[1])


def sub(a, b):
    return (a[0] - b[0], a[1] - b[1])


def minus_i(a):
    return (a[1], -a[0])


def dft4(x0, x1, x2, x3):
    t0, t1, t2, t3 = add(x0, x2), sub(x0, x2), add(x1, x3), sub(x1, x3)
    r = minus_i(t3)
    return add(t0, t2), add(t1, r), sub(t0, t2), sub(t1, r)


def dft8(x):
    e = dft4(x[0], x[2], x[4], x[6])
    o = dft4(x[1], x[3], x[5], x[7])
    h = math.sqrt(0.5)
    o1 = (h * (o[1][0] + o[1][1]), h * (o[1][1] - o[1][0]))
    o2 = minus_i(o[2])
    o3 = (h * (o[3][1] - o[3][0]), -h * (o[3][0] + o[3][1]))
    o = (o[0], o1, o2, o3)
    return [add(e[k], o[k]) for k in range(4)] + [sub(e[k], o[k]) for k in range(4)]


def radix_step(rec, tw, t_ref, parts, pairs, span):
    groups = pairs // 16
    count = 2 * parts * pairs

    row = lax.broadcasted_iota(jnp.int32, (16, 128), 0)
    for u in range(span // 128):
        lanes = pl.ds(u * 128, 128)
        lanes_im = pl.ds(span + u * 128, 128)
        extra = [jnp.zeros((16, 128), f32), jnp.zeros((16, 128), f32)]
        for g in range(groups):
            x = []
            for s in range(parts):
                re = rec[s, g * 16:g * 16 + 16, lanes].astype(f32)
                im = rec[s, pairs + g * 16:pairs + g * 16 + 16, lanes].astype(f32)
                x.append((re, -im))
            y = dft8(x)
            for b in range(parts):
                c, s = tw[b:b + 1, lanes], tw[parts + b:parts + b + 1, lanes]
                conj = y[(parts - b) % parts]
                for kind, (zr, zi) in enumerate((y[b], (conj[0], -conj[1]))):
                    tr = c * zr + s * zi
                    ti = c * zi - s * zr
                    base = (kind * parts + b) * pairs + g * 16
                    t_ref[base:base + 16, lanes] = tr.astype(bf16)
                    t_ref[base:base + 16, lanes_im] = ti.astype(bf16)
                    if g == 0:
                        hit = row == kind * parts + b
                        extra[0] = jnp.where(hit, jnp.broadcast_to(-ti[0:1], (16, 128)), extra[0])
                        extra[1] = jnp.where(hit, jnp.broadcast_to(tr[0:1], (16, 128)), extra[1])
        t_ref[count:count + 16, lanes] = extra[0].astype(bf16)
        t_ref[count:count + 16, lanes_im] = extra[1].astype(bf16)


def spread_step(o_ref, put, me, parts, pairs, u, half):
    count = 2 * parts * pairs
    lanes = pl.ds((u - half * parts // 4) * 128, 128)
    low = lax.broadcasted_iota(jnp.int32, (16, 128), 1) < 64
    row = lax.broadcasted_iota(jnp.int32, (16, 128), 0)
    special = (row == 0) & (jnp.zeros((16, 128), jnp.int32) + me == 0)
    extra = o_ref[count:count + 16, lanes]
    for p in range(parts // 2):
        for g in range(pairs // 16):
            v = [[None, None], [None, None]]
            for kind in range(2):
                for h in range(2):
                    base = (kind * parts + 2 * p + h) * pairs + g * 16
                    v[kind][h] = o_ref[base:base + 16, lanes]
            if g == 0:
                for h in range(2):
                    b = 2 * p + h
                    even = 0.5 * (v[0][h] + v[1][h])
                    odd = jnp.broadcast_to(0.5 * (extra[b:b + 1] - extra[parts + b:parts + b + 1]), (16, 128))
                    v[0][h] = jnp.where(special, even, v[0][h])
                    v[1][h] = jnp.where(special, odd, v[1][h])
            for kind in range(2):
                v0, v1 = v[kind]
                rows = pl.ds(kind * pairs + g * 16, 16)
                cols = pl.ds(p * 128, 128)
                put(2 * u, rows, cols, jnp.where(low, v0, pltpu.roll(v1, 64, 1)).astype(bf16))
                put(2 * u + 1, rows, cols, jnp.where(low, pltpu.roll(v0, 64, 1), v1).astype(bf16))


def fold(v):
    total = v[0:8]
    for k in range(8, v.shape[0], 8):
        total = total + v[k:k + 8]
    return total


def rows_of(ref, at):
    return jnp.concatenate([ref[c, at, :] for c in range(ref.shape[0])], axis=1)


def set_rows(ref, at, value):
    for c in range(ref.shape[0]):
        ref[c, at, :] = value[:, c * 128:(c + 1) * 128]


def mean_of(v):
    return jnp.mean(v, axis=-1, keepdims=True)


def gelu_pair(x):
    k = math.sqrt(2.0 / math.pi)
    c = 0.044715
    x2 = x * x
    half = 0.5 + 0.5 * jnp.tanh(x * (k + (k * c) * x2))
    value = x * half
    slope = half + value * (1.0 - half) * (2.0 * k + (6.0 * k * c) * x2)
    return value, slope


def ffn_hidden(x_get, nbuf, sbuf, alow, hid, slope, weight, vec, bias_in, rows_step):
    for r in range(0, nbuf.shape[1], rows_step):
        at = pl.ds(r, rows_step)
        v = x_get(at).astype(f32) + rows_of(nbuf, at)
        center = v - mean_of(v)
        inv = lax.rsqrt(mean_of(center * center) + epsilon)
        n = center * inv
        set_rows(nbuf, at, n)
        sbuf[at, :] = jnp.broadcast_to(inv, (rows_step, 128))
        alow[at, :] = (n * vec[0:1] + vec[1:2]).astype(bf16)
    for c in range(hid.shape[0]):
        value, back = gelu_pair(dot_nt(alow[...], weight(0, c)) + bias_in[c])
        hid[c] = value.astype(bf16)
        slope[c] = back.astype(bf16)


def ffn_branch(hid, acc, weight):
    steps = hid.shape[0]
    every = jnp.concatenate([hid[c] for c in range(steps)], axis=1)
    acc[...] = dot_nn(every, weight(1, 0, steps))


def ffn_middle(nbuf, acc, glow, cot, outv, vec, sums, rows_step):
    for r in range(0, nbuf.shape[1], rows_step):
        at = pl.ds(r, rows_step)
        v = rows_of(nbuf, at) * vec[0:1] + vec[1:2] + (acc[at, :] + vec[4:5])
        center = v - mean_of(v)
        inv = lax.rsqrt(mean_of(center * center) + epsilon)
        n = center * inv
        outv[at, :] = (n * vec[2:3] + vec[3:4]).astype(bf16)
        g = cot[at, :].astype(f32)
        q = g * vec[2:3]
        gr = inv * (q - mean_of(q) - n * mean_of(q * n))
        acc[at, :] = gr
        low = gr.astype(bf16)
        glow[at, :] = low
        sums[2] += fold(g * n)
        sums[3] += fold(g)
        sums[4] += fold(low.astype(f32))


def ffn_backward(nbuf, sbuf, hid, slope, acc, glow, weight, bsum, vec, sums, rows_step, put):
    for c in range(hid.shape[0]):
        gh = dot_nt(glow[...], weight(1, c))
        gpre = (gh * slope[c].astype(f32)).astype(bf16)
        slope[c] = gpre
        bsum[c] += fold(gpre.astype(f32))
        acc[...] += dot_nn(gpre, weight(0, c))
    for r in range(0, nbuf.shape[1], rows_step):
        at = pl.ds(r, rows_step)
        ga = acc[at, :]
        n = rows_of(nbuf, at)
        sums[0] += fold(ga * n)
        sums[1] += fold(ga)
        q = ga * vec[0:1]
        put(at, sbuf[at, 0:1] * (q - mean_of(q) - n * mean_of(q * n)))


def ffn_grads(alow, hid, slope, glow, dw):
    chunk = hid.shape[2]
    for c in range(hid.shape[0]):
        at = pl.ds(c * chunk, chunk)
        dw[1, at, :] += dot_tn(hid[c], glow[...])
        dw[0, at, :] += dot_tn(slope[c], alow[...])


def layer_kernel(geo, tok, cot, win_own, wout_own, hp_all, wd_all, cp_all, tw, b_in, *rest):
    vec_own = rest[:5]
    (out, gtok, grow, dwin_own, dwout_own, small,
                 tokv, cotv, outv, w0, w1, hp, wd, cp, dw, send1, recv1, send2, recv2, t_ref, o_ref,
                 nbuf, sbuf, alow, hid, slope, acc, glow, sums, bsum, rz, rze, rzl, sv, rv, va, ra, vec, bias_in,
                 ss1, rs1, ss2, rs2, free1, free2, load, io,
                 s_core, r_core, s_first, r_first, s_next, r_next, s_z, r_z, s_vec, r_vec, ready,
                 s_spread, r_spread, s_relay, r_relay, s_pair, r_pair, s_early, r_early, s_late, r_late, s_va, r_va) = rest[5:]
    parts, pairs, span, width, jobs, slots, chunk, rows_step, planes = geo
    shard = dw.shape[1] // (parts * planes)
    me = lax.axis_index("seq")
    plane = lax.axis_index("batch")

    def peer(d):
        return lax.rem(me + d, parts)

    def load_of(k):
        if k < jobs:
            return pltpu.make_async_copy(tok.at[k], tokv.at[k], load.at[k])
        a, b = ((hp_all, hp), (wd_all, wd), (cp_all, cp))[k - jobs]
        return pltpu.make_async_copy(a, b, load.at[k])

    for k in (jobs, 0, 1, jobs + 1, 2, 3, jobs + 2):
        load_of(k).start()

    core, quad = lax.rem(me, 2), me // 2
    quads = parts // 2
    x, y = lax.rem(quad, 2), quad // 2
    partner = (me + 1 - 2 * core, plane)
    x_peer = (me + 2 - 4 * x, plane)
    y_peer = (me + 4 - 8 * y, plane)
    quad_x, quad_y = quad + 1 - 2 * x, quad + 2 - 4 * y
    last = planes - 1

    def send(src, dst, s, r, to):
        return pltpu.make_async_remote_copy(
            src_ref=src, dst_ref=dst, send_sem=s, recv_sem=r, device_id=to, device_id_type=MESH)

    own_loads = (
        pltpu.make_async_copy(win_own, w0.at[quad, core, plane], load.at[jobs + 3]),
        pltpu.make_async_copy(wout_own, w1.at[quad, core, plane], load.at[jobs + 4]),
    )
    for copy in own_loads:
        copy.start()

    owner = me * planes + plane
    part = width // (parts * planes)
    per_row = width // shard
    bias_row = 5 + owner // per_row
    row16 = lax.broadcasted_iota(jnp.int32, (16, width), 0)
    is_bias = row16 == jnp.zeros((16, width), jnp.int32) + bias_row
    sv[0] = jnp.zeros_like(sv[0])
    for j in range(5):
        sv[0, j:j + 1, 0:part] = vec_own[j][...].astype(f32)
    sv[0, 8:9, 0:shard] = b_in[...].astype(f32)
    rows8 = pltpu.roll(sv[0, 0:8], owner * part, 1)
    bias8 = pltpu.roll(sv[0, 8:16], lax.rem(owner, per_row) * shard, 1)
    placed = jnp.concatenate([rows8, jnp.zeros((8, width), f32)], axis=0)
    placed = jnp.where(is_bias, jnp.broadcast_to(bias8[0:1], (16, width)), placed)
    va[0] = placed.astype(bf16)

    barrier = pltpu.get_barrier_semaphore()

    def greet(d, carry):
        pl.semaphore_signal(barrier, inc=1, device_id=(peer(d), plane), device_id_type=MESH)
        return carry

    def greet_z(d, carry):
        pl.semaphore_signal(barrier, inc=1, device_id=(me, lax.rem(plane + d, planes)), device_id_type=MESH)
        return carry

    lax.fori_loop(1, parts, greet, 0)
    lax.fori_loop(1, planes, greet_z, 0)
    pl.semaphore_wait(barrier, parts - 1 + planes - 1)

    def remote(send, recv, ss, rs, k, d):
        p = peer(d)
        return pltpu.make_async_remote_copy(
            src_ref=send.at[lax.rem(k, 2), p], dst_ref=recv.at[lax.rem(k, slots), me],
            send_sem=ss.at[lax.rem(k, 2), d], recv_sem=rs.at[lax.rem(k, slots), d],
            device_id=(p, plane), device_id_type=MESH)

    def wait_sends(send, recv, ss, rs, k):
        def one(d, carry):
            remote(send, recv, ss, rs, k, d).wait_send()
            return carry

        lax.fori_loop(1, parts, one, 0)

    def wait_recvs(send, recv, ss, rs, k):
        def one(d, carry):
            source = lax.rem(me + parts - d, parts)
            slot = lax.rem(k, slots)
            pltpu.make_async_remote_copy(
                src_ref=send.at[0, 0], dst_ref=recv.at[slot, source],
                send_sem=ss.at[0, d], recv_sem=rs.at[slot, d],
                device_id=(source, plane), device_id_type=MESH).wait_recv()
            return carry

        lax.fori_loop(1, parts, one, 0)

    def tell(sem, k):
        def one(d, carry):
            pl.semaphore_signal(sem.at[lax.rem(k, slots)], inc=1, device_id=(peer(d), plane), device_id_type=MESH)
            return carry

        lax.fori_loop(1, parts, one, 0)

    def in_plane(d):
        return 2 * lax.rem(quad + d, quads) + core

    def along(d):
        return lax.rem(plane + d, planes)

    def spread_z(d):
        block = w0.at[quad, core, plane]
        return send(block, block, s_spread.at[0, d], r_spread.at[0, d], (me, along(d)))

    def spread_out(d):
        block = w1.at[quad, core, plane]
        return send(block, block, s_spread.at[1, d], r_spread.at[1, d], (in_plane(d), plane))

    def spread_in(n):
        block = w0.at[quad, core]
        return send(block, block, s_spread.at[2, n], r_spread.at[2, n], (x_peer, y_peer)[n])

    def pass_in(n):
        block = w0.at[(quad_x, quad_y)[n], core, pl.ds(n * planes // 2, planes // 2)]
        return send(block, block, s_spread.at[2, 2 + n], r_spread.at[2, 2 + n], (y_peer, x_peer)[n])

    def relay(origin, up):
        block = w1.at[:, core, origin]
        return send(block, block, s_relay.at[up, origin], r_relay.at[origin], (me, plane + 2 * up - 1))

    def pair_in(q):
        block = w0.at[q, core]
        return send(block, block, s_pair.at[0, q], r_pair.at[0, q], partner)

    def pair_out(origin):
        block = w1.at[:, core, origin]
        return send(block, block, s_pair.at[1, origin], r_pair.at[1, origin], partner)

    def relay_step(j):
        below, above = plane - 1 - j, plane + 1 + j

        @pl.when(below >= 0)
        def _():
            relay(below, 1).wait_recv()

            @pl.when(plane < last)
            def _():
                relay(below, 1).start()

            pair_out(below).start()

        @pl.when(above <= last)
        def _():
            relay(above, 0).wait_recv()

            @pl.when(plane > 0)
            def _():
                relay(above, 0).start()

            pair_out(above).start()

    def vec_spread(k):
        to = (partner, x_peer, y_peer)[k] if k < 3 else (me, along(k - 2))
        return send(va.at[min(k, 3)], ra.at[k], s_va.at[k], r_va.at[k], to)

    def vec_gather(k):
        if k > 0:
            vec_spread(k - 1).wait_recv()
            va[k] = (va[k - 1].astype(f32) + ra[k - 1].astype(f32)).astype(bf16)
        for j in ((k,) if k < 3 else range(3, 2 + planes)):
            vec_spread(j).start()

    def gather_start():
        for copy in own_loads:
            copy.wait()
        for d in range(1, planes):
            spread_z(d).start()
        for d in range(1, quads):
            spread_out(d).start()

    def gather_out():
        for d in range(1, quads):
            spread_out(d).wait_recv()

        @pl.when(plane < last)
        def _():
            relay(plane, 1).start()

        @pl.when(plane > 0)
        def _():
            relay(plane, 0).start()

        pair_out(plane).start()

    def gather_in():
        for d in range(1, planes):
            spread_z(d).wait_recv()
        for n in range(2):
            spread_in(n).start()
        pair_in(quad).start()

    def gather_pass():
        for n in range(2):
            spread_in(n).wait_recv()
        for n in range(2):
            pass_in(n).start()
        pair_in(quad_x).start()
        pair_in(quad_y).start()

    def gather_diagonal():
        for n in range(2):
            pass_in(n).wait_recv()
        pair_in(quads - 1 - quad).start()

    def gather_end_out():
        for origin in range(planes):
            pair_out(origin).wait_recv()

    def gather_end_in():
        for q in range(quads):
            pair_in(q).wait_recv()

        total = va[3].astype(f32)
        for k in range(3, 2 + planes):
            vec_spread(k).wait_recv()
            total = total + ra[k].astype(f32)
        vec[...] = total[0:8]
        for f in range(0, bsum.shape[0] * chunk, width):
            bias_in[f // chunk, 0:1, f % chunk:f % chunk + width] = total[5 + f // width:6 + f // width]

    def gather_sent():
        for k in range(2 + planes):
            vec_spread(k).wait_send()
        for d in range(1, planes):
            spread_z(d).wait_send()
        for d in range(1, quads):
            spread_out(d).wait_send()
        for n in range(2):
            spread_in(n).wait_send()
            pass_in(n).wait_send()
        for q in range(quads):
            pair_in(q).wait_send()
        for origin in range(planes):
            pair_out(origin).wait_send()

            @pl.when((plane < last) & (origin <= plane))
            def _():
                relay(origin, 1).wait_send()

            @pl.when((plane > 0) & (origin >= plane))
            def _():
                relay(origin, 0).wait_send()

    def weight(m, c, count=1):
        n = chunk // (2 * planes * shard)
        at = pl.ds(c * n, count * n)
        block = w0[at] if m == 0 else w1[at]
        return block.reshape(count * chunk, width)

    def told(sem, k):
        pl.semaphore_wait(sem.at[lax.rem(k, slots)], parts - 1)

    one_way = (send1, recv1, ss1, rs1)
    way_back = (send2, recv2, ss2, rs2)

    def hidden_job(k):
        @pl.when(k >= 2)
        def _():
            wait_sends(*one_way, k - 2)

        @pl.when(k >= slots)
        def _():
            told(free1, k)

        table = dot_nt(hp[...], tokv[lax.rem(k, jobs)]).astype(bf16)
        send1[lax.rem(k, 2)] = table.reshape(parts, 2 * pairs, span)
        recv1[lax.rem(k, slots), me] = send1[lax.rem(k, 2), me]

        def one(d, carry):
            remote(*one_way, k, d).start()
            return carry

        lax.fori_loop(1, parts, one, 0)

    def sequence_job(k, carry):
        wait_recvs(*one_way, k)
        radix_step(recv1.at[lax.rem(k, slots)], tw, t_ref, parts, pairs, span)

        @pl.when(k < 2 * jobs - slots)
        def _():
            tell(free1, k)

        @pl.when(k >= 2)
        def _():
            wait_sends(*way_back, k - 2)

        @pl.when(k >= slots)
        def _():
            told(free2, k)

        slot = lax.rem(k, 2)
        half = span // 2

        def put(p, rows, cols, value):
            send2[slot, p, rows, cols] = value

        for base in range(2):
            o_ref[...] = dot_nn(t_ref[...], wd[:, base * half:(base + 1) * half])
            for u in range(base * parts // 4, (base + 1) * parts // 4):
                spread_step(o_ref, put, me, parts, pairs, u, base)
        recv2[lax.rem(k, slots), me] = send2[slot, me]

        def one(d, carry):
            remote(*way_back, k, d).start()
            return carry

        lax.fori_loop(1, parts, one, 0)
        return carry

    def mixed_job(k):
        wait_recvs(*way_back, k)
        blocks = recv2[lax.rem(k, slots)].reshape(width, span)
        natural = dot_tn(blocks, cp[...])
        step = span // parts
        for b in range(parts):
            for c in range(width // 128):
                nbuf[c, pl.ds(b, step, stride=parts), :] = natural[b * step:(b + 1) * step, c * 128:(c + 1) * 128]

    vec_gather(0)
    gather_start()
    vec_gather(1)
    load_of(jobs).wait()
    load_of(0).wait()
    hidden_job(0)
    dw[...] = jnp.zeros_like(dw)
    sums[...] = jnp.zeros_like(sums)
    bsum[...] = jnp.zeros_like(bsum)
    gather_out()
    vec_gather(2)
    gather_in()
    for k in (1, 2, 3, jobs + 1, jobs + 2):
        load_of(k).wait()

    sequence_job(0, 0)
    vec_gather(3)
    relay_step(0)
    gather_pass()
    hidden_job(1)
    relay_step(1)
    hidden_job(2)
    gather_diagonal()
    hidden_job(3)
    gather_end_in()

    def out_copy(i):
        return pltpu.make_async_copy(outv, out.at[i], io.at[0])

    def cot_copy(i):
        return pltpu.make_async_copy(cot.at[i], cotv, io.at[1])

    def row_copy(i):
        return pltpu.make_async_copy(acc, grow.at[i], io.at[2])

    def main(i, carry):
        cot_copy(i).start()
        mixed_job(i)
        tell(free2, i)
        ffn_hidden(lambda at: tokv[i, at, :], nbuf, sbuf, alow, hid, slope, weight, vec, bias_in, rows_step)
        lax.fori_loop(i + 1 + i // 3, i + 2 + i // 2 + i // 3, sequence_job, 0)

        @pl.when(i == 0)
        def _():
            relay_step(2)
            gather_end_out()

        ffn_branch(hid, acc, weight)
        cot_copy(i).wait()

        @pl.when(i > 0)
        def _():
            out_copy(i - 1).wait()

        ffn_middle(nbuf, acc, glow, cotv, outv, vec, sums, rows_step)
        out_copy(i).start()

        def put(at, value):
            acc[at, :] = value
            tokv[i, at, :] = value.astype(bf16)

        ffn_backward(nbuf, sbuf, hid, slope, acc, glow, weight, bsum, vec, sums, rows_step, put)
        row_copy(i).start()
        hidden_job(i + jobs)
        ffn_grads(alow, hid, slope, glow, dw)
        row_copy(i).wait()
        return carry

    lax.fori_loop(0, jobs, main, 0)

    rest_rows = 16
    most = shard - rest_rows

    def rows_at(start, count=shard):
        return pl.ds(pl.multiple_of(start, shard), count)

    def target(v):
        return lax.rem(plane + 1 + v, planes)

    def owned(q, c, v):
        return rows_at(((2 * q + c) * planes + target(v)) * shard)

    head = pl.ds(0, most)

    def core_copy(v):
        return send(w1.at[v], w0.at[v], s_core.at[v], r_core.at[v], partner)

    def first_copy(v, m):
        at = pl.ds(2 * m, 2)
        return send(w1.at[2 + v // 2, lax.rem(v, 2), at, head], w1.at[v // 2, lax.rem(v, 2), at, head],
                    s_first.at[v, m], r_first.at[v, m], (x_peer, y_peer)[m])

    def next_copy(v, m):
        return send(w0.at[0, v // 2, 2 * lax.rem(v, 2) + m, head],
                    (alow, glow)[m].at[pl.ds(pl.multiple_of(v * most, most), most)],
                    s_next.at[v, m], r_next.at[v, m], (y_peer, x_peer)[m])

    def z_copy(v):
        return send(w0.at[1, v // 2, pl.ds(2 * lax.rem(v, 2), 2), head], rz.at[v],
                    s_z.at[v], r_z.at[v], (me, target(v)))

    def early_copy(v):
        return send(hid.at[v, pl.ds(0, 2 * quads * rest_rows)], rze.at[v], s_early.at[v], r_early.at[v], (me, target(v)))

    def late_copy(d):
        q = lax.rem(quad + d, quads)
        return send(hid.at[last, pl.ds(pl.multiple_of(2 * q * rest_rows, 2 * rest_rows), 2 * rest_rows)], rzl.at[d - 1],
                    s_late.at[d - 1], r_late.at[d - 1], (in_plane(d), plane))

    def vec_copy(k):
        to = (partner, x_peer, y_peer)[k] if k < 3 else (me, target(k - 3))
        return send(sv.at[min(k, 3)], rv.at[k], s_vec.at[k], r_vec.at[k], to)

    def core_step(v, carry):
        for q in range(quads):
            for m in range(2):
                w1[v, q // 2, 2 * (q % 2) + m] = dw[m, owned(q, 1 - core, v)].astype(bf16)
        core_copy(v).start()
        return carry

    def owned_most(q, v):
        return rows_at(((2 * q + core) * planes + target(v)) * shard, most)

    def owned_rest(q, v):
        return pl.ds(pl.multiple_of(((2 * q + core) * planes + target(v)) * shard + most, 16), rest_rows)

    def first_step(v, carry):
        core_copy(v).wait_recv()
        for q in range(quads):
            for m in range(2):
                at = owned(q, core, v)
                dw[m, at] += w0[v, q // 2, 2 * (q % 2) + m].astype(f32)

        @pl.when(v < last)
        def _():
            for q in range(quads):
                for m in range(2):
                    at = pl.ds((2 * q + m) * rest_rows, rest_rows)
                    hid[v, at, :] = dw[m, owned_rest(q, v)].astype(bf16)
            early_copy(v).start()

        for k in range(2):
            for m in range(2):
                q = 2 * k + 1 - x if m == 0 else 2 * (1 - y) + k
                w1[2 + v // 2, lax.rem(v, 2), 2 * m + k, 0:most, :] = dw[m, owned_most(q, v)].astype(bf16)
        for m in range(2):
            first_copy(v, m).start()
        return carry

    def next_step(v, carry):
        for m in range(2):
            first_copy(v, m).wait_recv()
        for k in range(2):
            for m in range(2):
                q = 2 * k + x if m == 0 else 2 * y + k
                dw[m, owned_most(q, v)] += w1[v // 2, lax.rem(v, 2), 2 * m + k, 0:most, :].astype(f32)
        for m in range(2):
            q = 2 * (1 - y) + x if m == 0 else 2 * y + 1 - x
            w0[0, v // 2, 2 * lax.rem(v, 2) + m, 0:most, :] = dw[m, owned_most(q, v)].astype(bf16)
            next_copy(v, m).start()
        return carry

    def z_step(v, carry):
        for m in range(2):
            next_copy(v, m).wait_recv()
            dw[m, owned_most(quad, v)] += (alow, glow)[m][pl.ds(pl.multiple_of(v * most, most), most)].astype(f32)

        @pl.when(v < last)
        def _():
            for m in range(2):
                w0[1, v // 2, 2 * lax.rem(v, 2) + m, 0:most, :] = dw[m, owned_most(quad, v)].astype(bf16)
            z_copy(v).start()

        return carry

    def late_step():
        for v in range(last):
            early_copy(v).wait_recv()
        for q in range(quads):
            for m in range(2):
                at = owned_rest(q, last)
                total = dw[m, at]
                for v in range(last):
                    total = total + rze[v, (2 * q + m) * rest_rows:(2 * q + m + 1) * rest_rows].astype(f32)
                dw[m, at] = total
                hid[last, (2 * q + m) * rest_rows:(2 * q + m + 1) * rest_rows, :] = total.astype(bf16)
        for d in range(1, quads):
            late_copy(d).start()

    def vec_step(k):
        if k == 0:
            sv[0] = jnp.zeros_like(sv[0])
            for j in range(5):
                sv[0, j:j + 1] = jnp.sum(sums[j], axis=0, keepdims=True)
            piece = math.gcd(width, chunk)
            for f in range(0, bsum.shape[0] * chunk, piece):
                sv[0, 5 + f // width:6 + f // width, f % width:f % width + piece] = jnp.sum(
                    bsum[f // chunk, :, f % chunk:f % chunk + piece], axis=0, keepdims=True)
        else:
            vec_copy(k - 1).wait_recv()
            sv[k] = sv[k - 1] + rv[k - 1]
        for j in ((k,) if k < 3 else range(3, 2 + planes)):
            vec_copy(j).start()

    def gt_copy(i):
        return pltpu.make_async_copy(tokv.at[i], gtok.at[i], io.at[4 + i])

    def final(i, carry):
        back = pltpu.make_async_copy(grow.at[i], acc, io.at[2])
        back.start()
        mixed_job(i + jobs)
        back.wait()
        for c in range(width // 128):
            tokv[i, :, c * 128:(c + 1) * 128] = (nbuf[c] + acc[:, c * 128:(c + 1) * 128]).astype(bf16)
        gt_copy(i).start()
        return carry

    gather_sent()
    pl.semaphore_signal(ready.at[0], inc=1, device_id=partner, device_id_type=MESH)
    pl.semaphore_wait(ready.at[0], 1)
    lax.fori_loop(0, planes, core_step, 0)
    vec_step(0)

    def core_sent(v, carry):
        core_copy(v).wait_send()
        return carry

    lax.fori_loop(0, planes, core_sent, 0)
    pl.semaphore_signal(ready.at[1], inc=1, device_id=x_peer, device_id_type=MESH)
    pl.semaphore_signal(ready.at[2], inc=1, device_id=y_peer, device_id_type=MESH)
    vec_step(1)
    pl.semaphore_wait(ready.at[1], 1)
    pl.semaphore_wait(ready.at[2], 1)
    lax.fori_loop(0, planes, first_step, 0)
    final(0, 0)
    tell(free2, jobs)
    vec_step(2)
    lax.fori_loop(0, planes // 2, next_step, 0)
    sequence_job(2 * jobs - 1, 0)
    final(1, 0)
    lax.fori_loop(planes // 2, planes, next_step, 0)
    vec_step(3)
    final(2, 0)
    lax.fori_loop(0, planes, z_step, 0)
    late_step()
    final(3, 0)
    own_most, own_rest = owned_most(quad, last), owned_rest(quad, last)
    for v in range(last):
        z_copy(v).wait_recv()
    for d in range(1, quads):
        late_copy(d).wait_recv()
    for m in range(2):
        total = dw[m, own_most]
        for v in range(last):
            total = total + rz[v, m].astype(f32)
        (dwin_own, dwout_own)[m][0:most] = total
        total = dw[m, own_rest]
        for d in range(1, quads):
            total = total + rzl[d - 1, m * rest_rows:(m + 1) * rest_rows].astype(f32)
        (dwin_own, dwout_own)[m][most:shard] = total
    total = sv[3]
    for k in range(3, 2 + planes):
        vec_copy(k).wait_recv()
        total = total + rv[k]
    mine = jnp.sum(jnp.where(is_bias, total, 0.0), axis=0, keepdims=True)
    mine = pltpu.roll(jnp.broadcast_to(mine, (8, width)), width - lax.rem(owner, per_row) * shard, 1)
    rows8 = pltpu.roll(total[0:8], width - owner * part, 1)
    row8 = lax.broadcasted_iota(jnp.int32, (8, 128), 0)
    small[...] = jnp.where(row8 == 5, mine[:, 0:128], rows8[:, 0:128])

    def sent(v, carry):
        for m in range(2):
            first_copy(v, m).wait_send()
            next_copy(v, m).wait_send()
        return carry

    lax.fori_loop(0, planes, sent, 0)
    for k in range(2 * jobs - 2, 2 * jobs):
        wait_sends(*way_back, k)
        wait_sends(*one_way, k)
    for v in range(last):
        z_copy(v).wait_send()
        early_copy(v).wait_send()
    for d in range(1, quads):
        late_copy(d).wait_send()
    for k in range(2 + planes):
        vec_copy(k).wait_send()
    out_copy(jobs - 1).wait()
    for i in range(jobs):
        gt_copy(i).wait()


def layer_call(tok, cot, win_own, wout_own, b_in, vectors, parts, planes):
    jobs, span, width = tok.shape
    shard = wout_own.shape[0]
    ff = shard * parts * planes
    pairs = width // 2 // parts
    chunk, rows_step = ff // (parts // 2), span // 4
    steps = ff // chunk
    length = span * parts
    slots = 3
    geo = (parts, pairs, span, width, jobs, slots, chunk, rows_step, planes)
    tables = (
        jnp.asarray(packed_hidden(width, parts)),
        jnp.asarray(inner_table(span, length)),
        jnp.asarray(column_order(width, parts)),
        jnp.asarray(twiddles(parts, span)),
    )
    hbm, vmem, dma = pl.BlockSpec(memory_space=pl.ANY), pl.BlockSpec(memory_space=pltpu.VMEM), pltpu.SemaphoreType.DMA
    block = (parts, 2 * pairs, span)
    scratch = [
        pltpu.VMEM((jobs, span, width), bf16),
        pltpu.VMEM((span, width), bf16),
        pltpu.VMEM((span, width), bf16),
        pltpu.VMEM((parts // 2, 2, planes, shard, width), bf16),
        pltpu.VMEM((parts // 2, 2, planes, shard, width), bf16),
        pltpu.VMEM((width, width), bf16),
        pltpu.VMEM((2 * span, span), bf16),
        pltpu.VMEM((width, width), bf16),
        pltpu.VMEM((2, ff, width), f32),
        pltpu.VMEM((2,) + block, bf16),
        pltpu.VMEM((slots,) + block, bf16),
        pltpu.VMEM((2,) + block, bf16),
        pltpu.VMEM((slots,) + block, bf16),
        pltpu.VMEM((2 * parts * pairs + 16, 2 * span), bf16),
        pltpu.VMEM((2 * parts * pairs + 16, span // 2), f32),
        pltpu.VMEM((width // 128, span, 128), f32),
        pltpu.VMEM((span, 128), f32),
        pltpu.VMEM((span, width), bf16),
        pltpu.VMEM((steps, span, chunk), bf16),
        pltpu.VMEM((steps, span, chunk), bf16),
        pltpu.VMEM((span, width), f32),
        pltpu.VMEM((span, width), bf16),
        pltpu.VMEM((5, 8, width), f32),
        pltpu.VMEM((steps, 8, chunk), f32),
        pltpu.VMEM((planes - 1, 2, shard - 16, width), bf16),
        pltpu.VMEM((planes - 1, parts * 16, width), bf16),
        pltpu.VMEM((parts // 2 - 1, 2 * 16, width), bf16),
        pltpu.VMEM((4, 16, width), f32),
        pltpu.VMEM((2 + planes, 16, width), f32),
        pltpu.VMEM((4, 16, width), bf16),
        pltpu.VMEM((2 + planes, 16, width), bf16),
        pltpu.VMEM((8, width), f32),
        pltpu.VMEM((steps, 1, chunk), f32),
        dma((2, parts)), dma((slots, parts)), dma((2, parts)), dma((slots, parts)),
        pltpu.SemaphoreType.REGULAR((slots,)), pltpu.SemaphoreType.REGULAR((slots,)),
        dma((jobs + 5,)), dma((4 + jobs,)),
        dma((planes,)), dma((planes,)), dma((planes, 2)), dma((planes, 2)), dma((planes, 2)), dma((planes, 2)),
        dma((planes - 1,)), dma((planes - 1,)), dma((2 + planes,)), dma((2 + planes,)),
        pltpu.SemaphoreType.REGULAR((3,)),
        dma((3, max(parts // 2, planes))), dma((3, max(parts // 2, planes))), dma((2, planes)), dma((planes,)),
        dma((2, max(parts // 2, planes))), dma((2, max(parts // 2, planes))),
        dma((planes - 1,)), dma((planes - 1,)), dma((parts // 2 - 1,)), dma((parts // 2 - 1,)),
        dma((2 + planes,)), dma((2 + planes,)),
    ]
    shape = jax.ShapeDtypeStruct
    return pl.pallas_call(
        partial(layer_kernel, geo),
        out_shape=(
            shape(tok.shape, bf16),
            shape(tok.shape, bf16),
            shape(tok.shape, f32),
            shape((shard, width), f32),
            shape((shard, width), f32),
            shape((8, 128), f32),
        ),
        in_specs=[hbm] * 7 + [vmem] * 7,
        out_specs=(hbm,) * 3 + (vmem,) * 3,
        scratch_shapes=scratch,
        compiler_params=pltpu.CompilerParams(
            collective_id=1, has_side_effects=True, vmem_limit_bytes=64 * 1024 * 1024 - 256 * 1024),
        name="encoder_layer",
    )(tok, cot, win_own, wout_own, *tables, b_in, *vectors)


def local_fast(tokens, w_in, b_in, w_out, b_out, gain_one, shift_one, gain_two, shift_two, cotangent):
    both = ("seq", "batch")
    parts = lax.axis_size("seq")
    width = tokens.shape[2]
    shard = w_in.shape[1]
    planes = lax.axis_size("batch")
    part = b_out.shape[0]
    vectors = [v.reshape(1, part) for v in (gain_one, shift_one, gain_two, shift_two, b_out)]
    out, gtok, _, dwin, dwout, small = layer_call(
        tokens, cotangent, w_in.T, w_out, b_in.reshape(1, shard), vectors, parts, planes)
    rest = small[:5, :part]
    return (out, gtok, dwin.T, small[5, :shard], dwout, rest[4], rest[0], rest[1], rest[2], rest[3])


def hidden_table(extent):
    idx_all = jnp.arange(extent, dtype=jnp.int32)
    angles = (idx_all[:, None] * idx_all[None, :] % extent).astype(jnp.float32) * (
        2.0 * math.pi / extent
    )
    factor = 1.0 / math.sqrt(extent)
    return jnp.concatenate([jnp.cos(angles) * factor, jnp.sin(angles) * factor], axis=1).astype(
        jnp.bfloat16
    )


def sequence_table(length):
    block_rows = min(512, length)
    block_count = length // block_rows
    col_ids = jnp.arange(length, dtype=jnp.int32)
    factor = 1.0 / math.sqrt(length)

    def table_rows(block_index):
        row_ids = block_index * block_rows + jnp.arange(block_rows, dtype=jnp.int32)
        angles = (row_ids[:, None] * col_ids[None, :] % length).astype(jnp.float32) * (
            2.0 * math.pi / length
        )
        return (jnp.stack([jnp.cos(angles), -jnp.sin(angles)]) * factor).astype(jnp.bfloat16)

    blocks = lax.map(table_rows, jnp.arange(block_count, dtype=jnp.int32))
    return jnp.moveaxis(blocks, 1, 0).reshape(2, length, length)


def normalize(values, gain, shift):
    center = values - jnp.mean(values, axis=-1, keepdims=True)
    inv_std = lax.rsqrt(jnp.mean(center * center, axis=-1, keepdims=True) + epsilon)
    normed = center * inv_std
    return (normed * gain + shift, normed, inv_std)


def norm_back(grad_out, normed, inv_std, gain):
    scaled = grad_out * gain
    centered = scaled - jnp.mean(scaled, axis=-1, keepdims=True)
    return inv_std * (centered - normed * jnp.mean(scaled * normed, axis=-1, keepdims=True))


def local(tokens, w_in, b_in, w_out, b_out, gain_one, shift_one, gain_two, shift_two, cotangent):
    batch_rows, seq_part, model_width = tokens.shape
    length = seq_part * lax.axis_size("seq")
    w_in_all, b_in_all, w_out_all, b_out_all, g_one_all, s_one_all, g_two_all, s_two_all = (
        lax.all_gather(w_in, ("seq", "batch"), axis=1, tiled=True),
        lax.all_gather(b_in, ("seq", "batch"), axis=0, tiled=True),
        lax.all_gather(w_out, ("seq", "batch"), axis=0, tiled=True),
        lax.all_gather(b_out, ("seq", "batch"), axis=0, tiled=True),
        lax.all_gather(gain_one, ("seq", "batch"), axis=0, tiled=True),
        lax.all_gather(shift_one, ("seq", "batch"), axis=0, tiled=True),
        lax.all_gather(gain_two, ("seq", "batch"), axis=0, tiled=True),
        lax.all_gather(shift_two, ("seq", "batch"), axis=0, tiled=True),
    )
    h_table = hidden_table(model_width)
    s_table = sequence_table(length)
    flat_tokens = tokens.reshape(-1, model_width)
    spectra = jnp.dot(flat_tokens, h_table, preferred_element_type=jnp.float32).astype(jnp.bfloat16)
    spectra = spectra.reshape(batch_rows, seq_part, 2, model_width)
    mixed_cols = jnp.einsum(
        "plm,bmpc->blc",
        s_table,
        lax.all_to_all(spectra, "seq", split_axis=3, concat_axis=1, tiled=True),
        preferred_element_type=jnp.float32,
    ).astype(jnp.bfloat16)
    mixed = lax.all_to_all(mixed_cols, "seq", split_axis=1, concat_axis=2, tiled=True)
    resid_one = flat_tokens.astype(jnp.float32) + mixed.reshape(-1, model_width).astype(jnp.float32)
    act_one, normed_one, inv_one = normalize(
        resid_one, g_one_all.astype(jnp.float32), s_one_all.astype(jnp.float32)
    )
    act_low = act_one.astype(jnp.bfloat16)
    pre_act = jnp.dot(act_low, w_in_all, preferred_element_type=jnp.float32) + b_in_all.astype(
        jnp.float32
    )
    activ, gelu_back = jax.vjp(partial(jax.nn.gelu, approximate=True), pre_act)
    hidden_low = activ.astype(jnp.bfloat16)
    branch = jnp.dot(hidden_low, w_out_all, preferred_element_type=jnp.float32) + b_out_all.astype(
        jnp.float32
    )
    resid_two = act_one + branch
    result, normed_two, inv_two = normalize(
        resid_two, g_two_all.astype(jnp.float32), s_two_all.astype(jnp.float32)
    )
    grad_out = cotangent.reshape(-1, model_width).astype(jnp.float32)
    grad_g_two = jnp.sum(grad_out * normed_two, axis=0)
    grad_s_two = jnp.sum(grad_out, axis=0)
    grad_r_two = norm_back(grad_out, normed_two, inv_two, g_two_all.astype(jnp.float32))
    grad_branch = grad_r_two.astype(jnp.bfloat16)
    grad_b_out = jnp.sum(grad_branch.astype(jnp.float32), axis=0)
    grad_w_out = jnp.einsum(
        "tf,td->fd", hidden_low, grad_branch, preferred_element_type=jnp.float32
    )
    grad_hidden = jnp.einsum(
        "td,fd->tf", grad_branch, w_out_all, preferred_element_type=jnp.float32
    )
    grad_pre = gelu_back(grad_hidden)[0].astype(jnp.bfloat16)
    grad_b_in = jnp.sum(grad_pre.astype(jnp.float32), axis=0)
    grad_w_in = jnp.einsum("td,tf->df", act_low, grad_pre, preferred_element_type=jnp.float32)
    grad_a_one = grad_r_two + jnp.einsum(
        "tf,df->td", grad_pre, w_in_all, preferred_element_type=jnp.float32
    )
    grad_g_one = jnp.sum(grad_a_one * normed_one, axis=0)
    grad_s_one = jnp.sum(grad_a_one, axis=0)
    grad_r_one = norm_back(grad_a_one, normed_one, inv_one, g_one_all.astype(jnp.float32))
    grad_mix = grad_r_one.astype(jnp.bfloat16).reshape(batch_rows, seq_part, model_width)
    spec_grad = jnp.einsum(
        "plm,blc->bmpc",
        s_table,
        lax.all_to_all(grad_mix, "seq", split_axis=2, concat_axis=1, tiled=True),
        preferred_element_type=jnp.float32,
    ).astype(jnp.bfloat16)
    grad_spec = lax.all_to_all(spec_grad, "seq", split_axis=1, concat_axis=3, tiled=True)
    grad_flat = grad_r_one + jnp.einsum(
        "te,de->td",
        grad_spec.reshape(-1, 2 * model_width),
        h_table,
        preferred_element_type=jnp.float32,
    )
    sum_w_in, sum_b_in, sum_w_out, sum_b_out, sum_g_one, sum_s_one, sum_g_two, sum_s_two = (
        lax.psum_scatter(grad_w_in, ("seq", "batch"), scatter_dimension=1, tiled=True),
        lax.psum_scatter(grad_b_in, ("seq", "batch"), scatter_dimension=0, tiled=True),
        lax.psum_scatter(grad_w_out, ("seq", "batch"), scatter_dimension=0, tiled=True),
        lax.psum_scatter(grad_b_out, ("seq", "batch"), scatter_dimension=0, tiled=True),
        lax.psum_scatter(grad_g_one, ("seq", "batch"), scatter_dimension=0, tiled=True),
        lax.psum_scatter(grad_s_one, ("seq", "batch"), scatter_dimension=0, tiled=True),
        lax.psum_scatter(grad_g_two, ("seq", "batch"), scatter_dimension=0, tiled=True),
        lax.psum_scatter(grad_s_two, ("seq", "batch"), scatter_dimension=0, tiled=True),
    )
    output = result.astype(jnp.bfloat16).reshape(batch_rows, seq_part, model_width)
    grad_tokens = grad_flat.astype(jnp.bfloat16).reshape(batch_rows, seq_part, model_width)
    return (
        output,
        grad_tokens,
        sum_w_in,
        sum_b_in,
        sum_w_out,
        sum_b_out,
        sum_g_one,
        sum_s_one,
        sum_g_two,
        sum_s_two,
    )


def solution(mesh):
    every = P(("seq", "batch"))

    def whole(tokens, w_in, *rest):
        parts = mesh.shape["seq"]
        fits = (
            parts == 8
            and tokens.shape[1] == 512 * parts
            and tokens.shape[2] % (32 * parts) == 0
            and w_in.shape[1] % (3 * 128) == 0
            and tokens.shape[0] == 4 * mesh.shape["batch"]
        )
        return jax.shard_map(
            local_fast if fits else local,
            mesh=mesh,
            in_specs=(
                P("batch", "seq", None),
                P(None, ("seq", "batch")),
                every,
                P(("seq", "batch"), None),
                every,
                every,
                every,
                every,
                every,
                P("batch", "seq", None),
            ),
            out_specs=(
                P("batch", "seq", None),
                P("batch", "seq", None),
                P(None, ("seq", "batch")),
                every,
                P(("seq", "batch"), None),
                every,
                every,
                every,
                every,
                every,
            ),
            check_vma=False,
        )(tokens, w_in, *rest)

    return whole
```

```python
from functools import partial
import math

import jax
import jax.numpy as jnp
import ml_dtypes
import numpy as np
from jax import lax
from jax.experimental import pallas as pl
from jax.experimental.pallas import tpu as pltpu
from jax.sharding import PartitionSpec as P

epsilon = 1e-05
f32, bf16 = jnp.float32, jnp.bfloat16
MESH = pl.DeviceIdType.MESH


def dot_nn(a, b):
    return lax.dot_general(a, b, (((1,), (0,)), ((), ())), preferred_element_type=f32)


def dot_nt(a, b):
    return lax.dot_general(a, b, (((1,), (1,)), ((), ())), preferred_element_type=f32)


def dot_tn(a, b):
    return lax.dot_general(a, b, (((0,), (0,)), ((), ())), preferred_element_type=f32)


def plan_columns(width, parts):
    pairs = width // 2 // parts
    r = np.arange(width)
    dev, kind, i = r // (2 * pairs), (r // pairs) % 2, r % pairs
    j = dev * pairs + i
    first = (kind == 1) & (j == 0)
    return j, kind, first


def packed_hidden(width, parts):
    j, kind, first = plan_columns(width, parts)
    k = np.arange(width)
    angle = (j[:, None] * k[None, :] % width) * (2.0 * math.pi / width)
    table = np.where(kind[:, None] == 0, np.cos(angle), np.sin(angle))
    nyquist = np.cos(np.pi * (k % 2))
    table = np.where(first[:, None], nyquist[None, :], table) / math.sqrt(width)
    return table.astype(np.float32).astype(ml_dtypes.bfloat16)


def column_order(width, parts):
    j, kind, first = plan_columns(width, parts)
    col = np.where(kind == 0, j, np.where(first, width // 2, (width - j) % width))
    return (col[:, None] == np.arange(width)[None, :]).astype(ml_dtypes.bfloat16)


def inner_table(span, length):
    a = np.arange(span)
    angle = (a[:, None] * a[None, :] % span) * (2.0 * math.pi / span)
    table = np.concatenate([np.cos(angle), np.sin(angle)], axis=0)
    return (table / math.sqrt(length)).astype(np.float32).astype(ml_dtypes.bfloat16)


def twiddles(parts, span):
    b = np.arange(parts)[:, None]
    angle = b * np.arange(span)[None, :] * (2.0 * math.pi / (parts * span))
    return np.concatenate([np.cos(angle), np.sin(angle)], axis=0).astype(np.float32)


def add(a, b):
    return (a[0] + b[0], a[1] + b[1])


def sub(a, b):
    return (a[0] - b[0], a[1] - b[1])


def minus_i(a):
    return (a[1], -a[0])


def dft4(x0, x1, x2, x3):
    t0, t1, t2, t3 = add(x0, x2), sub(x0, x2), add(x1, x3), sub(x1, x3)
    r = minus_i(t3)
    return add(t0, t2), add(t1, r), sub(t0, t2), sub(t1, r)


def dft8(x):
    e = dft4(x[0], x[2], x[4], x[6])
    o = dft4(x[1], x[3], x[5], x[7])
    h = math.sqrt(0.5)
    o1 = (h * (o[1][0] + o[1][1]), h * (o[1][1] - o[1][0]))
    o2 = minus_i(o[2])
    o3 = (h * (o[3][1] - o[3][0]), -h * (o[3][0] + o[3][1]))
    o = (o[0], o1, o2, o3)
    return [add(e[k], o[k]) for k in range(4)] + [sub(e[k], o[k]) for k in range(4)]


def radix_step(rec, tw, t_ref, parts, pairs, span):
    groups = pairs // 16
    count = 2 * parts * pairs

    row = lax.broadcasted_iota(jnp.int32, (16, 128), 0)
    for u in range(span // 128):
        lanes = pl.ds(u * 128, 128)
        lanes_im = pl.ds(span + u * 128, 128)
        extra = [jnp.zeros((16, 128), f32), jnp.zeros((16, 128), f32)]
        for g in range(groups):
            x = []
            for s in range(parts):
                re = rec[s, g * 16:g * 16 + 16, lanes].astype(f32)
                im = rec[s, pairs + g * 16:pairs + g * 16 + 16, lanes].astype(f32)
                x.append((re, -im))
            y = dft8(x)
            for b in range(parts):
                c, s = tw[b:b + 1, lanes], tw[parts + b:parts + b + 1, lanes]
                conj = y[(parts - b) % parts]
                for kind, (zr, zi) in enumerate((y[b], (conj[0], -conj[1]))):
                    tr = c * zr + s * zi
                    ti = c * zi - s * zr
                    base = (kind * parts + b) * pairs + g * 16
                    t_ref[base:base + 16, lanes] = tr.astype(bf16)
                    t_ref[base:base + 16, lanes_im] = ti.astype(bf16)
                    if g == 0:
                        hit = row == kind * parts + b
                        extra[0] = jnp.where(hit, jnp.broadcast_to(-ti[0:1], (16, 128)), extra[0])
                        extra[1] = jnp.where(hit, jnp.broadcast_to(tr[0:1], (16, 128)), extra[1])
        t_ref[count:count + 16, lanes] = extra[0].astype(bf16)
        t_ref[count:count + 16, lanes_im] = extra[1].astype(bf16)


def spread_step(o_ref, put, me, parts, pairs, u, half):
    count = 2 * parts * pairs
    lanes = pl.ds((u - half * parts // 4) * 128, 128)
    low = lax.broadcasted_iota(jnp.int32, (16, 128), 1) < 64
    row = lax.broadcasted_iota(jnp.int32, (16, 128), 0)
    special = (row == 0) & (jnp.zeros((16, 128), jnp.int32) + me == 0)
    extra = o_ref[count:count + 16, lanes]
    for p in range(parts // 2):
        for g in range(pairs // 16):
            v = [[None, None], [None, None]]
            for kind in range(2):
                for h in range(2):
                    base = (kind * parts + 2 * p + h) * pairs + g * 16
                    v[kind][h] = o_ref[base:base + 16, lanes]
            if g == 0:
                for h in range(2):
                    b = 2 * p + h
                    even = 0.5 * (v[0][h] + v[1][h])
                    odd = jnp.broadcast_to(0.5 * (extra[b:b + 1] - extra[parts + b:parts + b + 1]), (16, 128))
                    v[0][h] = jnp.where(special, even, v[0][h])
                    v[1][h] = jnp.where(special, odd, v[1][h])
            for kind in range(2):
                v0, v1 = v[kind]
                rows = pl.ds(kind * pairs + g * 16, 16)
                cols = pl.ds(p * 128, 128)
                put(2 * u, rows, cols, jnp.where(low, v0, pltpu.roll(v1, 64, 1)).astype(bf16))
                put(2 * u + 1, rows, cols, jnp.where(low, pltpu.roll(v0, 64, 1), v1).astype(bf16))


def fold(v):
    total = v[0:8]
    for k in range(8, v.shape[0], 8):
        total = total + v[k:k + 8]
    return total


def rows_of(ref, at):
    return jnp.concatenate([ref[c, at, :] for c in range(ref.shape[0])], axis=1)


def set_rows(ref, at, value):
    for c in range(ref.shape[0]):
        ref[c, at, :] = value[:, c * 128:(c + 1) * 128]


def mean_of(v):
    return jnp.mean(v, axis=-1, keepdims=True)


def gelu_pair(x):
    k = math.sqrt(2.0 / math.pi)
    c = 0.044715
    x2 = x * x
    half = 0.5 + 0.5 * jnp.tanh(x * (k + (k * c) * x2))
    value = x * half
    slope = half + value * (1.0 - half) * (2.0 * k + (6.0 * k * c) * x2)
    return value, slope


def ffn_hidden(x_get, nbuf, sbuf, alow, hid, slope, weight, vec, bias_in, rows_step):
    for r in range(0, nbuf.shape[1], rows_step):
        at = pl.ds(r, rows_step)
        v = x_get(at).astype(f32) + rows_of(nbuf, at)
        center = v - mean_of(v)
        inv = lax.rsqrt(mean_of(center * center) + epsilon)
        n = center * inv
        set_rows(nbuf, at, n)
        sbuf[at, :] = jnp.broadcast_to(inv, (rows_step, 128))
        alow[at, :] = (n * vec[0:1] + vec[1:2]).astype(bf16)
    for c in range(hid.shape[0]):
        value, back = gelu_pair(dot_nt(alow[...], weight(0, c)) + bias_in[c])
        hid[c] = value.astype(bf16)
        slope[c] = back.astype(bf16)


def ffn_branch(hid, acc, weight):
    steps = hid.shape[0]
    every = jnp.concatenate([hid[c] for c in range(steps)], axis=1)
    acc[...] = dot_nn(every, weight(1, 0, steps))


def ffn_middle(nbuf, acc, glow, cot, outv, vec, sums, rows_step):
    for r in range(0, nbuf.shape[1], rows_step):
        at = pl.ds(r, rows_step)
        v = rows_of(nbuf, at) * vec[0:1] + vec[1:2] + (acc[at, :] + vec[4:5])
        center = v - mean_of(v)
        inv = lax.rsqrt(mean_of(center * center) + epsilon)
        n = center * inv
        outv[at, :] = (n * vec[2:3] + vec[3:4]).astype(bf16)
        g = cot[at, :].astype(f32)
        q = g * vec[2:3]
        gr = inv * (q - mean_of(q) - n * mean_of(q * n))
        acc[at, :] = gr
        low = gr.astype(bf16)
        glow[at, :] = low
        sums[2] += fold(g * n)
        sums[3] += fold(g)
        sums[4] += fold(low.astype(f32))


def ffn_backward(nbuf, sbuf, hid, slope, acc, glow, weight, bsum, vec, sums, rows_step, put):
    for c in range(hid.shape[0]):
        gh = dot_nt(glow[...], weight(1, c))
        gpre = (gh * slope[c].astype(f32)).astype(bf16)
        slope[c] = gpre
        bsum[c] += fold(gpre.astype(f32))
        acc[...] += dot_nn(gpre, weight(0, c))
    for r in range(0, nbuf.shape[1], rows_step):
        at = pl.ds(r, rows_step)
        ga = acc[at, :]
        n = rows_of(nbuf, at)
        sums[0] += fold(ga * n)
        sums[1] += fold(ga)
        q = ga * vec[0:1]
        put(at, sbuf[at, 0:1] * (q - mean_of(q) - n * mean_of(q * n)))


def ffn_grads(alow, hid, slope, glow, dw):
    chunk = hid.shape[2]
    for c in range(hid.shape[0]):
        at = pl.ds(c * chunk, chunk)
        dw[1, at, :] += dot_tn(hid[c], glow[...])
        dw[0, at, :] += dot_tn(slope[c], alow[...])


def layer_kernel(geo, tok, cot, win_own, wout_own, hp_all, wd_all, cp_all, tw, b_in, *rest):
    vec_own = rest[:5]
    (out, gtok, grow, dwin_own, dwout_own, small,
                 tokv, cotv, outv, w0, w1, hp, wd, cp, dw, send1, recv1, send2, recv2, t_ref, o_ref,
                 nbuf, sbuf, alow, hid, slope, acc, glow, sums, bsum, rz, rze, rzl, sv, rv, va, ra, vec, bias_in,
                 ss1, rs1, ss2, rs2, free1, free2, load, io,
                 s_core, r_core, s_first, r_first, s_next, r_next, s_z, r_z, s_vec, r_vec, ready,
                 s_spread, r_spread, s_relay, r_relay, s_pair, r_pair, s_early, r_early, s_late, r_late, s_va, r_va) = rest[5:]
    parts, pairs, span, width, jobs, slots, chunk, rows_step, planes = geo
    shard = dw.shape[1] // (parts * planes)
    me = lax.axis_index("seq")
    plane = lax.axis_index("batch")

    def peer(d):
        return lax.rem(me + d, parts)

    def load_of(k):
        if k < jobs:
            return pltpu.make_async_copy(tok.at[k], tokv.at[k], load.at[k])
        a, b = ((hp_all, hp), (wd_all, wd), (cp_all, cp))[k - jobs]
        return pltpu.make_async_copy(a, b, load.at[k])

    for k in (jobs, 0, 1, jobs + 1, 2, 3, jobs + 2):
        load_of(k).start()

    core, quad = lax.rem(me, 2), me // 2
    quads = parts // 2
    x, y = lax.rem(quad, 2), quad // 2
    partner = (me + 1 - 2 * core, plane)
    x_peer = (me + 2 - 4 * x, plane)
    y_peer = (me + 4 - 8 * y, plane)
    quad_x, quad_y = quad + 1 - 2 * x, quad + 2 - 4 * y
    last = planes - 1

    def send(src, dst, s, r, to):
        return pltpu.make_async_remote_copy(
            src_ref=src, dst_ref=dst, send_sem=s, recv_sem=r, device_id=to, device_id_type=MESH)

    own_loads = (
        pltpu.make_async_copy(win_own, w0.at[quad, core, plane], load.at[jobs + 3]),
        pltpu.make_async_copy(wout_own, w1.at[quad, core, plane], load.at[jobs + 4]),
    )
    for copy in own_loads:
        copy.start()

    owner = me * planes + plane
    part = width // (parts * planes)
    per_row = width // shard
    bias_row = 5 + owner // per_row
    row16 = lax.broadcasted_iota(jnp.int32, (16, width), 0)
    is_bias = row16 == jnp.zeros((16, width), jnp.int32) + bias_row
    sv[0] = jnp.zeros_like(sv[0])
    for j in range(5):
        sv[0, j:j + 1, 0:part] = vec_own[j][...].astype(f32)
    sv[0, 8:9, 0:shard] = b_in[...].astype(f32)
    rows8 = pltpu.roll(sv[0, 0:8], owner * part, 1)
    bias8 = pltpu.roll(sv[0, 8:16], lax.rem(owner, per_row) * shard, 1)
    placed = jnp.concatenate([rows8, jnp.zeros((8, width), f32)], axis=0)
    placed = jnp.where(is_bias, jnp.broadcast_to(bias8[0:1], (16, width)), placed)
    va[0] = placed.astype(bf16)

    barrier = pltpu.get_barrier_semaphore()

    def greet(d, carry):
        pl.semaphore_signal(barrier, inc=1, device_id=(peer(d), plane), device_id_type=MESH)
        return carry

    def greet_z(d, carry):
        pl.semaphore_signal(barrier, inc=1, device_id=(me, lax.rem(plane + d, planes)), device_id_type=MESH)
        return carry

    lax.fori_loop(1, parts, greet, 0)
    lax.fori_loop(1, planes, greet_z, 0)
    pl.semaphore_wait(barrier, parts - 1 + planes - 1)

    def remote(send, recv, ss, rs, k, d):
        p = peer(d)
        return pltpu.make_async_remote_copy(
            src_ref=send.at[lax.rem(k, 2), p], dst_ref=recv.at[lax.rem(k, slots), me],
            send_sem=ss.at[lax.rem(k, 2), d], recv_sem=rs.at[lax.rem(k, slots), d],
            device_id=(p, plane), device_id_type=MESH)

    def wait_sends(send, recv, ss, rs, k):
        def one(d, carry):
            remote(send, recv, ss, rs, k, d).wait_send()
            return carry

        lax.fori_loop(1, parts, one, 0)

    def wait_recvs(send, recv, ss, rs, k):
        def one(d, carry):
            source = lax.rem(me + parts - d, parts)
            slot = lax.rem(k, slots)
            pltpu.make_async_remote_copy(
                src_ref=send.at[0, 0], dst_ref=recv.at[slot, source],
                send_sem=ss.at[0, d], recv_sem=rs.at[slot, d],
                device_id=(source, plane), device_id_type=MESH).wait_recv()
            return carry

        lax.fori_loop(1, parts, one, 0)

    def tell(sem, k):
        def one(d, carry):
            pl.semaphore_signal(sem.at[lax.rem(k, slots)], inc=1, device_id=(peer(d), plane), device_id_type=MESH)
            return carry

        lax.fori_loop(1, parts, one, 0)

    def in_plane(d):
        return 2 * lax.rem(quad + d, quads) + core

    def along(d):
        return lax.rem(plane + d, planes)

    def spread_z(d):
        block = w0.at[quad, core, plane]
        return send(block, block, s_spread.at[0, d], r_spread.at[0, d], (me, along(d)))

    def spread_out(d):
        block = w1.at[quad, core, plane]
        return send(block, block, s_spread.at[1, d], r_spread.at[1, d], (in_plane(d), plane))

    def spread_in(n):
        block = w0.at[quad, core]
        return send(block, block, s_spread.at[2, n], r_spread.at[2, n], (x_peer, y_peer)[n])

    def pass_in(n):
        block = w0.at[(quad_x, quad_y)[n], core, pl.ds(n * planes // 2, planes // 2)]
        return send(block, block, s_spread.at[2, 2 + n], r_spread.at[2, 2 + n], (y_peer, x_peer)[n])

    def relay(origin, up):
        block = w1.at[:, core, origin]
        return send(block, block, s_relay.at[up, origin], r_relay.at[origin], (me, plane + 2 * up - 1))

    def pair_in(q):
        block = w0.at[q, core]
        return send(block, block, s_pair.at[0, q], r_pair.at[0, q], partner)

    def pair_out(origin):
        block = w1.at[:, core, origin]
        return send(block, block, s_pair.at[1, origin], r_pair.at[1, origin], partner)

    def relay_step(j):
        below, above = plane - 1 - j, plane + 1 + j

        @pl.when(below >= 0)
        def _():
            relay(below, 1).wait_recv()

            @pl.when(plane < last)
            def _():
                relay(below, 1).start()

            pair_out(below).start()

        @pl.when(above <= last)
        def _():
            relay(above, 0).wait_recv()

            @pl.when(plane > 0)
            def _():
                relay(above, 0).start()

            pair_out(above).start()

    def vec_spread(k):
        to = (partner, x_peer, y_peer)[k] if k < 3 else (me, along(k - 2))
        return send(va.at[min(k, 3)], ra.at[k], s_va.at[k], r_va.at[k], to)

    def vec_gather(k):
        if k > 0:
            vec_spread(k - 1).wait_recv()
            va[k] = (va[k - 1].astype(f32) + ra[k - 1].astype(f32)).astype(bf16)
        for j in ((k,) if k < 3 else range(3, 2 + planes)):
            vec_spread(j).start()

    def gather_start():
        for copy in own_loads:
            copy.wait()
        for d in range(1, planes):
            spread_z(d).start()
        for d in range(1, quads):
            spread_out(d).start()

    def gather_out():
        for d in range(1, quads):
            spread_out(d).wait_recv()

        @pl.when(plane < last)
        def _():
            relay(plane, 1).start()

        @pl.when(plane > 0)
        def _():
            relay(plane, 0).start()

        pair_out(plane).start()

    def gather_in():
        for d in range(1, planes):
            spread_z(d).wait_recv()
        for n in range(2):
            spread_in(n).start()
        pair_in(quad).start()

    def gather_pass():
        for n in range(2):
            spread_in(n).wait_recv()
        for n in range(2):
            pass_in(n).start()
        pair_in(quad_x).start()
        pair_in(quad_y).start()

    def gather_diagonal():
        for n in range(2):
            pass_in(n).wait_recv()
        pair_in(quads - 1 - quad).start()

    def gather_end_out():
        for origin in range(planes):
            pair_out(origin).wait_recv()

    def gather_end_in():
        for q in range(quads):
            pair_in(q).wait_recv()

        total = va[3].astype(f32)
        for k in range(3, 2 + planes):
            vec_spread(k).wait_recv()
            total = total + ra[k].astype(f32)
        vec[...] = total[0:8]
        for f in range(0, bsum.shape[0] * chunk, width):
            bias_in[f // chunk, 0:1, f % chunk:f % chunk + width] = total[5 + f // width:6 + f // width]

    def gather_sent():
        for k in range(2 + planes):
            vec_spread(k).wait_send()
        for d in range(1, planes):
            spread_z(d).wait_send()
        for d in range(1, quads):
            spread_out(d).wait_send()
        for n in range(2):
            spread_in(n).wait_send()
            pass_in(n).wait_send()
        for q in range(quads):
            pair_in(q).wait_send()
        for origin in range(planes):
            pair_out(origin).wait_send()

            @pl.when((plane < last) & (origin <= plane))
            def _():
                relay(origin, 1).wait_send()

            @pl.when((plane > 0) & (origin >= plane))
            def _():
                relay(origin, 0).wait_send()

    def weight(m, c, count=1):
        n = chunk // (2 * planes * shard)
        at = pl.ds(c * n, count * n)
        block = w0[at] if m == 0 else w1[at]
        return block.reshape(count * chunk, width)

    def told(sem, k):
        pl.semaphore_wait(sem.at[lax.rem(k, slots)], parts - 1)

    one_way = (send1, recv1, ss1, rs1)
    way_back = (send2, recv2, ss2, rs2)

    def hidden_job(k):
        @pl.when(k >= 2)
        def _():
            wait_sends(*one_way, k - 2)

        @pl.when(k >= slots)
        def _():
            told(free1, k)

        table = dot_nt(hp[...], tokv[lax.rem(k, jobs)]).astype(bf16)
        send1[lax.rem(k, 2)] = table.reshape(parts, 2 * pairs, span)
        recv1[lax.rem(k, slots), me] = send1[lax.rem(k, 2), me]

        def one(d, carry):
            remote(*one_way, k, d).start()
            return carry

        lax.fori_loop(1, parts, one, 0)

    def sequence_job(k, carry):
        wait_recvs(*one_way, k)
        radix_step(recv1.at[lax.rem(k, slots)], tw, t_ref, parts, pairs, span)

        @pl.when(k < 2 * jobs - slots)
        def _():
            tell(free1, k)

        @pl.when(k >= 2)
        def _():
            wait_sends(*way_back, k - 2)

        @pl.when(k >= slots)
        def _():
            told(free2, k)

        slot = lax.rem(k, 2)
        half = span // 2

        def put(p, rows, cols, value):
            send2[slot, p, rows, cols] = value

        for base in range(2):
            o_ref[...] = dot_nn(t_ref[...], wd[:, base * half:(base + 1) * half])
            for u in range(base * parts // 4, (base + 1) * parts // 4):
                spread_step(o_ref, put, me, parts, pairs, u, base)
        recv2[lax.rem(k, slots), me] = send2[slot, me]

        def one(d, carry):
            remote(*way_back, k, d).start()
            return carry

        lax.fori_loop(1, parts, one, 0)
        return carry

    def mixed_job(k):
        wait_recvs(*way_back, k)
        blocks = recv2[lax.rem(k, slots)].reshape(width, span)
        natural = dot_tn(blocks, cp[...])
        step = span // parts
        for b in range(parts):
            for c in range(width // 128):
                nbuf[c, pl.ds(b, step, stride=parts), :] = natural[b * step:(b + 1) * step, c * 128:(c + 1) * 128]

    vec_gather(0)
    gather_start()
    vec_gather(1)
    load_of(jobs).wait()
    load_of(0).wait()
    hidden_job(0)
    dw[...] = jnp.zeros_like(dw)
    sums[...] = jnp.zeros_like(sums)
    bsum[...] = jnp.zeros_like(bsum)
    gather_out()
    vec_gather(2)
    gather_in()
    for k in (1, 2, 3, jobs + 1, jobs + 2):
        load_of(k).wait()

    sequence_job(0, 0)
    vec_gather(3)
    relay_step(0)
    gather_pass()
    hidden_job(1)
    relay_step(1)
    hidden_job(2)
    gather_diagonal()
    hidden_job(3)
    gather_end_in()

    def out_copy(i):
        return pltpu.make_async_copy(outv, out.at[i], io.at[0])

    def cot_copy(i):
        return pltpu.make_async_copy(cot.at[i], cotv, io.at[1])

    def row_copy(i):
        return pltpu.make_async_copy(acc, grow.at[i], io.at[2])

    def main(i, carry):
        cot_copy(i).start()
        mixed_job(i)
        tell(free2, i)
        ffn_hidden(lambda at: tokv[i, at, :], nbuf, sbuf, alow, hid, slope, weight, vec, bias_in, rows_step)
        @pl.when(i != 1)
        def _():
            sequence_job(i + 1 + (i + 1) // 2, 0)

        @pl.when(i == 0)
        def _():
            relay_step(2)
            gather_end_out()

        ffn_branch(hid, acc, weight)
        cot_copy(i).wait()

        @pl.when(i > 0)
        def _():
            out_copy(i - 1).wait()

        ffn_middle(nbuf, acc, glow, cotv, outv, vec, sums, rows_step)
        out_copy(i).start()

        def put(at, value):
            acc[at, :] = value
            tokv[i, at, :] = value.astype(bf16)

        ffn_backward(nbuf, sbuf, hid, slope, acc, glow, weight, bsum, vec, sums, rows_step, put)
        row_copy(i).start()
        hidden_job(i + jobs)

        @pl.when(i < 3)
        def _():
            sequence_job(i + 2 + i // 2, 0)

        ffn_grads(alow, hid, slope, glow, dw)
        row_copy(i).wait()
        return carry

    lax.fori_loop(0, jobs, main, 0)

    rest_rows = 16
    most = shard - rest_rows

    def rows_at(start, count=shard):
        return pl.ds(pl.multiple_of(start, shard), count)

    def target(v):
        return lax.rem(plane + 1 + v, planes)

    def owned(q, c, v):
        return rows_at(((2 * q + c) * planes + target(v)) * shard)

    head = pl.ds(0, most)

    def core_copy(v):
        return send(w1.at[v], w0.at[v], s_core.at[v], r_core.at[v], partner)

    def first_copy(v, m):
        at = pl.ds(2 * m, 2)
        return send(w1.at[2 + v // 2, lax.rem(v, 2), at, head], w1.at[v // 2, lax.rem(v, 2), at, head],
                    s_first.at[v, m], r_first.at[v, m], (x_peer, y_peer)[m])

    def next_copy(v, m):
        return send(w0.at[0, v // 2, 2 * lax.rem(v, 2) + m, head],
                    (alow, glow)[m].at[pl.ds(pl.multiple_of(v * most, most), most)],
                    s_next.at[v, m], r_next.at[v, m], (y_peer, x_peer)[m])

    def z_copy(v):
        return send(w0.at[1, v // 2, pl.ds(2 * lax.rem(v, 2), 2), head], rz.at[v],
                    s_z.at[v], r_z.at[v], (me, target(v)))

    def early_copy(v):
        return send(hid.at[v, pl.ds(0, 2 * quads * rest_rows)], rze.at[v], s_early.at[v], r_early.at[v], (me, target(v)))

    def late_copy(d):
        q = lax.rem(quad + d, quads)
        return send(hid.at[last, pl.ds(pl.multiple_of(2 * q * rest_rows, 2 * rest_rows), 2 * rest_rows)], rzl.at[d - 1],
                    s_late.at[d - 1], r_late.at[d - 1], (in_plane(d), plane))

    def vec_copy(k):
        to = (partner, x_peer, y_peer)[k] if k < 3 else (me, target(k - 3))
        return send(sv.at[min(k, 3)], rv.at[k], s_vec.at[k], r_vec.at[k], to)

    def core_step(v, carry):
        for q in range(quads):
            for m in range(2):
                w1[v, q // 2, 2 * (q % 2) + m] = dw[m, owned(q, 1 - core, v)].astype(bf16)
        core_copy(v).start()
        return carry

    def owned_most(q, v):
        return rows_at(((2 * q + core) * planes + target(v)) * shard, most)

    def owned_rest(q, v):
        return pl.ds(pl.multiple_of(((2 * q + core) * planes + target(v)) * shard + most, 16), rest_rows)

    def first_step(v, carry):
        core_copy(v).wait_recv()
        for q in range(quads):
            for m in range(2):
                at = owned(q, core, v)
                dw[m, at] += w0[v, q // 2, 2 * (q % 2) + m].astype(f32)

        @pl.when(v < last)
        def _():
            for q in range(quads):
                for m in range(2):
                    at = pl.ds((2 * q + m) * rest_rows, rest_rows)
                    hid[v, at, :] = dw[m, owned_rest(q, v)].astype(bf16)
            early_copy(v).start()

        for k in range(2):
            for m in range(2):
                q = 2 * k + 1 - x if m == 0 else 2 * (1 - y) + k
                w1[2 + v // 2, lax.rem(v, 2), 2 * m + k, 0:most, :] = dw[m, owned_most(q, v)].astype(bf16)
        for m in range(2):
            first_copy(v, m).start()
        return carry

    def next_step(v, carry):
        for m in range(2):
            first_copy(v, m).wait_recv()
        for k in range(2):
            for m in range(2):
                q = 2 * k + x if m == 0 else 2 * y + k
                dw[m, owned_most(q, v)] += w1[v // 2, lax.rem(v, 2), 2 * m + k, 0:most, :].astype(f32)
        for m in range(2):
            q = 2 * (1 - y) + x if m == 0 else 2 * y + 1 - x
            w0[0, v // 2, 2 * lax.rem(v, 2) + m, 0:most, :] = dw[m, owned_most(q, v)].astype(bf16)
            next_copy(v, m).start()
        return carry

    def z_step(v, carry):
        for m in range(2):
            next_copy(v, m).wait_recv()
            dw[m, owned_most(quad, v)] += (alow, glow)[m][pl.ds(pl.multiple_of(v * most, most), most)].astype(f32)

        @pl.when(v < last)
        def _():
            for m in range(2):
                w0[1, v // 2, 2 * lax.rem(v, 2) + m, 0:most, :] = dw[m, owned_most(quad, v)].astype(bf16)
            z_copy(v).start()

        return carry

    def late_step():
        for v in range(last):
            early_copy(v).wait_recv()
        for q in range(quads):
            for m in range(2):
                at = owned_rest(q, last)
                total = dw[m, at]
                for v in range(last):
                    total = total + rze[v, (2 * q + m) * rest_rows:(2 * q + m + 1) * rest_rows].astype(f32)
                dw[m, at] = total
                hid[last, (2 * q + m) * rest_rows:(2 * q + m + 1) * rest_rows, :] = total.astype(bf16)
        for d in range(1, quads):
            late_copy(d).start()

    def vec_step(k):
        if k == 0:
            sv[0] = jnp.zeros_like(sv[0])
            for j in range(5):
                sv[0, j:j + 1] = jnp.sum(sums[j], axis=0, keepdims=True)
            piece = math.gcd(width, chunk)
            for f in range(0, bsum.shape[0] * chunk, piece):
                sv[0, 5 + f // width:6 + f // width, f % width:f % width + piece] = jnp.sum(
                    bsum[f // chunk, :, f % chunk:f % chunk + piece], axis=0, keepdims=True)
        else:
            vec_copy(k - 1).wait_recv()
            sv[k] = sv[k - 1] + rv[k - 1]
        for j in ((k,) if k < 3 else range(3, 2 + planes)):
            vec_copy(j).start()

    def gt_copy(i):
        return pltpu.make_async_copy(tokv.at[i], gtok.at[i], io.at[4 + i])

    def final(i, carry):
        back = pltpu.make_async_copy(grow.at[i], acc, io.at[2])
        back.start()
        mixed_job(i + jobs)
        back.wait()
        for c in range(width // 128):
            tokv[i, :, c * 128:(c + 1) * 128] = (nbuf[c] + acc[:, c * 128:(c + 1) * 128]).astype(bf16)
        gt_copy(i).start()
        return carry

    gather_sent()
    pl.semaphore_signal(ready.at[0], inc=1, device_id=partner, device_id_type=MESH)
    pl.semaphore_wait(ready.at[0], 1)
    lax.fori_loop(0, planes, core_step, 0)
    vec_step(0)

    def core_sent(v, carry):
        core_copy(v).wait_send()
        return carry

    lax.fori_loop(0, planes, core_sent, 0)
    pl.semaphore_signal(ready.at[1], inc=1, device_id=x_peer, device_id_type=MESH)
    pl.semaphore_signal(ready.at[2], inc=1, device_id=y_peer, device_id_type=MESH)
    vec_step(1)
    pl.semaphore_wait(ready.at[1], 1)
    pl.semaphore_wait(ready.at[2], 1)
    first_step(0, 0)
    final(0, 0)
    tell(free2, jobs)
    lax.fori_loop(1, last, first_step, 0)
    next_step(0, 0)
    vec_step(2)
    final(2, 0)
    next_step(1, 0)
    final(1, 0)
    lax.fori_loop(2, last, next_step, 0)
    z_step(0, 0)
    first_step(last, 0)
    vec_step(3)
    z_step(1, 0)
    sequence_job(2 * jobs - 1, 0)
    lax.fori_loop(2, last, z_step, 0)
    next_step(last, 0)
    late_step()
    final(3, 0)
    z_step(last, 0)
    own_most, own_rest = owned_most(quad, last), owned_rest(quad, last)
    for v in range(last):
        z_copy(v).wait_recv()
    for d in range(1, quads):
        late_copy(d).wait_recv()
    for m in range(2):
        total = dw[m, own_most]
        for v in range(last):
            total = total + rz[v, m].astype(f32)
        (dwin_own, dwout_own)[m][0:most] = total
        total = dw[m, own_rest]
        for d in range(1, quads):
            total = total + rzl[d - 1, m * rest_rows:(m + 1) * rest_rows].astype(f32)
        (dwin_own, dwout_own)[m][most:shard] = total
    total = sv[3]
    for k in range(3, 2 + planes):
        vec_copy(k).wait_recv()
        total = total + rv[k]
    mine = jnp.sum(jnp.where(is_bias, total, 0.0), axis=0, keepdims=True)
    mine = pltpu.roll(jnp.broadcast_to(mine, (8, width)), width - lax.rem(owner, per_row) * shard, 1)
    rows8 = pltpu.roll(total[0:8], width - owner * part, 1)
    row8 = lax.broadcasted_iota(jnp.int32, (8, 128), 0)
    small[...] = jnp.where(row8 == 5, mine[:, 0:128], rows8[:, 0:128])

    def sent(v, carry):
        for m in range(2):
            first_copy(v, m).wait_send()
            next_copy(v, m).wait_send()
        return carry

    lax.fori_loop(0, planes, sent, 0)
    for k in range(2 * jobs - 2, 2 * jobs):
        wait_sends(*way_back, k)
        wait_sends(*one_way, k)
    for v in range(last):
        z_copy(v).wait_send()
        early_copy(v).wait_send()
    for d in range(1, quads):
        late_copy(d).wait_send()
    for k in range(2 + planes):
        vec_copy(k).wait_send()
    out_copy(jobs - 1).wait()
    for i in range(jobs):
        gt_copy(i).wait()


def layer_call(tok, cot, win_own, wout_own, b_in, vectors, parts, planes):
    jobs, span, width = tok.shape
    shard = wout_own.shape[0]
    ff = shard * parts * planes
    pairs = width // 2 // parts
    chunk, rows_step = ff // (parts // 2), span // 4
    steps = ff // chunk
    length = span * parts
    slots = 3
    geo = (parts, pairs, span, width, jobs, slots, chunk, rows_step, planes)
    tables = (
        jnp.asarray(packed_hidden(width, parts)),
        jnp.asarray(inner_table(span, length)),
        jnp.asarray(column_order(width, parts)),
        jnp.asarray(twiddles(parts, span)),
    )
    hbm, vmem, dma = pl.BlockSpec(memory_space=pl.ANY), pl.BlockSpec(memory_space=pltpu.VMEM), pltpu.SemaphoreType.DMA
    block = (parts, 2 * pairs, span)
    scratch = [
        pltpu.VMEM((jobs, span, width), bf16),
        pltpu.VMEM((span, width), bf16),
        pltpu.VMEM((span, width), bf16),
        pltpu.VMEM((parts // 2, 2, planes, shard, width), bf16),
        pltpu.VMEM((parts // 2, 2, planes, shard, width), bf16),
        pltpu.VMEM((width, width), bf16),
        pltpu.VMEM((2 * span, span), bf16),
        pltpu.VMEM((width, width), bf16),
        pltpu.VMEM((2, ff, width), f32),
        pltpu.VMEM((2,) + block, bf16),
        pltpu.VMEM((slots,) + block, bf16),
        pltpu.VMEM((2,) + block, bf16),
        pltpu.VMEM((slots,) + block, bf16),
        pltpu.VMEM((2 * parts * pairs + 16, 2 * span), bf16),
        pltpu.VMEM((2 * parts * pairs + 16, span // 2), f32),
        pltpu.VMEM((width // 128, span, 128), f32),
        pltpu.VMEM((span, 128), f32),
        pltpu.VMEM((span, width), bf16),
        pltpu.VMEM((steps, span, chunk), bf16),
        pltpu.VMEM((steps, span, chunk), bf16),
        pltpu.VMEM((span, width), f32),
        pltpu.VMEM((span, width), bf16),
        pltpu.VMEM((5, 8, width), f32),
        pltpu.VMEM((steps, 8, chunk), f32),
        pltpu.VMEM((planes - 1, 2, shard - 16, width), bf16),
        pltpu.VMEM((planes - 1, parts * 16, width), bf16),
        pltpu.VMEM((parts // 2 - 1, 2 * 16, width), bf16),
        pltpu.VMEM((4, 16, width), f32),
        pltpu.VMEM((2 + planes, 16, width), f32),
        pltpu.VMEM((4, 16, width), bf16),
        pltpu.VMEM((2 + planes, 16, width), bf16),
        pltpu.VMEM((8, width), f32),
        pltpu.VMEM((steps, 1, chunk), f32),
        dma((2, parts)), dma((slots, parts)), dma((2, parts)), dma((slots, parts)),
        pltpu.SemaphoreType.REGULAR((slots,)), pltpu.SemaphoreType.REGULAR((slots,)),
        dma((jobs + 5,)), dma((4 + jobs,)),
        dma((planes,)), dma((planes,)), dma((planes, 2)), dma((planes, 2)), dma((planes, 2)), dma((planes, 2)),
        dma((planes - 1,)), dma((planes - 1,)), dma((2 + planes,)), dma((2 + planes,)),
        pltpu.SemaphoreType.REGULAR((3,)),
        dma((3, max(parts // 2, planes))), dma((3, max(parts // 2, planes))), dma((2, planes)), dma((planes,)),
        dma((2, max(parts // 2, planes))), dma((2, max(parts // 2, planes))),
        dma((planes - 1,)), dma((planes - 1,)), dma((parts // 2 - 1,)), dma((parts // 2 - 1,)),
        dma((2 + planes,)), dma((2 + planes,)),
    ]
    shape = jax.ShapeDtypeStruct
    return pl.pallas_call(
        partial(layer_kernel, geo),
        out_shape=(
            shape(tok.shape, bf16),
            shape(tok.shape, bf16),
            shape(tok.shape, f32),
            shape((shard, width), f32),
            shape((shard, width), f32),
            shape((8, 128), f32),
        ),
        in_specs=[hbm] * 7 + [vmem] * 7,
        out_specs=(hbm,) * 3 + (vmem,) * 3,
        scratch_shapes=scratch,
        compiler_params=pltpu.CompilerParams(
            collective_id=1, has_side_effects=True, vmem_limit_bytes=64 * 1024 * 1024 - 256 * 1024),
        name="encoder_layer",
    )(tok, cot, win_own, wout_own, *tables, b_in, *vectors)


def local_fast(tokens, w_in, b_in, w_out, b_out, gain_one, shift_one, gain_two, shift_two, cotangent):
    both = ("seq", "batch")
    parts = lax.axis_size("seq")
    width = tokens.shape[2]
    shard = w_in.shape[1]
    planes = lax.axis_size("batch")
    part = b_out.shape[0]
    vectors = [v.reshape(1, part) for v in (gain_one, shift_one, gain_two, shift_two, b_out)]
    out, gtok, _, dwin, dwout, small = layer_call(
        tokens, cotangent, w_in.T, w_out, b_in.reshape(1, shard), vectors, parts, planes)
    rest = small[:5, :part]
    return (out, gtok, dwin.T, small[5, :shard], dwout, rest[4], rest[0], rest[1], rest[2], rest[3])


def hidden_table(extent):
    idx_all = jnp.arange(extent, dtype=jnp.int32)
    angles = (idx_all[:, None] * idx_all[None, :] % extent).astype(jnp.float32) * (
        2.0 * math.pi / extent
    )
    factor = 1.0 / math.sqrt(extent)
    return jnp.concatenate([jnp.cos(angles) * factor, jnp.sin(angles) * factor], axis=1).astype(
        jnp.bfloat16
    )


def sequence_table(length):
    block_rows = min(512, length)
    block_count = length // block_rows
    col_ids = jnp.arange(length, dtype=jnp.int32)
    factor = 1.0 / math.sqrt(length)

    def table_rows(block_index):
        row_ids = block_index * block_rows + jnp.arange(block_rows, dtype=jnp.int32)
        angles = (row_ids[:, None] * col_ids[None, :] % length).astype(jnp.float32) * (
            2.0 * math.pi / length
        )
        return (jnp.stack([jnp.cos(angles), -jnp.sin(angles)]) * factor).astype(jnp.bfloat16)

    blocks = lax.map(table_rows, jnp.arange(block_count, dtype=jnp.int32))
    return jnp.moveaxis(blocks, 1, 0).reshape(2, length, length)


def normalize(values, gain, shift):
    center = values - jnp.mean(values, axis=-1, keepdims=True)
    inv_std = lax.rsqrt(jnp.mean(center * center, axis=-1, keepdims=True) + epsilon)
    normed = center * inv_std
    return (normed * gain + shift, normed, inv_std)


def norm_back(grad_out, normed, inv_std, gain):
    scaled = grad_out * gain
    centered = scaled - jnp.mean(scaled, axis=-1, keepdims=True)
    return inv_std * (centered - normed * jnp.mean(scaled * normed, axis=-1, keepdims=True))


def local(tokens, w_in, b_in, w_out, b_out, gain_one, shift_one, gain_two, shift_two, cotangent):
    batch_rows, seq_part, model_width = tokens.shape
    length = seq_part * lax.axis_size("seq")
    w_in_all, b_in_all, w_out_all, b_out_all, g_one_all, s_one_all, g_two_all, s_two_all = (
        lax.all_gather(w_in, ("seq", "batch"), axis=1, tiled=True),
        lax.all_gather(b_in, ("seq", "batch"), axis=0, tiled=True),
        lax.all_gather(w_out, ("seq", "batch"), axis=0, tiled=True),
        lax.all_gather(b_out, ("seq", "batch"), axis=0, tiled=True),
        lax.all_gather(gain_one, ("seq", "batch"), axis=0, tiled=True),
        lax.all_gather(shift_one, ("seq", "batch"), axis=0, tiled=True),
        lax.all_gather(gain_two, ("seq", "batch"), axis=0, tiled=True),
        lax.all_gather(shift_two, ("seq", "batch"), axis=0, tiled=True),
    )
    h_table = hidden_table(model_width)
    s_table = sequence_table(length)
    flat_tokens = tokens.reshape(-1, model_width)
    spectra = jnp.dot(flat_tokens, h_table, preferred_element_type=jnp.float32).astype(jnp.bfloat16)
    spectra = spectra.reshape(batch_rows, seq_part, 2, model_width)
    mixed_cols = jnp.einsum(
        "plm,bmpc->blc",
        s_table,
        lax.all_to_all(spectra, "seq", split_axis=3, concat_axis=1, tiled=True),
        preferred_element_type=jnp.float32,
    ).astype(jnp.bfloat16)
    mixed = lax.all_to_all(mixed_cols, "seq", split_axis=1, concat_axis=2, tiled=True)
    resid_one = flat_tokens.astype(jnp.float32) + mixed.reshape(-1, model_width).astype(jnp.float32)
    act_one, normed_one, inv_one = normalize(
        resid_one, g_one_all.astype(jnp.float32), s_one_all.astype(jnp.float32)
    )
    act_low = act_one.astype(jnp.bfloat16)
    pre_act = jnp.dot(act_low, w_in_all, preferred_element_type=jnp.float32) + b_in_all.astype(
        jnp.float32
    )
    activ, gelu_back = jax.vjp(partial(jax.nn.gelu, approximate=True), pre_act)
    hidden_low = activ.astype(jnp.bfloat16)
    branch = jnp.dot(hidden_low, w_out_all, preferred_element_type=jnp.float32) + b_out_all.astype(
        jnp.float32
    )
    resid_two = act_one + branch
    result, normed_two, inv_two = normalize(
        resid_two, g_two_all.astype(jnp.float32), s_two_all.astype(jnp.float32)
    )
    grad_out = cotangent.reshape(-1, model_width).astype(jnp.float32)
    grad_g_two = jnp.sum(grad_out * normed_two, axis=0)
    grad_s_two = jnp.sum(grad_out, axis=0)
    grad_r_two = norm_back(grad_out, normed_two, inv_two, g_two_all.astype(jnp.float32))
    grad_branch = grad_r_two.astype(jnp.bfloat16)
    grad_b_out = jnp.sum(grad_branch.astype(jnp.float32), axis=0)
    grad_w_out = jnp.einsum(
        "tf,td->fd", hidden_low, grad_branch, preferred_element_type=jnp.float32
    )
    grad_hidden = jnp.einsum(
        "td,fd->tf", grad_branch, w_out_all, preferred_element_type=jnp.float32
    )
    grad_pre = gelu_back(grad_hidden)[0].astype(jnp.bfloat16)
    grad_b_in = jnp.sum(grad_pre.astype(jnp.float32), axis=0)
    grad_w_in = jnp.einsum("td,tf->df", act_low, grad_pre, preferred_element_type=jnp.float32)
    grad_a_one = grad_r_two + jnp.einsum(
        "tf,df->td", grad_pre, w_in_all, preferred_element_type=jnp.float32
    )
    grad_g_one = jnp.sum(grad_a_one * normed_one, axis=0)
    grad_s_one = jnp.sum(grad_a_one, axis=0)
    grad_r_one = norm_back(grad_a_one, normed_one, inv_one, g_one_all.astype(jnp.float32))
    grad_mix = grad_r_one.astype(jnp.bfloat16).reshape(batch_rows, seq_part, model_width)
    spec_grad = jnp.einsum(
        "plm,blc->bmpc",
        s_table,
        lax.all_to_all(grad_mix, "seq", split_axis=2, concat_axis=1, tiled=True),
        preferred_element_type=jnp.float32,
    ).astype(jnp.bfloat16)
    grad_spec = lax.all_to_all(spec_grad, "seq", split_axis=1, concat_axis=3, tiled=True)
    grad_flat = grad_r_one + jnp.einsum(
        "te,de->td",
        grad_spec.reshape(-1, 2 * model_width),
        h_table,
        preferred_element_type=jnp.float32,
    )
    sum_w_in, sum_b_in, sum_w_out, sum_b_out, sum_g_one, sum_s_one, sum_g_two, sum_s_two = (
        lax.psum_scatter(grad_w_in, ("seq", "batch"), scatter_dimension=1, tiled=True),
        lax.psum_scatter(grad_b_in, ("seq", "batch"), scatter_dimension=0, tiled=True),
        lax.psum_scatter(grad_w_out, ("seq", "batch"), scatter_dimension=0, tiled=True),
        lax.psum_scatter(grad_b_out, ("seq", "batch"), scatter_dimension=0, tiled=True),
        lax.psum_scatter(grad_g_one, ("seq", "batch"), scatter_dimension=0, tiled=True),
        lax.psum_scatter(grad_s_one, ("seq", "batch"), scatter_dimension=0, tiled=True),
        lax.psum_scatter(grad_g_two, ("seq", "batch"), scatter_dimension=0, tiled=True),
        lax.psum_scatter(grad_s_two, ("seq", "batch"), scatter_dimension=0, tiled=True),
    )
    output = result.astype(jnp.bfloat16).reshape(batch_rows, seq_part, model_width)
    grad_tokens = grad_flat.astype(jnp.bfloat16).reshape(batch_rows, seq_part, model_width)
    return (
        output,
        grad_tokens,
        sum_w_in,
        sum_b_in,
        sum_w_out,
        sum_b_out,
        sum_g_one,
        sum_s_one,
        sum_g_two,
        sum_s_two,
    )


def solution(mesh):
    every = P(("seq", "batch"))

    def whole(tokens, w_in, *rest):
        parts = mesh.shape["seq"]
        fits = (
            parts == 8
            and tokens.shape[1] == 512 * parts
            and tokens.shape[2] % (32 * parts) == 0
            and w_in.shape[1] % (3 * 128) == 0
            and tokens.shape[0] == 4 * mesh.shape["batch"]
        )
        return jax.shard_map(
            local_fast if fits else local,
            mesh=mesh,
            in_specs=(
                P("batch", "seq", None),
                P(None, ("seq", "batch")),
                every,
                P(("seq", "batch"), None),
                every,
                every,
                every,
                every,
                every,
                P("batch", "seq", None),
            ),
            out_specs=(
                P("batch", "seq", None),
                P("batch", "seq", None),
                P(None, ("seq", "batch")),
                every,
                P(("seq", "batch"), None),
                every,
                every,
                every,
                every,
                every,
            ),
            check_vma=False,
        )(tokens, w_in, *rest)

    return whole
```

```python
from functools import partial
import math

import jax
import jax.numpy as jnp
import ml_dtypes
import numpy as np
from jax import lax
from jax.experimental import pallas as pl
from jax.experimental.pallas import tpu as pltpu
from jax.sharding import PartitionSpec as P

epsilon = 1e-05
f32, bf16 = jnp.float32, jnp.bfloat16
MESH = pl.DeviceIdType.MESH


def dot_nn(a, b):
    return lax.dot_general(a, b, (((1,), (0,)), ((), ())), preferred_element_type=f32)


def dot_nt(a, b):
    return lax.dot_general(a, b, (((1,), (1,)), ((), ())), preferred_element_type=f32)


def dot_tn(a, b):
    return lax.dot_general(a, b, (((0,), (0,)), ((), ())), preferred_element_type=f32)


def plan_columns(width, parts):
    pairs = width // 2 // parts
    r = np.arange(width)
    dev, kind, i = r // (2 * pairs), (r // pairs) % 2, r % pairs
    j = dev * pairs + i
    first = (kind == 1) & (j == 0)
    return j, kind, first


def packed_hidden(width, parts):
    j, kind, first = plan_columns(width, parts)
    k = np.arange(width)
    angle = (j[:, None] * k[None, :] % width) * (2.0 * math.pi / width)
    table = np.where(kind[:, None] == 0, np.cos(angle), np.sin(angle))
    nyquist = np.cos(np.pi * (k % 2))
    table = np.where(first[:, None], nyquist[None, :], table) / math.sqrt(width)
    return table.astype(np.float32).astype(ml_dtypes.bfloat16)


def column_order(width, parts):
    j, kind, first = plan_columns(width, parts)
    col = np.where(kind == 0, j, np.where(first, width // 2, (width - j) % width))
    return (col[:, None] == np.arange(width)[None, :]).astype(ml_dtypes.bfloat16)


def inner_table(span, length):
    a = np.arange(span)
    angle = (a[:, None] * a[None, :] % span) * (2.0 * math.pi / span)
    table = np.concatenate([np.cos(angle), np.sin(angle)], axis=0)
    return (table / math.sqrt(length)).astype(np.float32).astype(ml_dtypes.bfloat16)


def twiddles(parts, span):
    b = np.arange(parts)[:, None]
    angle = b * np.arange(span)[None, :] * (2.0 * math.pi / (parts * span))
    return np.concatenate([np.cos(angle), np.sin(angle)], axis=0).astype(np.float32)


def add(a, b):
    return (a[0] + b[0], a[1] + b[1])


def sub(a, b):
    return (a[0] - b[0], a[1] - b[1])


def minus_i(a):
    return (a[1], -a[0])


def dft4(x0, x1, x2, x3):
    t0, t1, t2, t3 = add(x0, x2), sub(x0, x2), add(x1, x3), sub(x1, x3)
    r = minus_i(t3)
    return add(t0, t2), add(t1, r), sub(t0, t2), sub(t1, r)


def dft8(x):
    e = dft4(x[0], x[2], x[4], x[6])
    o = dft4(x[1], x[3], x[5], x[7])
    h = math.sqrt(0.5)
    o1 = (h * (o[1][0] + o[1][1]), h * (o[1][1] - o[1][0]))
    o2 = minus_i(o[2])
    o3 = (h * (o[3][1] - o[3][0]), -h * (o[3][0] + o[3][1]))
    o = (o[0], o1, o2, o3)
    return [add(e[k], o[k]) for k in range(4)] + [sub(e[k], o[k]) for k in range(4)]


def radix_step(rec, tw, t_ref, parts, pairs, span):
    groups = pairs // 16
    count = 2 * parts * pairs

    row = lax.broadcasted_iota(jnp.int32, (16, 128), 0)
    for u in range(span // 128):
        lanes = pl.ds(u * 128, 128)
        lanes_im = pl.ds(span + u * 128, 128)
        extra = [jnp.zeros((16, 128), f32), jnp.zeros((16, 128), f32)]
        for g in range(groups):
            x = []
            for s in range(parts):
                re = rec[s, g * 16:g * 16 + 16, lanes].astype(f32)
                im = rec[s, pairs + g * 16:pairs + g * 16 + 16, lanes].astype(f32)
                x.append((re, -im))
            y = dft8(x)
            for b in range(parts):
                c, s = tw[b:b + 1, lanes], tw[parts + b:parts + b + 1, lanes]
                conj = y[(parts - b) % parts]
                for kind, (zr, zi) in enumerate((y[b], (conj[0], -conj[1]))):
                    tr = c * zr + s * zi
                    ti = c * zi - s * zr
                    base = (kind * parts + b) * pairs + g * 16
                    t_ref[base:base + 16, lanes] = tr.astype(bf16)
                    t_ref[base:base + 16, lanes_im] = ti.astype(bf16)
                    if g == 0:
                        hit = row == kind * parts + b
                        extra[0] = jnp.where(hit, jnp.broadcast_to(-ti[0:1], (16, 128)), extra[0])
                        extra[1] = jnp.where(hit, jnp.broadcast_to(tr[0:1], (16, 128)), extra[1])
        t_ref[count:count + 16, lanes] = extra[0].astype(bf16)
        t_ref[count:count + 16, lanes_im] = extra[1].astype(bf16)


def spread_step(o_ref, put, me, parts, pairs, u, half):
    count = 2 * parts * pairs
    lanes = pl.ds((u - half * parts // 4) * 128, 128)
    low = lax.broadcasted_iota(jnp.int32, (16, 128), 1) < 64
    row = lax.broadcasted_iota(jnp.int32, (16, 128), 0)
    special = (row == 0) & (jnp.zeros((16, 128), jnp.int32) + me == 0)
    extra = o_ref[count:count + 16, lanes]
    for p in range(parts // 2):
        for g in range(pairs // 16):
            v = [[None, None], [None, None]]
            for kind in range(2):
                for h in range(2):
                    base = (kind * parts + 2 * p + h) * pairs + g * 16
                    v[kind][h] = o_ref[base:base + 16, lanes]
            if g == 0:
                for h in range(2):
                    b = 2 * p + h
                    even = 0.5 * (v[0][h] + v[1][h])
                    odd = jnp.broadcast_to(0.5 * (extra[b:b + 1] - extra[parts + b:parts + b + 1]), (16, 128))
                    v[0][h] = jnp.where(special, even, v[0][h])
                    v[1][h] = jnp.where(special, odd, v[1][h])
            for kind in range(2):
                v0, v1 = v[kind]
                rows = pl.ds(kind * pairs + g * 16, 16)
                cols = pl.ds(p * 128, 128)
                put(2 * u, rows, cols, jnp.where(low, v0, pltpu.roll(v1, 64, 1)).astype(bf16))
                put(2 * u + 1, rows, cols, jnp.where(low, pltpu.roll(v0, 64, 1), v1).astype(bf16))


def fold(v):
    total = v[0:8]
    for k in range(8, v.shape[0], 8):
        total = total + v[k:k + 8]
    return total


def rows_of(ref, at):
    return jnp.concatenate([ref[c, at, :] for c in range(ref.shape[0])], axis=1)


def set_rows(ref, at, value):
    for c in range(ref.shape[0]):
        ref[c, at, :] = value[:, c * 128:(c + 1) * 128]


def mean_of(v):
    return jnp.mean(v, axis=-1, keepdims=True)


def gelu_pair(x):
    k = math.sqrt(2.0 / math.pi)
    c = 0.044715
    x2 = x * x
    half = 0.5 + 0.5 * jnp.tanh(x * (k + (k * c) * x2))
    value = x * half
    slope = half + value * (1.0 - half) * (2.0 * k + (6.0 * k * c) * x2)
    return value, slope


def ffn_hidden(x_get, nbuf, sbuf, alow, hid, slope, weight, vec, bias_in, rows_step):
    for r in range(0, nbuf.shape[1], rows_step):
        at = pl.ds(r, rows_step)
        v = x_get(at).astype(f32) + rows_of(nbuf, at)
        center = v - mean_of(v)
        inv = lax.rsqrt(mean_of(center * center) + epsilon)
        n = center * inv
        set_rows(nbuf, at, n)
        sbuf[at, :] = jnp.broadcast_to(inv, (rows_step, 128))
        alow[at, :] = (n * vec[0:1] + vec[1:2]).astype(bf16)
    for c in range(hid.shape[0]):
        value, back = gelu_pair(dot_nt(alow[...], weight(0, c)) + bias_in[c])
        hid[c] = value.astype(bf16)
        slope[c] = back.astype(bf16)


def ffn_branch(hid, acc, weight):
    steps = hid.shape[0]
    every = jnp.concatenate([hid[c] for c in range(steps)], axis=1)
    acc[...] = dot_nn(every, weight(1, 0, steps))


def ffn_middle(nbuf, acc, glow, cot, outv, vec, sums, rows_step):
    for r in range(0, nbuf.shape[1], rows_step):
        at = pl.ds(r, rows_step)
        v = rows_of(nbuf, at) * vec[0:1] + vec[1:2] + (acc[at, :] + vec[4:5])
        center = v - mean_of(v)
        inv = lax.rsqrt(mean_of(center * center) + epsilon)
        n = center * inv
        outv[at, :] = (n * vec[2:3] + vec[3:4]).astype(bf16)
        g = cot[at, :].astype(f32)
        q = g * vec[2:3]
        gr = inv * (q - mean_of(q) - n * mean_of(q * n))
        acc[at, :] = gr
        low = gr.astype(bf16)
        glow[at, :] = low
        sums[2] += fold(g * n)
        sums[3] += fold(g)
        sums[4] += fold(low.astype(f32))


def ffn_backward(nbuf, sbuf, hid, slope, acc, glow, weight, bsum, vec, sums, rows_step, put):
    for c in range(hid.shape[0]):
        gh = dot_nt(glow[...], weight(1, c))
        gpre = (gh * slope[c].astype(f32)).astype(bf16)
        slope[c] = gpre
        bsum[c] += fold(gpre.astype(f32))
        acc[...] += dot_nn(gpre, weight(0, c))
    for r in range(0, nbuf.shape[1], rows_step):
        at = pl.ds(r, rows_step)
        ga = acc[at, :]
        n = rows_of(nbuf, at)
        sums[0] += fold(ga * n)
        sums[1] += fold(ga)
        q = ga * vec[0:1]
        put(at, sbuf[at, 0:1] * (q - mean_of(q) - n * mean_of(q * n)))


def ffn_grads(alow, hid, slope, glow, dw):
    chunk = hid.shape[2]
    for c in range(hid.shape[0]):
        at = pl.ds(c * chunk, chunk)
        dw[1, at, :] += dot_tn(hid[c], glow[...])
        dw[0, at, :] += dot_tn(slope[c], alow[...])


def layer_kernel(geo, tok, cot, win_own, wout_own, hp_all, wd_all, cp_all, tw, b_in, *rest):
    vec_own = rest[:5]
    (out, gtok, grow, dwin_own, dwout_own, small,
                 tokv, cotv, outv, w0, w1, hp, wd, cp, dw, send1, recv1, send2, recv2, t_ref, o_ref,
                 nbuf, sbuf, alow, hid, slope, acc, glow, sums, bsum, rz, rze, rzl, sv, rv, va, ra, vec, bias_in,
                 ss1, rs1, ss2, rs2, free1, free2, load, io,
                 s_core, r_core, s_first, r_first, s_next, r_next, s_z, r_z, s_vec, r_vec, ready,
                 s_spread, r_spread, s_relay, r_relay, s_pair, r_pair, s_early, r_early, s_late, r_late, s_va, r_va) = rest[5:]
    parts, pairs, span, width, jobs, slots, chunk, rows_step, planes = geo
    shard = dw.shape[1] // (parts * planes)
    me = lax.axis_index("seq")
    plane = lax.axis_index("batch")

    def peer(d):
        return lax.rem(me + d, parts)

    def load_of(k):
        if k < jobs:
            return pltpu.make_async_copy(tok.at[k], tokv.at[k], load.at[k])
        a, b = ((hp_all, hp), (wd_all, wd), (cp_all, cp))[k - jobs]
        return pltpu.make_async_copy(a, b, load.at[k])

    barrier = pltpu.get_barrier_semaphore()

    def greet(d, carry):
        pl.semaphore_signal(barrier, inc=1, device_id=(peer(d), plane), device_id_type=MESH)
        return carry

    def greet_z(d, carry):
        pl.semaphore_signal(barrier, inc=1, device_id=(me, lax.rem(plane + d, planes)), device_id_type=MESH)
        return carry

    lax.fori_loop(1, parts, greet, 0)
    lax.fori_loop(1, planes, greet_z, 0)
    core, quad = lax.rem(me, 2), me // 2
    quads = parts // 2
    x, y = lax.rem(quad, 2), quad // 2
    partner = (me + 1 - 2 * core, plane)
    x_peer = (me + 2 - 4 * x, plane)
    y_peer = (me + 4 - 8 * y, plane)
    quad_x, quad_y = quad + 1 - 2 * x, quad + 2 - 4 * y
    last = planes - 1

    def send(src, dst, s, r, to):
        return pltpu.make_async_remote_copy(
            src_ref=src, dst_ref=dst, send_sem=s, recv_sem=r, device_id=to, device_id_type=MESH)

    own_loads = (
        pltpu.make_async_copy(win_own, w0.at[quad, core, plane], load.at[jobs + 3]),
        pltpu.make_async_copy(wout_own, w1.at[quad, core, plane], load.at[jobs + 4]),
    )
    for copy in own_loads:
        copy.start()
    for k in (jobs, 0, 1, jobs + 1, 2, 3, jobs + 2):
        load_of(k).start()

    owner = me * planes + plane
    part = width // (parts * planes)
    per_row = width // shard
    bias_row = 5 + owner // per_row
    row16 = lax.broadcasted_iota(jnp.int32, (16, width), 0)
    is_bias = row16 == jnp.zeros((16, width), jnp.int32) + bias_row
    sv[0] = jnp.zeros_like(sv[0])
    for j in range(5):
        sv[0, j:j + 1, 0:part] = vec_own[j][...].astype(f32)
    sv[0, 8:9, 0:shard] = b_in[...].astype(f32)
    rows8 = pltpu.roll(sv[0, 0:8], owner * part, 1)
    bias8 = pltpu.roll(sv[0, 8:16], lax.rem(owner, per_row) * shard, 1)
    placed = jnp.concatenate([rows8, jnp.zeros((8, width), f32)], axis=0)
    placed = jnp.where(is_bias, jnp.broadcast_to(bias8[0:1], (16, width)), placed)
    va[0] = placed.astype(bf16)

    pl.semaphore_wait(barrier, parts - 1 + planes - 1)

    def remote(send, recv, ss, rs, k, d):
        p = peer(d)
        return pltpu.make_async_remote_copy(
            src_ref=send.at[lax.rem(k, 2), p], dst_ref=recv.at[lax.rem(k, slots), me],
            send_sem=ss.at[lax.rem(k, 2), d], recv_sem=rs.at[lax.rem(k, slots), d],
            device_id=(p, plane), device_id_type=MESH)

    def wait_sends(send, recv, ss, rs, k):
        def one(d, carry):
            remote(send, recv, ss, rs, k, d).wait_send()
            return carry

        lax.fori_loop(1, parts, one, 0)

    def wait_recvs(send, recv, ss, rs, k):
        def one(d, carry):
            source = lax.rem(me + parts - d, parts)
            slot = lax.rem(k, slots)
            pltpu.make_async_remote_copy(
                src_ref=send.at[0, 0], dst_ref=recv.at[slot, source],
                send_sem=ss.at[0, d], recv_sem=rs.at[slot, d],
                device_id=(source, plane), device_id_type=MESH).wait_recv()
            return carry

        lax.fori_loop(1, parts, one, 0)

    def tell(sem, k):
        def one(d, carry):
            pl.semaphore_signal(sem.at[lax.rem(k, slots)], inc=1, device_id=(peer(d), plane), device_id_type=MESH)
            return carry

        lax.fori_loop(1, parts, one, 0)

    def in_plane(d):
        return 2 * lax.rem(quad + d, quads) + core

    def along(d):
        return lax.rem(plane + d, planes)

    def spread_z(d):
        block = w0.at[quad, core, plane]
        return send(block, block, s_spread.at[0, d], r_spread.at[0, d], (me, along(d)))

    def spread_out(d):
        block = w1.at[quad, core, plane]
        return send(block, block, s_spread.at[1, d], r_spread.at[1, d], (in_plane(d), plane))

    def spread_in(n):
        block = w0.at[quad, core]
        return send(block, block, s_spread.at[2, n], r_spread.at[2, n], (x_peer, y_peer)[n])

    def pass_in(n):
        block = w0.at[(quad_x, quad_y)[n], core, pl.ds(n * planes // 2, planes // 2)]
        return send(block, block, s_spread.at[2, 2 + n], r_spread.at[2, 2 + n], (y_peer, x_peer)[n])

    def relay(origin, up):
        block = w1.at[:, core, origin]
        return send(block, block, s_relay.at[up, origin], r_relay.at[origin], (me, plane + 2 * up - 1))

    def pair_in(q):
        block = w0.at[q, core]
        return send(block, block, s_pair.at[0, q], r_pair.at[0, q], partner)

    def pair_out(origin):
        block = w1.at[:, core, origin]
        return send(block, block, s_pair.at[1, origin], r_pair.at[1, origin], partner)

    def relay_step(j):
        below, above = plane - 1 - j, plane + 1 + j

        @pl.when(below >= 0)
        def _():
            relay(below, 1).wait_recv()

            @pl.when(plane < last)
            def _():
                relay(below, 1).start()

            pair_out(below).start()

        @pl.when(above <= last)
        def _():
            relay(above, 0).wait_recv()

            @pl.when(plane > 0)
            def _():
                relay(above, 0).start()

            pair_out(above).start()

    def vec_spread(k):
        to = (partner, x_peer, y_peer)[k] if k < 3 else (me, along(k - 2))
        return send(va.at[min(k, 3)], ra.at[k], s_va.at[k], r_va.at[k], to)

    def vec_gather(k):
        if k > 0:
            vec_spread(k - 1).wait_recv()
            va[k] = (va[k - 1].astype(f32) + ra[k - 1].astype(f32)).astype(bf16)
        for j in ((k,) if k < 3 else range(3, 2 + planes)):
            vec_spread(j).start()

    def gather_start():
        for copy in own_loads:
            copy.wait()
        for d in range(1, planes):
            spread_z(d).start()
        for d in range(1, quads):
            spread_out(d).start()

    def gather_out():
        for d in range(1, quads):
            spread_out(d).wait_recv()

        @pl.when(plane < last)
        def _():
            relay(plane, 1).start()

        @pl.when(plane > 0)
        def _():
            relay(plane, 0).start()

        pair_out(plane).start()

    def gather_in():
        for d in range(1, planes):
            spread_z(d).wait_recv()
        for n in range(2):
            spread_in(n).start()
        pair_in(quad).start()

    def gather_pass():
        for n in range(2):
            spread_in(n).wait_recv()
        for n in range(2):
            pass_in(n).start()
        pair_in(quad_x).start()
        pair_in(quad_y).start()

    def gather_diagonal():
        for n in range(2):
            pass_in(n).wait_recv()
        pair_in(quads - 1 - quad).start()

    def gather_end_out():
        for origin in range(planes):
            pair_out(origin).wait_recv()

    def gather_end_in():
        for q in range(quads):
            pair_in(q).wait_recv()

        total = va[3].astype(f32)
        for k in range(3, 2 + planes):
            vec_spread(k).wait_recv()
            total = total + ra[k].astype(f32)
        vec[...] = total[0:8]
        for f in range(0, bsum.shape[0] * chunk, width):
            bias_in[f // chunk, 0:1, f % chunk:f % chunk + width] = total[5 + f // width:6 + f // width]

    def gather_sent():
        for k in range(2 + planes):
            vec_spread(k).wait_send()
        for d in range(1, planes):
            spread_z(d).wait_send()
        for d in range(1, quads):
            spread_out(d).wait_send()
        for n in range(2):
            spread_in(n).wait_send()
            pass_in(n).wait_send()
        for q in range(quads):
            pair_in(q).wait_send()
        for origin in range(planes):
            pair_out(origin).wait_send()

            @pl.when((plane < last) & (origin <= plane))
            def _():
                relay(origin, 1).wait_send()

            @pl.when((plane > 0) & (origin >= plane))
            def _():
                relay(origin, 0).wait_send()

    def weight(m, c, count=1):
        n = chunk // (2 * planes * shard)
        at = pl.ds(c * n, count * n)
        block = w0[at] if m == 0 else w1[at]
        return block.reshape(count * chunk, width)

    def told(sem, k):
        pl.semaphore_wait(sem.at[lax.rem(k, slots)], parts - 1)

    one_way = (send1, recv1, ss1, rs1)
    way_back = (send2, recv2, ss2, rs2)

    def hidden_job(k):
        @pl.when(k >= 2)
        def _():
            wait_sends(*one_way, k - 2)

        @pl.when(k >= slots)
        def _():
            told(free1, k)

        table = dot_nt(hp[...], tokv[lax.rem(k, jobs)]).astype(bf16)
        send1[lax.rem(k, 2)] = table.reshape(parts, 2 * pairs, span)
        recv1[lax.rem(k, slots), me] = send1[lax.rem(k, 2), me]

        def one(d, carry):
            remote(*one_way, k, d).start()
            return carry

        lax.fori_loop(1, parts, one, 0)

    def sequence_job(k, carry):
        wait_recvs(*one_way, k)
        radix_step(recv1.at[lax.rem(k, slots)], tw, t_ref, parts, pairs, span)

        @pl.when(k < 2 * jobs - slots)
        def _():
            tell(free1, k)

        @pl.when(k >= 2)
        def _():
            wait_sends(*way_back, k - 2)

        @pl.when(k >= slots)
        def _():
            told(free2, k)

        slot = lax.rem(k, 2)
        half = span // 2

        def put(p, rows, cols, value):
            send2[slot, p, rows, cols] = value

        for base in range(2):
            o_ref[...] = dot_nn(t_ref[...], wd[:, base * half:(base + 1) * half])
            for u in range(base * parts // 4, (base + 1) * parts // 4):
                spread_step(o_ref, put, me, parts, pairs, u, base)
        recv2[lax.rem(k, slots), me] = send2[slot, me]

        def one(d, carry):
            remote(*way_back, k, d).start()
            return carry

        lax.fori_loop(1, parts, one, 0)
        return carry

    def mixed_job(k):
        wait_recvs(*way_back, k)
        blocks = recv2[lax.rem(k, slots)].reshape(width, span)
        natural = dot_tn(blocks, cp[...])
        step = span // parts
        for b in range(parts):
            for c in range(width // 128):
                nbuf[c, pl.ds(b, step, stride=parts), :] = natural[b * step:(b + 1) * step, c * 128:(c + 1) * 128]

    vec_gather(0)
    gather_start()
    vec_gather(1)
    load_of(jobs).wait()
    load_of(0).wait()
    hidden_job(0)
    dw[...] = jnp.zeros_like(dw)
    sums[...] = jnp.zeros_like(sums)
    bsum[...] = jnp.zeros_like(bsum)
    gather_out()
    vec_gather(2)
    gather_in()
    for k in (1, 2, 3, jobs + 1, jobs + 2):
        load_of(k).wait()

    sequence_job(0, 0)
    vec_gather(3)
    relay_step(0)
    gather_pass()
    hidden_job(1)
    relay_step(1)
    hidden_job(2)
    gather_diagonal()
    hidden_job(3)
    gather_end_in()

    def out_copy(i):
        return pltpu.make_async_copy(outv, out.at[i], io.at[0])

    def cot_copy(i):
        return pltpu.make_async_copy(cot.at[i], cotv, io.at[1])

    def row_copy(i):
        return pltpu.make_async_copy(acc, grow.at[i], io.at[2])

    def main(i, carry):
        cot_copy(i).start()
        mixed_job(i)
        tell(free2, i)
        ffn_hidden(lambda at: tokv[i, at, :], nbuf, sbuf, alow, hid, slope, weight, vec, bias_in, rows_step)
        @pl.when(i != 1)
        def _():
            sequence_job(i + 1 + (i + 1) // 2, 0)

        @pl.when(i == 0)
        def _():
            relay_step(2)
            gather_end_out()

        ffn_branch(hid, acc, weight)
        cot_copy(i).wait()

        @pl.when(i > 0)
        def _():
            out_copy(i - 1).wait()

        ffn_middle(nbuf, acc, glow, cotv, outv, vec, sums, rows_step)
        out_copy(i).start()

        def put(at, value):
            acc[at, :] = value
            tokv[i, at, :] = value.astype(bf16)

        ffn_backward(nbuf, sbuf, hid, slope, acc, glow, weight, bsum, vec, sums, rows_step, put)
        row_copy(i).start()
        hidden_job(i + jobs)

        @pl.when(i < 3)
        def _():
            sequence_job(i + 2 + i // 2, 0)

        ffn_grads(alow, hid, slope, glow, dw)
        row_copy(i).wait()
        return carry

    lax.fori_loop(0, jobs, main, 0)

    rest_rows = 16
    most = shard - rest_rows

    def rows_at(start, count=shard):
        return pl.ds(pl.multiple_of(start, shard), count)

    def target(v):
        return lax.rem(plane + 1 + v, planes)

    def owned(q, c, v):
        return rows_at(((2 * q + c) * planes + target(v)) * shard)

    head = pl.ds(0, most)

    def core_copy(v):
        return send(w1.at[v], w0.at[v], s_core.at[v], r_core.at[v], partner)

    staged = 2 * quads * rest_rows

    def first_copy(v, m):
        return send(hid.at[v, pl.ds(staged + 2 * m * most, 2 * most)], slope.at[v, pl.ds(2 * m * most, 2 * most)],
                    s_first.at[v, m], r_first.at[v, m], (x_peer, y_peer)[m])

    def next_copy(v, m):
        return send(w0.at[0, v // 2, 2 * lax.rem(v, 2) + m, head],
                    (alow, glow)[m].at[pl.ds(pl.multiple_of(v * most, most), most)],
                    s_next.at[v, m], r_next.at[v, m], (y_peer, x_peer)[m])

    def z_copy(v):
        return send(w0.at[1, v // 2, pl.ds(2 * lax.rem(v, 2), 2), head], rz.at[v],
                    s_z.at[v], r_z.at[v], (me, target(v)))

    def early_copy(v):
        return send(hid.at[v, pl.ds(0, 2 * quads * rest_rows)], rze.at[v], s_early.at[v], r_early.at[v], (me, target(v)))

    def late_copy(d):
        q = lax.rem(quad + d, quads)
        return send(hid.at[last, pl.ds(pl.multiple_of(2 * q * rest_rows, 2 * rest_rows), 2 * rest_rows)], rzl.at[d - 1],
                    s_late.at[d - 1], r_late.at[d - 1], (in_plane(d), plane))

    def vec_copy(k):
        to = (partner, x_peer, y_peer)[k] if k < 3 else (me, target(k - 3))
        return send(sv.at[min(k, 3)], rv.at[k], s_vec.at[k], r_vec.at[k], to)

    def core_step(v, carry):
        for q in range(quads):
            for m in range(2):
                w1[v, q // 2, 2 * (q % 2) + m] = dw[m, owned(q, 1 - core, v)].astype(bf16)
        core_copy(v).start()
        return carry

    def owned_most(q, v):
        return rows_at(((2 * q + core) * planes + target(v)) * shard, most)

    def owned_rest(q, v):
        return pl.ds(pl.multiple_of(((2 * q + core) * planes + target(v)) * shard + most, 16), rest_rows)

    def first_step(v, carry):
        core_copy(v).wait_recv()
        for q in range(quads):
            for m in range(2):
                at = owned(q, core, v)
                dw[m, at] += w0[v, q // 2, 2 * (q % 2) + m].astype(f32)

        @pl.when(v < last)
        def _():
            for q in range(quads):
                for m in range(2):
                    at = pl.ds((2 * q + m) * rest_rows, rest_rows)
                    hid[v, at, :] = dw[m, owned_rest(q, v)].astype(bf16)
            early_copy(v).start()

        for k in range(2):
            for m in range(2):
                q = 2 * k + 1 - x if m == 0 else 2 * (1 - y) + k
                at = pl.ds(staged + (2 * m + k) * most, most)
                hid[v, at, :] = dw[m, owned_most(q, v)].astype(bf16)
        for m in range(2):
            first_copy(v, m).start()
        return carry

    def next_step(v, carry):
        for m in range(2):
            first_copy(v, m).wait_recv()
        for k in range(2):
            for m in range(2):
                q = 2 * k + x if m == 0 else 2 * y + k
                dw[m, owned_most(q, v)] += slope[v, (2 * m + k) * most:(2 * m + k + 1) * most, :].astype(f32)
        for m in range(2):
            q = 2 * (1 - y) + x if m == 0 else 2 * y + 1 - x
            w0[0, v // 2, 2 * lax.rem(v, 2) + m, 0:most, :] = dw[m, owned_most(q, v)].astype(bf16)
            next_copy(v, m).start()
        return carry

    def z_step(v, carry):
        for m in range(2):
            next_copy(v, m).wait_recv()
            dw[m, owned_most(quad, v)] += (alow, glow)[m][pl.ds(pl.multiple_of(v * most, most), most)].astype(f32)

        @pl.when(v < last)
        def _():
            for m in range(2):
                w0[1, v // 2, 2 * lax.rem(v, 2) + m, 0:most, :] = dw[m, owned_most(quad, v)].astype(bf16)
            z_copy(v).start()

        return carry

    def late_step():
        for v in range(last):
            early_copy(v).wait_recv()
        for q in range(quads):
            for m in range(2):
                at = owned_rest(q, last)
                total = dw[m, at]
                for v in range(last):
                    total = total + rze[v, (2 * q + m) * rest_rows:(2 * q + m + 1) * rest_rows].astype(f32)
                dw[m, at] = total
                hid[last, (2 * q + m) * rest_rows:(2 * q + m + 1) * rest_rows, :] = total.astype(bf16)
        for d in range(1, quads):
            late_copy(d).start()

    def vec_step(k):
        if k == 0:
            sv[0] = jnp.zeros_like(sv[0])
            for j in range(5):
                sv[0, j:j + 1] = jnp.sum(sums[j], axis=0, keepdims=True)
            piece = math.gcd(width, chunk)
            for f in range(0, bsum.shape[0] * chunk, piece):
                sv[0, 5 + f // width:6 + f // width, f % width:f % width + piece] = jnp.sum(
                    bsum[f // chunk, :, f % chunk:f % chunk + piece], axis=0, keepdims=True)
        else:
            vec_copy(k - 1).wait_recv()
            sv[k] = sv[k - 1] + rv[k - 1]
        for j in ((k,) if k < 3 else range(3, 2 + planes)):
            vec_copy(j).start()

    def gt_copy(i):
        return pltpu.make_async_copy(tokv.at[i], gtok.at[i], io.at[4 + i])

    def final(i, carry):
        back = pltpu.make_async_copy(grow.at[i], acc, io.at[2])
        back.start()
        mixed_job(i + jobs)
        back.wait()
        for c in range(width // 128):
            tokv[i, :, c * 128:(c + 1) * 128] = (nbuf[c] + acc[:, c * 128:(c + 1) * 128]).astype(bf16)
        gt_copy(i).start()
        return carry

    gather_sent()
    for n, to in enumerate((partner, x_peer, y_peer)):
        pl.semaphore_signal(ready.at[n], inc=1, device_id=to, device_id_type=MESH)
    pl.semaphore_wait(ready.at[0], 1)
    lax.fori_loop(0, planes, core_step, 0)
    vec_step(0)
    vec_step(1)
    pl.semaphore_wait(ready.at[1], 1)
    pl.semaphore_wait(ready.at[2], 1)
    first_step(0, 0)
    final(0, 0)
    tell(free2, jobs)
    lax.fori_loop(1, last, first_step, 0)
    next_step(0, 0)
    vec_step(2)
    final(2, 0)
    next_step(1, 0)
    final(1, 0)
    lax.fori_loop(2, last, next_step, 0)
    z_step(0, 0)
    first_step(last, 0)
    vec_step(3)
    z_step(1, 0)
    sequence_job(2 * jobs - 1, 0)
    lax.fori_loop(2, last, z_step, 0)
    next_step(last, 0)
    late_step()
    final(3, 0)
    z_step(last, 0)
    own_most, own_rest = owned_most(quad, last), owned_rest(quad, last)
    for v in range(last):
        z_copy(v).wait_recv()
    for d in range(1, quads):
        late_copy(d).wait_recv()
    for m in range(2):
        total = dw[m, own_most]
        for v in range(last):
            total = total + rz[v, m].astype(f32)
        (dwin_own, dwout_own)[m][0:most] = total
        total = dw[m, own_rest]
        for d in range(1, quads):
            total = total + rzl[d - 1, m * rest_rows:(m + 1) * rest_rows].astype(f32)
        (dwin_own, dwout_own)[m][most:shard] = total
    total = sv[3]
    for k in range(3, 2 + planes):
        vec_copy(k).wait_recv()
        total = total + rv[k]
    mine = jnp.sum(jnp.where(is_bias, total, 0.0), axis=0, keepdims=True)
    mine = pltpu.roll(jnp.broadcast_to(mine, (8, width)), width - lax.rem(owner, per_row) * shard, 1)
    rows8 = pltpu.roll(total[0:8], width - owner * part, 1)
    row8 = lax.broadcasted_iota(jnp.int32, (8, 128), 0)
    small[...] = jnp.where(row8 == 5, mine[:, 0:128], rows8[:, 0:128])

    def sent(v, carry):
        core_copy(v).wait_send()
        for m in range(2):
            first_copy(v, m).wait_send()
            next_copy(v, m).wait_send()
        return carry

    lax.fori_loop(0, planes, sent, 0)
    for k in range(2 * jobs - 2, 2 * jobs):
        wait_sends(*way_back, k)
        wait_sends(*one_way, k)
    for v in range(last):
        z_copy(v).wait_send()
        early_copy(v).wait_send()
    for d in range(1, quads):
        late_copy(d).wait_send()
    for k in range(2 + planes):
        vec_copy(k).wait_send()
    out_copy(jobs - 1).wait()
    for i in range(jobs):
        gt_copy(i).wait()


def layer_call(tok, cot, win_own, wout_own, b_in, vectors, parts, planes):
    jobs, span, width = tok.shape
    shard = wout_own.shape[0]
    ff = shard * parts * planes
    pairs = width // 2 // parts
    chunk, rows_step = ff // (parts // 2), span // 4
    steps = ff // chunk
    length = span * parts
    slots = 3
    geo = (parts, pairs, span, width, jobs, slots, chunk, rows_step, planes)
    tables = (
        jnp.asarray(packed_hidden(width, parts)),
        jnp.asarray(inner_table(span, length)),
        jnp.asarray(column_order(width, parts)),
        jnp.asarray(twiddles(parts, span)),
    )
    hbm, vmem, dma = pl.BlockSpec(memory_space=pl.ANY), pl.BlockSpec(memory_space=pltpu.VMEM), pltpu.SemaphoreType.DMA
    block = (parts, 2 * pairs, span)
    scratch = [
        pltpu.VMEM((jobs, span, width), bf16),
        pltpu.VMEM((span, width), bf16),
        pltpu.VMEM((span, width), bf16),
        pltpu.VMEM((parts // 2, 2, planes, shard, width), bf16),
        pltpu.VMEM((parts // 2, 2, planes, shard, width), bf16),
        pltpu.VMEM((width, width), bf16),
        pltpu.VMEM((2 * span, span), bf16),
        pltpu.VMEM((width, width), bf16),
        pltpu.VMEM((2, ff, width), f32),
        pltpu.VMEM((2,) + block, bf16),
        pltpu.VMEM((slots,) + block, bf16),
        pltpu.VMEM((2,) + block, bf16),
        pltpu.VMEM((slots,) + block, bf16),
        pltpu.VMEM((2 * parts * pairs + 16, 2 * span), bf16),
        pltpu.VMEM((2 * parts * pairs + 16, span // 2), f32),
        pltpu.VMEM((width // 128, span, 128), f32),
        pltpu.VMEM((span, 128), f32),
        pltpu.VMEM((span, width), bf16),
        pltpu.VMEM((steps, span, chunk), bf16),
        pltpu.VMEM((steps, span, chunk), bf16),
        pltpu.VMEM((span, width), f32),
        pltpu.VMEM((span, width), bf16),
        pltpu.VMEM((5, 8, width), f32),
        pltpu.VMEM((steps, 8, chunk), f32),
        pltpu.VMEM((planes - 1, 2, shard - 16, width), bf16),
        pltpu.VMEM((planes - 1, parts * 16, width), bf16),
        pltpu.VMEM((parts // 2 - 1, 2 * 16, width), bf16),
        pltpu.VMEM((4, 16, width), f32),
        pltpu.VMEM((2 + planes, 16, width), f32),
        pltpu.VMEM((4, 16, width), bf16),
        pltpu.VMEM((2 + planes, 16, width), bf16),
        pltpu.VMEM((8, width), f32),
        pltpu.VMEM((steps, 1, chunk), f32),
        dma((2, parts)), dma((slots, parts)), dma((2, parts)), dma((slots, parts)),
        pltpu.SemaphoreType.REGULAR((slots,)), pltpu.SemaphoreType.REGULAR((slots,)),
        dma((jobs + 5,)), dma((4 + jobs,)),
        dma((planes,)), dma((planes,)), dma((planes, 2)), dma((planes, 2)), dma((planes, 2)), dma((planes, 2)),
        dma((planes - 1,)), dma((planes - 1,)), dma((2 + planes,)), dma((2 + planes,)),
        pltpu.SemaphoreType.REGULAR((3,)),
        dma((3, max(parts // 2, planes))), dma((3, max(parts // 2, planes))), dma((2, planes)), dma((planes,)),
        dma((2, max(parts // 2, planes))), dma((2, max(parts // 2, planes))),
        dma((planes - 1,)), dma((planes - 1,)), dma((parts // 2 - 1,)), dma((parts // 2 - 1,)),
        dma((2 + planes,)), dma((2 + planes,)),
    ]
    shape = jax.ShapeDtypeStruct
    return pl.pallas_call(
        partial(layer_kernel, geo),
        out_shape=(
            shape(tok.shape, bf16),
            shape(tok.shape, bf16),
            shape(tok.shape, f32),
            shape((shard, width), f32),
            shape((shard, width), f32),
            shape((8, 128), f32),
        ),
        in_specs=[hbm] * 7 + [vmem] * 7,
        out_specs=(hbm,) * 3 + (vmem,) * 3,
        scratch_shapes=scratch,
        compiler_params=pltpu.CompilerParams(
            collective_id=1, has_side_effects=True, vmem_limit_bytes=64 * 1024 * 1024 - 256 * 1024),
        name="encoder_layer",
    )(tok, cot, win_own, wout_own, *tables, b_in, *vectors)


def local_fast(tokens, w_in, b_in, w_out, b_out, gain_one, shift_one, gain_two, shift_two, cotangent):
    both = ("seq", "batch")
    parts = lax.axis_size("seq")
    width = tokens.shape[2]
    shard = w_in.shape[1]
    planes = lax.axis_size("batch")
    part = b_out.shape[0]
    vectors = [v.reshape(1, part) for v in (gain_one, shift_one, gain_two, shift_two, b_out)]
    out, gtok, _, dwin, dwout, small = layer_call(
        tokens, cotangent, w_in.T, w_out, b_in.reshape(1, shard), vectors, parts, planes)
    rest = small[:5, :part]
    return (out, gtok, dwin.T, small[5, :shard], dwout, rest[4], rest[0], rest[1], rest[2], rest[3])


def hidden_table(extent):
    idx_all = jnp.arange(extent, dtype=jnp.int32)
    angles = (idx_all[:, None] * idx_all[None, :] % extent).astype(jnp.float32) * (
        2.0 * math.pi / extent
    )
    factor = 1.0 / math.sqrt(extent)
    return jnp.concatenate([jnp.cos(angles) * factor, jnp.sin(angles) * factor], axis=1).astype(
        jnp.bfloat16
    )


def sequence_table(length):
    block_rows = min(512, length)
    block_count = length // block_rows
    col_ids = jnp.arange(length, dtype=jnp.int32)
    factor = 1.0 / math.sqrt(length)

    def table_rows(block_index):
        row_ids = block_index * block_rows + jnp.arange(block_rows, dtype=jnp.int32)
        angles = (row_ids[:, None] * col_ids[None, :] % length).astype(jnp.float32) * (
            2.0 * math.pi / length
        )
        return (jnp.stack([jnp.cos(angles), -jnp.sin(angles)]) * factor).astype(jnp.bfloat16)

    blocks = lax.map(table_rows, jnp.arange(block_count, dtype=jnp.int32))
    return jnp.moveaxis(blocks, 1, 0).reshape(2, length, length)


def normalize(values, gain, shift):
    center = values - jnp.mean(values, axis=-1, keepdims=True)
    inv_std = lax.rsqrt(jnp.mean(center * center, axis=-1, keepdims=True) + epsilon)
    normed = center * inv_std
    return (normed * gain + shift, normed, inv_std)


def norm_back(grad_out, normed, inv_std, gain):
    scaled = grad_out * gain
    centered = scaled - jnp.mean(scaled, axis=-1, keepdims=True)
    return inv_std * (centered - normed * jnp.mean(scaled * normed, axis=-1, keepdims=True))


def local(tokens, w_in, b_in, w_out, b_out, gain_one, shift_one, gain_two, shift_two, cotangent):
    batch_rows, seq_part, model_width = tokens.shape
    length = seq_part * lax.axis_size("seq")
    w_in_all, b_in_all, w_out_all, b_out_all, g_one_all, s_one_all, g_two_all, s_two_all = (
        lax.all_gather(w_in, ("seq", "batch"), axis=1, tiled=True),
        lax.all_gather(b_in, ("seq", "batch"), axis=0, tiled=True),
        lax.all_gather(w_out, ("seq", "batch"), axis=0, tiled=True),
        lax.all_gather(b_out, ("seq", "batch"), axis=0, tiled=True),
        lax.all_gather(gain_one, ("seq", "batch"), axis=0, tiled=True),
        lax.all_gather(shift_one, ("seq", "batch"), axis=0, tiled=True),
        lax.all_gather(gain_two, ("seq", "batch"), axis=0, tiled=True),
        lax.all_gather(shift_two, ("seq", "batch"), axis=0, tiled=True),
    )
    h_table = hidden_table(model_width)
    s_table = sequence_table(length)
    flat_tokens = tokens.reshape(-1, model_width)
    spectra = jnp.dot(flat_tokens, h_table, preferred_element_type=jnp.float32).astype(jnp.bfloat16)
    spectra = spectra.reshape(batch_rows, seq_part, 2, model_width)
    mixed_cols = jnp.einsum(
        "plm,bmpc->blc",
        s_table,
        lax.all_to_all(spectra, "seq", split_axis=3, concat_axis=1, tiled=True),
        preferred_element_type=jnp.float32,
    ).astype(jnp.bfloat16)
    mixed = lax.all_to_all(mixed_cols, "seq", split_axis=1, concat_axis=2, tiled=True)
    resid_one = flat_tokens.astype(jnp.float32) + mixed.reshape(-1, model_width).astype(jnp.float32)
    act_one, normed_one, inv_one = normalize(
        resid_one, g_one_all.astype(jnp.float32), s_one_all.astype(jnp.float32)
    )
    act_low = act_one.astype(jnp.bfloat16)
    pre_act = jnp.dot(act_low, w_in_all, preferred_element_type=jnp.float32) + b_in_all.astype(
        jnp.float32
    )
    activ, gelu_back = jax.vjp(partial(jax.nn.gelu, approximate=True), pre_act)
    hidden_low = activ.astype(jnp.bfloat16)
    branch = jnp.dot(hidden_low, w_out_all, preferred_element_type=jnp.float32) + b_out_all.astype(
        jnp.float32
    )
    resid_two = act_one + branch
    result, normed_two, inv_two = normalize(
        resid_two, g_two_all.astype(jnp.float32), s_two_all.astype(jnp.float32)
    )
    grad_out = cotangent.reshape(-1, model_width).astype(jnp.float32)
    grad_g_two = jnp.sum(grad_out * normed_two, axis=0)
    grad_s_two = jnp.sum(grad_out, axis=0)
    grad_r_two = norm_back(grad_out, normed_two, inv_two, g_two_all.astype(jnp.float32))
    grad_branch = grad_r_two.astype(jnp.bfloat16)
    grad_b_out = jnp.sum(grad_branch.astype(jnp.float32), axis=0)
    grad_w_out = jnp.einsum(
        "tf,td->fd", hidden_low, grad_branch, preferred_element_type=jnp.float32
    )
    grad_hidden = jnp.einsum(
        "td,fd->tf", grad_branch, w_out_all, preferred_element_type=jnp.float32
    )
    grad_pre = gelu_back(grad_hidden)[0].astype(jnp.bfloat16)
    grad_b_in = jnp.sum(grad_pre.astype(jnp.float32), axis=0)
    grad_w_in = jnp.einsum("td,tf->df", act_low, grad_pre, preferred_element_type=jnp.float32)
    grad_a_one = grad_r_two + jnp.einsum(
        "tf,df->td", grad_pre, w_in_all, preferred_element_type=jnp.float32
    )
    grad_g_one = jnp.sum(grad_a_one * normed_one, axis=0)
    grad_s_one = jnp.sum(grad_a_one, axis=0)
    grad_r_one = norm_back(grad_a_one, normed_one, inv_one, g_one_all.astype(jnp.float32))
    grad_mix = grad_r_one.astype(jnp.bfloat16).reshape(batch_rows, seq_part, model_width)
    spec_grad = jnp.einsum(
        "plm,blc->bmpc",
        s_table,
        lax.all_to_all(grad_mix, "seq", split_axis=2, concat_axis=1, tiled=True),
        preferred_element_type=jnp.float32,
    ).astype(jnp.bfloat16)
    grad_spec = lax.all_to_all(spec_grad, "seq", split_axis=1, concat_axis=3, tiled=True)
    grad_flat = grad_r_one + jnp.einsum(
        "te,de->td",
        grad_spec.reshape(-1, 2 * model_width),
        h_table,
        preferred_element_type=jnp.float32,
    )
    sum_w_in, sum_b_in, sum_w_out, sum_b_out, sum_g_one, sum_s_one, sum_g_two, sum_s_two = (
        lax.psum_scatter(grad_w_in, ("seq", "batch"), scatter_dimension=1, tiled=True),
        lax.psum_scatter(grad_b_in, ("seq", "batch"), scatter_dimension=0, tiled=True),
        lax.psum_scatter(grad_w_out, ("seq", "batch"), scatter_dimension=0, tiled=True),
        lax.psum_scatter(grad_b_out, ("seq", "batch"), scatter_dimension=0, tiled=True),
        lax.psum_scatter(grad_g_one, ("seq", "batch"), scatter_dimension=0, tiled=True),
        lax.psum_scatter(grad_s_one, ("seq", "batch"), scatter_dimension=0, tiled=True),
        lax.psum_scatter(grad_g_two, ("seq", "batch"), scatter_dimension=0, tiled=True),
        lax.psum_scatter(grad_s_two, ("seq", "batch"), scatter_dimension=0, tiled=True),
    )
    output = result.astype(jnp.bfloat16).reshape(batch_rows, seq_part, model_width)
    grad_tokens = grad_flat.astype(jnp.bfloat16).reshape(batch_rows, seq_part, model_width)
    return (
        output,
        grad_tokens,
        sum_w_in,
        sum_b_in,
        sum_w_out,
        sum_b_out,
        sum_g_one,
        sum_s_one,
        sum_g_two,
        sum_s_two,
    )


def solution(mesh):
    every = P(("seq", "batch"))

    def whole(tokens, w_in, *rest):
        parts = mesh.shape["seq"]
        fits = (
            parts == 8
            and tokens.shape[1] == 512 * parts
            and tokens.shape[2] % (32 * parts) == 0
            and w_in.shape[1] % (3 * 128) == 0
            and tokens.shape[0] == 4 * mesh.shape["batch"]
        )
        return jax.shard_map(
            local_fast if fits else local,
            mesh=mesh,
            in_specs=(
                P("batch", "seq", None),
                P(None, ("seq", "batch")),
                every,
                P(("seq", "batch"), None),
                every,
                every,
                every,
                every,
                every,
                P("batch", "seq", None),
            ),
            out_specs=(
                P("batch", "seq", None),
                P("batch", "seq", None),
                P(None, ("seq", "batch")),
                every,
                P(("seq", "batch"), None),
                every,
                every,
                every,
                every,
                every,
            ),
            check_vma=False,
        )(tokens, w_in, *rest)

    return whole
```
